512 devices in a mesh: role: 4 (over x), seq: 32 (over z_lo, y), mp: 4 (over z_hi, core).
Axes of the slice: x: 4, y: 8, z: 8 (z_hi: 2, z_lo: 4; z = z_hi * 4 + z_lo), core: 2. Of those that a mesh axis runs over, the one named last changes fastest.
Arguments:
- gen_hidden: bfloat16 [4096, 5120], P('seq', 'mp'), may hold values from -0.59765625 to 0.59765625
- out_weight: bfloat16 [5120, 64], P('mp'), may hold values from -0.078125 to 0.078125
- noise: bfloat16 [4096, 64], P('seq'), may hold values from -12 to 12
- step_index: int32 [1], replicated, may hold values from 200 to 799
- token_order: int32 [4096], P('seq'), may hold values from 0 to 4095, each once
- time_weight: float32 [4, 256, 2, 5120], P('role', None, None, ('seq', 'mp')), may hold values from -0.375 to 0.375
- embed_weight: bfloat16 [4, 64, 5120], P('role'), may hold values from -0.75 to 0.75
- qkv_weight: bfloat16 [4, 32, 5120, 384], P('role', 'seq'), may hold values from -0.078125 to 0.078125
- readout_weight: bfloat16 [4, 32, 128, 64], P('role', 'seq'), may hold values from -0.09375 to 0.09375
Outputs:
- hidden_grad: bfloat16 [4096, 5120], P('seq', 'mp')
- weight_grad: float32 [5120, 64], P('mp')
The draws below stay inside these ranges and needn't reach their ends.
Inputs may be any that keep to these rules, and one draw needn't show every extreme that they name: `token_order`: each row's position in the clip, every position once.
All inputs are finite; a program needn't handle non-finite values. Where the reference program divides by a largest or mean magnitude, that divisor is 1e-20 or more.
Results may differ from the reference program's by a relative error of at most 0.035.
Values may be sent and summed in bfloat16 or wider, within the bound.
No kernel may reach another device: no remote copies, remote signals or barrier semaphores. Data moves between devices by JAX's collectives and lax.ppermute only.
A program may use at most 64 MiB of HBM per device.

```python
import math
import jax
import jax.numpy as jnp
from jax import lax

D = 5120
LAT = 64
HD = 128
FREQ = 256
T_STEPS = 1000
HEADS = 32
TOKENS = 4096
N_ROLE = 4


def draw_noise(key, part):
    key = jax.random.fold_in(key, 11)
    first = jax.random.fold_in(key, 0)
    positions = jnp.arange(TOKENS, dtype=jnp.float32)
    rising = jnp.exp(math.log(3.0) * positions / max(TOKENS - 1, 1))
    values = jax.random.truncated_normal(first, -4.0, 4.0, (TOKENS, LAT)) * rising[:, None]
    return values.astype(jnp.bfloat16)


def levels(own_key, dims, cuts, low, largest):
    level = 1.0
    for axis_at, blocks in cuts:
        steps = jax.random.uniform(jax.random.fold_in(jax.random.fold_in(own_key, 6), axis_at), (blocks,), jnp.float32, low / len(cuts), largest / len(cuts))
        level = level * jnp.repeat(jnp.exp(steps), dims[axis_at] // blocks).reshape((-1,) + (1,) * (len(dims) - 1 - axis_at))
    return level


def scatter_about(rng, dims, deviation, most, cuts=(), held_as=jnp.bfloat16):
    entries = deviation * jax.random.normal(rng, dims, jnp.float32)
    if cuts:
        entries = entries * levels(rng, dims, cuts, -0.22, 0.18)
    return jnp.clip(entries, -most, most).astype(held_as)


def setup_inputs(seed: int = 0) -> dict:
    key_of = jax.random.split(jax.random.key(seed), 10)
    return {
        "gen_hidden": scatter_about(key_of[0], (TOKENS, D), 0.1, 0.59765625, ((0, 32), (1, 4))),
        "out_weight": scatter_about(key_of[1], (D, LAT), D ** -0.5, 0.078125, ((0, 4),)),
        "noise": draw_noise(jax.random.fold_in(key_of[9], 71), 0),
        "step_index": jax.random.randint(key_of[3], (1,), 200, 800).astype(jnp.int32),
        "token_order": jax.random.permutation(key_of[4], TOKENS).astype(jnp.int32),
        "time_weight": scatter_about(key_of[5], (N_ROLE, FREQ, 2, D), FREQ ** -0.5, 0.375, ((0, 4), (3, 128)), jnp.float32),
        "embed_weight": scatter_about(key_of[6], (N_ROLE, LAT, D), LAT ** -0.5, 0.75, ((0, 4),)),
        "qkv_weight": scatter_about(key_of[7], (N_ROLE, HEADS, D, 3 * HD), D ** -0.5, 0.078125, ((0, 4), (1, 32))),
        "readout_weight": scatter_about(key_of[8], (N_ROLE, HEADS, HD, LAT), (HEADS * HD) ** -0.5, 0.09375, ((0, 4), (1, 32))),
    }


EPS_NORM = 1e-06
EPS_MEAN = 1e-05
GUIDANCE = 5.0
ROPE_BASE = 10000.0
SHARPNESS = 4.0

def normalize_rope(vectors, cosines, sines):
    rescaled = vectors * lax.rsqrt(lax.optimization_barrier(jnp.mean(vectors * vectors, axis=1, keepdims=True)) + EPS_NORM)
    width = vectors.shape[1] // 2
    front = rescaled[:, :width]
    back = rescaled[:, width:]
    return jnp.concatenate([front * cosines - back * sines, front * sines + back * cosines], axis=1).astype(jnp.bfloat16)

def pass_score(noisy, activated, cosines, sines, time_part, embed_part, qkv_part, readout_part):
    modulation = jnp.einsum('f,fcd->cd', activated, time_part, precision=lax.Precision.HIGHEST)
    embedded = jnp.dot(noisy, embed_part, preferred_element_type=jnp.float32)
    normed = embedded * lax.rsqrt(lax.optimization_barrier(jnp.mean(embedded * embedded, axis=1, keepdims=True)) + EPS_NORM)
    modulated = (normed * (1.0 + modulation[1]) + modulation[0]).astype(jnp.bfloat16)

    def one_head(weights):
        projection, readout = weights
        combined = jnp.dot(modulated, projection, preferred_element_type=jnp.float32)
        queries = normalize_rope(combined[:, :HD], cosines, sines)
        keys = normalize_rope(combined[:, HD:2 * HD], cosines, sines)
        values = combined[:, 2 * HD:].astype(jnp.bfloat16)
        scores = jnp.dot(queries, keys.T, preferred_element_type=jnp.float32) * (SHARPNESS / math.sqrt(HD))
        exponent = jnp.exp(scores)
        numerator = jnp.dot(exponent.astype(jnp.bfloat16), values, preferred_element_type=jnp.float32)
        denominator = lax.optimization_barrier(jnp.sum(exponent, axis=1))
        attended = (numerator / denominator[:, None]).astype(jnp.bfloat16)
        return jnp.dot(attended, readout, preferred_element_type=jnp.float32)
    return lax.optimization_barrier(jnp.sum(lax.map(one_head, (qkv_part, readout_part)), axis=0))

def reference(gen_hidden, out_weight, noise, step_index, token_order, time_weight, embed_weight, qkv_weight, readout_weight):
    hidden_wide = gen_hidden.astype(jnp.float32)
    projected = jnp.dot(gen_hidden, out_weight, preferred_element_type=jnp.float32)
    root_mean = jnp.sqrt(lax.optimization_barrier(jnp.sum(hidden_wide * hidden_wide, axis=1)) / D + EPS_NORM)
    latent = projected / root_mean[:, None]
    timestep = step_index[0].astype(jnp.float32)
    noise_level = timestep / T_STEPS
    noisy = ((1.0 - noise_level) * latent + noise_level * noise.astype(jnp.float32)).astype(jnp.bfloat16)
    half_freq = FREQ // 2
    frequencies = jnp.exp(-math.log(ROPE_BASE) * jnp.arange(half_freq, dtype=jnp.float32) / half_freq)
    phases = timestep * frequencies
    activated = jax.nn.silu(jnp.concatenate([jnp.cos(phases), jnp.sin(phases)]))
    inverse = jnp.exp(-math.log(ROPE_BASE) * jnp.arange(HD // 2, dtype=jnp.float32) * 2.0 / HD)
    angles = token_order.astype(jnp.float32)[:, None] * inverse[None, :]
    cosines = jnp.cos(angles)
    sines = jnp.sin(angles)
    scores = []
    for index in range(1, 4):
        scores.append(pass_score(noisy, activated, cosines, sines, time_weight[index], embed_weight[index], qkv_weight[index], readout_weight[index]))
    realistic = GUIDANCE * scores[0] + (1.0 - GUIDANCE) * scores[1]
    difference = scores[2] - realistic
    spread = jnp.mean(jnp.abs(latent - (noisy.astype(jnp.float32) - noise_level * realistic))) + EPS_MEAN
    latent_grad = -noise_level * difference / spread
    backward = jnp.dot(latent_grad, out_weight.astype(jnp.float32).T, precision=lax.Precision.HIGHEST)
    row_terms = lax.optimization_barrier(jnp.sum(latent_grad * projected, axis=1))
    cubed = root_mean * root_mean * root_mean
    hidden_grad = (backward / root_mean[:, None] - hidden_wide * (row_terms / (D * cubed))[:, None]).astype(jnp.bfloat16)
    weight_grad = jnp.dot((hidden_wide / root_mean[:, None]).T, latent_grad, precision=lax.Precision.HIGHEST) / math.sqrt(TOKENS)
    return (hidden_grad, weight_grad)
```

```python
import functools
import math

import jax
import jax.numpy as jnp
from jax import lax
from jax.experimental import pallas as pl
from jax.experimental.pallas import tpu as pltpu
from jax.sharding import PartitionSpec as P

D = 5120
FREQ = 256
T_STEPS = 1000


EPS_NORM = 1e-06
EPS_MEAN = 1e-05
GUIDANCE = 5.0
ROPE_BASE = 10000.0
SHARPNESS = 4.0


def pack(block):
    count = block.shape[0] // 2
    return jnp.concatenate([block[:count], block[count:]], axis=1)


def unpack(block):
    width = block.shape[1] // 2
    return jnp.concatenate([block[:, :width], block[:, width:]], axis=0)


def split(values):
    high = values.astype(jnp.bfloat16)
    return high, (values - high.astype(jnp.float32)).astype(jnp.bfloat16)


def exchange(chunks, axes):
    return lax.all_to_all(chunks, axes, 0, 0, tiled=True)


def to_all(chunk, axes, count):
    return exchange(jnp.broadcast_to(chunk[None], (count, *chunk.shape)), axes)


def dot32(left, right):
    return jnp.dot(left, right, preferred_element_type=jnp.float32)


def normalize_rope(vectors, cosines, sines):
    rescaled = vectors * lax.rsqrt(jnp.mean(vectors * vectors, axis=1, keepdims=True) + EPS_NORM)
    width = vectors.shape[1] // 2
    front = rescaled[:, :width]
    back = rescaled[:, width:]
    return jnp.concatenate(
        [front * cosines - back * sines, front * sines + back * cosines], axis=1
    ).astype(jnp.bfloat16)


def attend_kernel(query_ref, key_ref, value_ref, readout_ref, score_ref, wide, attended):
    query_rows, head_dim = query_ref.shape
    key_rows = key_ref.shape[0]
    rows, width = 256, 512
    wide[:, :head_dim] = value_ref[...]
    wide[:, head_dim:] = jnp.ones((key_rows, head_dim), jnp.bfloat16)
    factor = SHARPNESS / math.sqrt(head_dim) * math.log2(math.e)

    def step(index, carry):
        at = pl.multiple_of(index * rows, rows)
        queries = query_ref[pl.ds(at, rows), :]
        total = jnp.zeros((rows, 2 * head_dim), jnp.float32)
        for begin in range(0, key_rows, width):
            scores = lax.dot_general(
                queries,
                key_ref[begin : begin + width, :],
                (((1,), (1,)), ((), ())),
                preferred_element_type=jnp.float32,
            )
            weights = jnp.exp2(scores * factor).astype(jnp.bfloat16)
            total = total + dot32(weights, wide[begin : begin + width, :])
        attended[pl.ds(at, rows), :] = (total[:, :head_dim] / total[:, head_dim:]).astype(
            jnp.bfloat16
        )
        return carry

    lax.fori_loop(0, query_rows // rows, step, 0)
    half = query_rows // 2
    score_ref[...] = jnp.concatenate(
        [dot32(attended[:half, :], readout_ref[...]), dot32(attended[half:, :], readout_ref[...])],
        axis=1,
    ).astype(jnp.bfloat16)


def attend(queries, keys, values, readout):
    query_rows, head_dim = queries.shape
    key_rows = keys.shape[0]
    return pl.pallas_call(
        attend_kernel,
        out_shape=jax.ShapeDtypeStruct((query_rows // 2, 2 * readout.shape[1]), jnp.bfloat16),
        in_specs=[pl.BlockSpec(memory_space=pltpu.VMEM)] * 4,
        out_specs=pl.BlockSpec(memory_space=pltpu.VMEM),
        scratch_shapes=[
            pltpu.VMEM((key_rows, 2 * head_dim), jnp.bfloat16),
            pltpu.VMEM((query_rows, head_dim), jnp.bfloat16),
        ],
        compiler_params=pltpu.CompilerParams(vmem_limit_bytes=32 * 1024 * 1024),
    )(queries, keys, values, readout)


def body(
    gen_hidden,
    out_weight,
    noise,
    step_index,
    token_order,
    time_weight,
    embed_weight,
    qkv_weight,
    readout_weight,
):
    seq_count = lax.axis_size("seq")
    mp_count = lax.axis_size("mp")
    role_count = lax.axis_size("role")
    mp_index = lax.axis_index("mp")
    local_rows = gen_hidden.shape[0]
    packed_rows = local_rows // 2
    quarter = packed_rows // mp_count
    head_dim = qkv_weight.shape[3] // 3
    lat_dim = out_weight.shape[1]
    lanes = 2 * lat_dim
    mod_width = time_weight.shape[3]
    f32 = jnp.float32
    timestep = step_index[0].astype(f32)
    noise_level = timestep / T_STEPS

    half_freq = FREQ // 2
    frequencies = jnp.exp(-math.log(ROPE_BASE) * jnp.arange(half_freq, dtype=f32) / half_freq)
    phases = timestep * frequencies
    activated = jax.nn.silu(jnp.concatenate([jnp.cos(phases), jnp.sin(phases)]))
    modulation_part = jnp.sum(activated[:, None, None] * time_weight[0], axis=0)

    hidden_wide = gen_hidden.astype(f32)
    mod_row = jnp.pad(modulation_part.reshape(1, 2 * mod_width), ((0, 0), (0, lanes - 2 * mod_width)))
    first = jnp.concatenate(
        [
            pack(dot32(gen_hidden, out_weight)),
            jnp.sum(hidden_wide * hidden_wide, axis=1)[None],
            mod_row,
            jnp.zeros((6, lanes), f32),
        ]
    )
    first = to_all(first, "mp", mp_count)
    projected = jnp.sum(first[:, :packed_rows], axis=0)
    squares = jnp.sum(first[:, packed_rows], axis=0)
    root_mean = jnp.sqrt(squares / D + EPS_NORM)
    root_packed = pack(jnp.broadcast_to(root_mean[:, None], (local_rows, lat_dim)))
    latent = projected / root_packed
    noisy = ((1.0 - noise_level) * latent + noise_level * pack(noise).astype(f32)).astype(
        jnp.bfloat16
    )

    mod_rows = -(-2 * mp_count * mod_width // lanes)
    mod_mine = (
        first[:, packed_rows + 1, : 2 * mod_width]
        .reshape(mp_count, 2, mod_width)
        .transpose(1, 0, 2)
        .reshape(2 * mp_count * mod_width)
    )
    mod_mine = jnp.pad(mod_mine, (0, mod_rows * lanes - mod_mine.shape[0])).reshape(mod_rows, lanes)
    order = jnp.stack([token_order // 64, token_order % 64]).astype(jnp.bfloat16)
    used = packed_rows + 2 + 2 * mod_rows
    second = jnp.concatenate(
        [noisy, order, *split(mod_mine), jnp.zeros((-used % 16, lanes), jnp.bfloat16)]
    )
    second = to_all(second, "seq", seq_count)
    rows = second[:, :packed_rows]
    order_wide = second[:, packed_rows : packed_rows + 2].astype(f32)
    positions = order_wide[:, 0] * 64.0 + order_wide[:, 1]
    mod_at = packed_rows + 2
    modulation = (
        second[:, mod_at : mod_at + mod_rows].astype(f32)
        + second[:, mod_at + mod_rows : mod_at + 2 * mod_rows].astype(f32)
    ).reshape(seq_count, mod_rows * lanes)[:, : 2 * mp_count * mod_width]
    modulation = modulation.reshape(seq_count, 2, mp_count * mod_width).transpose(1, 0, 2).reshape(2, D)

    embed = embed_weight[0]
    weights = qkv_weight[0, 0]
    scaled = split(embed.astype(f32) * (1.0 + modulation[1])[None])
    shifted = split(modulation[0][None])
    folded = dot32(jnp.concatenate([*scaled, *shifted], axis=0), weights)
    matrix = folded[:lat_dim] + folded[lat_dim : 2 * lat_dim]
    offset = folded[2 * lat_dim] + folded[2 * lat_dim + 1]
    gram = lax.dot_general(embed, embed, (((1,), (1,)), ((), ())), preferred_element_type=f32)
    matrix_parts = split(jnp.concatenate([matrix, gram], axis=1))

    def project(block):
        product = dot32(block, matrix_parts[0]) + dot32(block, matrix_parts[1])
        mean = jnp.sum(block.astype(f32) * product[:, 3 * head_dim :], axis=1, keepdims=True) / D
        return product[:, : 3 * head_dim] * lax.rsqrt(mean + EPS_NORM) + offset[None]

    inverse = jnp.exp(-math.log(ROPE_BASE) * jnp.arange(head_dim // 2, dtype=f32) * 2.0 / head_dim)

    def turn(places):
        angles = places.reshape(-1)[:, None] * inverse[None, :]
        return jnp.cos(angles), jnp.sin(angles)

    mine = lax.dynamic_slice_in_dim(rows, mp_index * quarter, quarter, 1)
    all_rows = jnp.concatenate(
        [rows[:, :, :lat_dim].reshape(-1, lat_dim), rows[:, :, lat_dim:].reshape(-1, lat_dim)]
    )
    combined = project(all_rows)
    cosines, sines = turn(
        jnp.concatenate([positions[:, :packed_rows].reshape(-1), positions[:, packed_rows:].reshape(-1)])
    )
    keys = normalize_rope(combined[:, head_dim : 2 * head_dim], cosines, sines)
    values = combined[:, 2 * head_dim :].astype(jnp.bfloat16)

    def own(array):
        grid = array.reshape(2, seq_count, packed_rows, array.shape[1])
        return lax.dynamic_slice_in_dim(grid, mp_index * quarter, quarter, 2).reshape(-1, array.shape[1])

    queries = normalize_rope(own(combined[:, :head_dim]), own(cosines), own(sines))
    scores = attend(queries, keys, values, readout_weight[0, 0])

    scores = exchange(scores.reshape(seq_count, quarter, lanes), "seq")
    score = jnp.sum(scores.astype(f32), axis=0)

    score = to_all(score, ("role", "mp"), role_count * mp_count).reshape(
        role_count, packed_rows, lanes
    )
    realistic = GUIDANCE * score[1] + (1.0 - GUIDANCE) * score[2]
    difference = score[3] - realistic
    magnitude = jnp.sum(jnp.abs(latent - (noisy.astype(f32) - noise_level * realistic)))

    direction = split(unpack(difference / root_packed))
    both = jnp.concatenate(direction, axis=1)
    weight_part = lax.dot_general(
        gen_hidden, both, (((0,), (0,)), ((), ())), preferred_element_type=f32
    )
    weight_part = pack(weight_part[:, :lat_dim] + weight_part[:, lat_dim:])
    share = weight_part.shape[0] // seq_count
    pieces = []
    rest = magnitude
    for unused in range(3):
        piece = rest.astype(jnp.bfloat16)
        rest = rest - piece.astype(f32)
        pieces.append(piece)
    extra = jnp.pad(jnp.stack(pieces)[None], ((0, 0), (0, lanes - 3)))
    padding = -(share + 1) % 16
    third = jnp.concatenate(
        [
            weight_part.astype(jnp.bfloat16).reshape(seq_count, share, lanes),
            jnp.broadcast_to(extra[None], (seq_count, 1, lanes)),
            jnp.zeros((seq_count, padding, lanes), jnp.bfloat16),
        ],
        axis=1,
    )
    third = jnp.sum(exchange(third, "seq").astype(f32), axis=0)
    cell_count = local_rows * seq_count * lat_dim
    spread = jnp.sum(third[share]) / cell_count + EPS_MEAN
    factor = -noise_level / spread
    fourth = (third[: share + 1 + padding] * (factor / math.sqrt(local_rows * seq_count))).astype(
        jnp.bfloat16
    )
    fourth = to_all(fourth, "seq", seq_count)
    weight_grad = unpack(fourth[:, :share].reshape(seq_count * share, lanes).astype(f32))

    backward = lax.dot_general(
        both,
        jnp.concatenate([out_weight, out_weight], axis=1),
        (((1,), (1,)), ((), ())),
        preferred_element_type=f32,
    )
    row_terms = jnp.sum(unpack(difference * projected), axis=1)
    cubed = root_mean * root_mean * root_mean
    hidden_grad = (
        factor * (backward - hidden_wide * (row_terms / (D * cubed))[:, None])
    ).astype(jnp.bfloat16)
    return (hidden_grad, weight_grad)


def solution(mesh):
    placed = (
        P("seq", "mp"),
        P("mp", None),
        P("seq", None),
        P(),
        P("seq"),
        P("role", None, None, ("seq", "mp")),
        P("role", None, None),
        P("role", "seq", None, None),
        P("role", "seq", None, None),
    )
    return jax.shard_map(
        body, mesh=mesh, in_specs=placed, out_specs=(P("seq", "mp"), P("mp", None)), check_vma=False
    )
```

```python
import math

import jax
import jax.numpy as jnp
import numpy as np
from jax import lax
from jax.experimental import pallas as pl
from jax.experimental.pallas import tpu as pltpu
from jax.sharding import PartitionSpec as P

D = 5120
FREQ = 256
T_STEPS = 1000


EPS_NORM = 1e-06
EPS_MEAN = 1e-05
GUIDANCE = 5.0
ROPE_BASE = 10000.0
SHARPNESS = 4.0


def pack(block):
    count = block.shape[0] // 2
    return jnp.concatenate([block[:count], block[count:]], axis=1)


def unpack(block):
    width = block.shape[1] // 2
    return jnp.concatenate([block[:, :width], block[:, width:]], axis=0)


def split(values):
    high = values.astype(jnp.bfloat16)
    return high, (values - high.astype(jnp.float32)).astype(jnp.bfloat16)


def exchange(chunks, axes):
    return lax.all_to_all(chunks, axes, 0, 0, tiled=True)


def to_all(chunk, axes, count):
    return exchange(jnp.broadcast_to(chunk[None], (count, *chunk.shape)), axes)


def dot32(left, right):
    return jnp.dot(left, right, preferred_element_type=jnp.float32)


def rotation_tables(head_dim):
    turns = ROPE_BASE ** (-2.0 * np.arange(head_dim // 2) / head_dim) / (2.0 * np.pi)
    grain = 2.0 ** (np.floor(np.log2(turns)) - 11)
    high = np.floor(turns / grain) * grain
    return tuple(
        np.ascontiguousarray(np.broadcast_to(part[:, None], (head_dim // 2, 128)), np.float32)
        for part in (high, turns - high)
    )


def rotations(positions, high, low):
    tiles = positions.shape[1] // high.shape[1]
    high = jnp.concatenate([high] * tiles, axis=1)
    low = jnp.concatenate([low] * tiles, axis=1)
    whole = positions * high
    part = (whole - jnp.round(whole)) + positions * low
    angle = (part - jnp.round(part)) * math.pi
    square = angle * angle
    sine = square * (-1.0 / 39916800) + 1.0 / 362880
    sine = sine * square - 1.0 / 5040
    sine = sine * square + 1.0 / 120
    sine = sine * square - 1.0 / 6
    sine = (sine * square + 1.0) * angle
    cosine = square * (1.0 / 479001600) - 1.0 / 3628800
    cosine = cosine * square + 1.0 / 40320
    cosine = cosine * square - 1.0 / 720
    cosine = cosine * square + 1.0 / 24
    cosine = cosine * square - 0.5
    cosine = cosine * square + 1.0
    return 1.0 - 2.0 * sine * sine, 2.0 * sine * cosine


def normalize_rope(vectors, cosines, sines):
    rescaled = vectors * lax.rsqrt(jnp.mean(vectors * vectors, axis=0, keepdims=True) + EPS_NORM)
    width = vectors.shape[0] // 2
    front = rescaled[:width]
    back = rescaled[width:]
    return jnp.concatenate([front * cosines - back * sines, front * sines + back * cosines], axis=0)


def pass_kernel(
    place_ref,
    gathered_ref,
    embed_ref,
    weight_ref,
    readout_ref,
    high_ref,
    low_ref,
    score_ref,
    modulation,
    scaled,
    clip,
    places,
    own,
    own_places,
    query,
    key,
    wide,
    attended,
):
    f32 = jnp.float32
    blocks, used, lanes = gathered_ref.shape
    lat_dim, width = embed_ref.shape
    head_dim = weight_ref.shape[1] // 3
    key_rows = blocks * lanes
    query_rows = query.shape[0]
    quarter = query_rows // blocks
    per_tile = lanes // quarter
    piece = width // blocks
    place = place_ref[0]

    for block in range(blocks):
        at = slice(block * lanes, (block + 1) * lanes)
        clip[:lat_dim, at] = gathered_ref[block, :lat_dim, :]
        clip[lat_dim:, at] = gathered_ref[block, :lat_dim, :]
        extra = gathered_ref[block, lat_dim : lat_dim + 16, :].astype(f32)
        places[0:1, at] = extra[0:1] * 64.0 + extra[1:2]
        pair = extra[2:6] + extra[6:10]
        begin = block * piece
        modulation[0:1, begin : begin + lanes] = pair[0:1]
        modulation[0:1, begin + lanes : begin + piece] = pair[1:2, : piece - lanes]
        modulation[1:2, begin : begin + lanes] = pair[2:3]
        modulation[1:2, begin + lanes : begin + piece] = pair[3:4, : piece - lanes]

    lane = lax.broadcasted_iota(jnp.int32, (lat_dim + 16, lanes), 1)
    for tile in range(blocks // per_tile):
        found = jnp.zeros((lat_dim + 16, lanes), f32)
        for part in range(per_tile):
            block = gathered_ref[tile * per_tile + part, : lat_dim + 16, :].astype(f32)
            shift = lax.rem((part - place + per_tile) * quarter, lanes)
            found = jnp.where(lane // quarter == part, pltpu.roll(block, shift, 1), found)
        at = slice(tile * lanes, (tile + 1) * lanes)
        rows = found[:lat_dim].astype(jnp.bfloat16)
        own[:lat_dim, at] = rows
        own[lat_dim:, at] = rows
        own_places[0:1, at] = found[lat_dim : lat_dim + 1] * 64.0 + found[lat_dim + 1 : lat_dim + 2]

    chunk = width // 5
    for begin in range(0, width, chunk):
        at = slice(begin, begin + chunk)
        high, low = split(embed_ref[:, at].astype(f32) * (1.0 + modulation[1:2, at]))
        scaled[:lat_dim, at] = high
        scaled[lat_dim : 2 * lat_dim, at] = low
        row = lax.broadcasted_iota(jnp.int32, (16, chunk), 0)
        shifted = jnp.broadcast_to(modulation[0:1, at], (16, chunk))
        shifted_high = shifted.astype(jnp.bfloat16).astype(f32)
        shifted = jnp.where(row == 0, shifted_high, shifted - shifted_high)
        scaled[2 * lat_dim :, at] = jnp.where(row < 2, shifted, 0.0).astype(jnp.bfloat16)
    folded = dot32(scaled[...], weight_ref[...])
    gram = lax.dot_general(
        embed_ref[...], embed_ref[...], (((1,), (1,)), ((), ())), preferred_element_type=f32
    )
    matrix = folded[:lat_dim] + folded[lat_dim : 2 * lat_dim]
    offset = folded[2 * lat_dim : 2 * lat_dim + 1] + folded[2 * lat_dim + 1 : 2 * lat_dim + 2]
    turned = jnp.concatenate(
        [matrix, jnp.broadcast_to(offset, (lanes - lat_dim, 3 * head_dim))], axis=0
    ).T
    offsets = jnp.broadcast_to(turned[:, lat_dim : lat_dim + 1], (3 * head_dim, lanes))
    matrix_parts = jnp.concatenate(split(turned[:, :lat_dim]), axis=1)
    gram_parts = jnp.concatenate(split(gram), axis=1)

    def project(parts, offsets, rows):
        product = dot32(jnp.concatenate([parts, gram_parts], axis=0), rows)
        count = parts.shape[0]
        mean = jnp.sum(rows[:lat_dim].astype(f32) * product[count:], axis=0, keepdims=True) / width
        offsets = jnp.concatenate([offsets] * (rows.shape[1] // lanes), axis=1)
        return product[:count] * lax.rsqrt(mean + EPS_NORM) + offsets

    step = 4 * lanes
    wide[:, head_dim:] = jnp.ones((key_rows, head_dim), jnp.bfloat16)
    for begin in range(0, query_rows, step):
        at = slice(begin, begin + step)
        vectors = project(matrix_parts[:head_dim], offsets[:head_dim], own[:, at])
        turns = rotations(own_places[0:1, at], high_ref[...], low_ref[...])
        query[at, :] = normalize_rope(vectors, *turns).T.astype(jnp.bfloat16)

    def keys_and_values(index, carry):
        at = pl.ds(pl.multiple_of(index * step, step), step)
        vectors = project(matrix_parts[head_dim:], offsets[head_dim:], clip[:, at])
        turns = rotations(places[0:1, at], high_ref[...], low_ref[...])
        key[:, at] = normalize_rope(vectors[:head_dim], *turns).astype(jnp.bfloat16)
        wide[at, :head_dim] = vectors[head_dim:].T.astype(jnp.bfloat16)
        return carry

    lax.fori_loop(0, key_rows // step, keys_and_values, 0)

    rows = 256
    factor = SHARPNESS / math.sqrt(head_dim) * math.log2(math.e)

    def attend(index, carry):
        at = pl.ds(pl.multiple_of(index * rows, rows), rows)
        queries = query[at, :]
        total = jnp.zeros((rows, 2 * head_dim), f32)
        for begin in range(0, key_rows, step):
            scores = dot32(queries, key[:, begin : begin + step])
            weights = jnp.exp2(scores * factor).astype(jnp.bfloat16)
            total = total + dot32(weights, wide[begin : begin + step, :])
        result = (total[:, :head_dim] / total[:, head_dim:]).astype(jnp.bfloat16)
        attended[pl.ds(index * (rows // quarter), rows // quarter)] = result.reshape(
            rows // quarter, quarter, head_dim
        )
        return carry

    lax.fori_loop(0, query_rows // rows, attend, 0)
    half = quarter // 2
    halves = [
        dot32(attended[:, begin : begin + half, :].reshape(blocks * half, head_dim), readout_ref[...])
        for begin in (0, half)
    ]
    score_ref[...] = (
        jnp.concatenate(halves, axis=1).astype(jnp.bfloat16).reshape(blocks, half, 2 * lat_dim)
    )


def run_pass(place, gathered, embed, weights, readout):
    blocks, unused, lanes = gathered.shape
    lat_dim, width = embed.shape
    head_dim = weights.shape[1] // 3
    key_rows = blocks * lanes
    query_rows = key_rows // 4
    bf16, f32 = jnp.bfloat16, jnp.float32
    vmem = pl.BlockSpec(memory_space=pltpu.VMEM)
    return pl.pallas_call(
        pass_kernel,
        out_shape=jax.ShapeDtypeStruct((blocks, lanes // 8, lanes), bf16),
        in_specs=[pl.BlockSpec(memory_space=pltpu.SMEM)] + [vmem] * 6,
        out_specs=vmem,
        scratch_shapes=[
            pltpu.VMEM((8, width), f32),
            pltpu.VMEM((2 * lat_dim + 16, width), bf16),
            pltpu.VMEM((2 * lat_dim, key_rows), bf16),
            pltpu.VMEM((8, key_rows), f32),
            pltpu.VMEM((2 * lat_dim, query_rows), bf16),
            pltpu.VMEM((8, query_rows), f32),
            pltpu.VMEM((query_rows, head_dim), bf16),
            pltpu.VMEM((head_dim, key_rows), bf16),
            pltpu.VMEM((key_rows, 2 * head_dim), bf16),
            pltpu.VMEM((blocks, lanes // 4, head_dim), bf16),
        ],
        compiler_params=pltpu.CompilerParams(vmem_limit_bytes=32 * 1024 * 1024),
    )(place, gathered, embed, weights, readout, *rotation_tables(head_dim))


def body(
    gen_hidden,
    out_weight,
    noise,
    step_index,
    token_order,
    time_weight,
    embed_weight,
    qkv_weight,
    readout_weight,
):
    seq_count = lax.axis_size("seq")
    mp_count = lax.axis_size("mp")
    role_count = lax.axis_size("role")
    mp_index = lax.axis_index("mp")
    local_rows = gen_hidden.shape[0]
    packed_rows = local_rows // 2
    lat_dim = out_weight.shape[1]
    lanes = 2 * lat_dim
    mod_width = time_weight.shape[3]
    bf16, f32 = jnp.bfloat16, jnp.float32
    timestep = step_index[0].astype(f32)
    noise_level = timestep / T_STEPS

    half_freq = FREQ // 2
    frequencies = jnp.exp(-math.log(ROPE_BASE) * jnp.arange(half_freq, dtype=f32) / half_freq)
    phases = timestep * frequencies
    activated = jax.nn.silu(jnp.concatenate([jnp.cos(phases), jnp.sin(phases)]))
    modulation_part = jnp.sum(activated[:, None, None] * time_weight[0], axis=0)

    hidden_wide = gen_hidden.astype(f32)
    mod_row = jnp.pad(modulation_part.reshape(1, 2 * mod_width), ((0, 0), (0, lanes - 2 * mod_width)))
    first = jnp.concatenate(
        [
            pack(dot32(gen_hidden, out_weight)),
            jnp.sum(hidden_wide * hidden_wide, axis=1)[None],
            mod_row,
            jnp.zeros((6, lanes), f32),
        ]
    )
    first = to_all(first, "mp", mp_count)
    projected = unpack(jnp.sum(first[:, :packed_rows], axis=0))
    squares = jnp.sum(first[:, packed_rows], axis=0)
    root_mean = jnp.sqrt(squares / D + EPS_NORM)
    latent = projected / root_mean[:, None]
    noisy = ((1.0 - noise_level) * latent + noise_level * noise.astype(f32)).astype(bf16)

    piece = mp_count * mod_width
    mod_mine = first[:, packed_rows + 1, : 2 * mod_width].reshape(mp_count, 2, mod_width)
    mod_mine = mod_mine.transpose(1, 0, 2).reshape(2, piece)
    mod_mine = jnp.pad(mod_mine, ((0, 0), (0, 2 * lanes - piece))).reshape(4, lanes)
    order = jnp.stack([token_order // 64, token_order % 64]).astype(bf16)
    second = jnp.concatenate([noisy.T, order, *split(mod_mine), jnp.zeros((6, lanes), bf16)])
    second = to_all(second, "seq", seq_count)

    scores = run_pass(
        mp_index.astype(jnp.int32)[None], second, embed_weight[0], qkv_weight[0, 0], readout_weight[0, 0]
    )

    score = jnp.sum(exchange(scores, "seq").astype(f32), axis=0)

    score = to_all(score, ("role", "mp"), role_count * mp_count)
    score = score.reshape(role_count, mp_count, local_rows // (2 * mp_count), 2, lat_dim)
    score = score.transpose(0, 1, 3, 2, 4).reshape(role_count, local_rows, lat_dim)
    realistic = GUIDANCE * score[1] + (1.0 - GUIDANCE) * score[2]
    difference = score[3] - realistic
    magnitude = jnp.sum(jnp.abs(latent - (noisy.astype(f32) - noise_level * realistic)))

    both = jnp.concatenate(split(difference / root_mean[:, None]), axis=1)
    weight_part = lax.dot_general(
        gen_hidden, both, (((0,), (0,)), ((), ())), preferred_element_type=f32
    )
    weight_part = pack(weight_part[:, :lat_dim] + weight_part[:, lat_dim:])
    share = weight_part.shape[0] // seq_count
    pieces = []
    rest = magnitude
    for unused in range(3):
        part = rest.astype(bf16)
        rest = rest - part.astype(f32)
        pieces.append(part)
    extra = jnp.pad(jnp.stack(pieces)[None], ((0, 0), (0, lanes - 3)))
    padding = -(share + 1) % 16
    third = jnp.concatenate(
        [
            weight_part.astype(bf16).reshape(seq_count, share, lanes),
            jnp.broadcast_to(extra[None], (seq_count, 1, lanes)),
            jnp.zeros((seq_count, padding, lanes), bf16),
        ],
        axis=1,
    )
    third = jnp.sum(exchange(third, "seq").astype(f32), axis=0)
    cell_count = local_rows * seq_count * lat_dim
    spread = jnp.sum(third[share]) / cell_count + EPS_MEAN
    factor = -noise_level / spread
    fourth = (third * (factor / math.sqrt(local_rows * seq_count))).astype(bf16)
    fourth = to_all(fourth, "seq", seq_count)
    weight_grad = unpack(fourth[:, :share].reshape(seq_count * share, lanes).astype(f32))

    backward = lax.dot_general(
        both,
        jnp.concatenate([out_weight, out_weight], axis=1),
        (((1,), (1,)), ((), ())),
        preferred_element_type=f32,
    )
    row_terms = jnp.sum(difference * projected, axis=1)
    cubed = root_mean * root_mean * root_mean
    hidden_grad = (
        factor * (backward - hidden_wide * (row_terms / (D * cubed))[:, None])
    ).astype(bf16)
    return (hidden_grad, weight_grad)


def solution(mesh):
    placed = (
        P("seq", "mp"),
        P("mp", None),
        P("seq", None),
        P(),
        P("seq"),
        P("role", None, None, ("seq", "mp")),
        P("role", None, None),
        P("role", "seq", None, None),
        P("role", "seq", None, None),
    )
    return jax.shard_map(
        body, mesh=mesh, in_specs=placed, out_specs=(P("seq", "mp"), P("mp", None)), check_vma=False
    )
```

```python
import functools
import math

import jax
import jax.numpy as jnp
import numpy as np
from jax import lax
from jax.experimental import pallas as pl
from jax.experimental.pallas import tpu as pltpu
from jax.sharding import PartitionSpec as P

D = 5120
FREQ = 256
T_STEPS = 1000


EPS_NORM = 1e-06
EPS_MEAN = 1e-05
GUIDANCE = 5.0
ROPE_BASE = 10000.0
SHARPNESS = 4.0


def split(values):
    high = values.astype(jnp.bfloat16)
    return high, (values - high.astype(jnp.float32)).astype(jnp.bfloat16)


def exchange(chunks, axes):
    return lax.all_to_all(chunks, axes, 0, 0, tiled=True)


def dot32(left, right):
    return jnp.dot(left, right, preferred_element_type=jnp.float32)


def dot_rows(left, right):
    return lax.dot_general(
        left, right, (((1,), (1,)), ((), ())), preferred_element_type=jnp.float32
    )


def rotation_tables(head_dim):
    turns = ROPE_BASE ** (-2.0 * np.arange(head_dim // 2) / head_dim) / (2.0 * np.pi)
    grain = 2.0 ** (np.floor(np.log2(turns)) - 11)
    high = np.floor(turns / grain) * grain
    return tuple(
        np.ascontiguousarray(np.broadcast_to(part[:, None], (head_dim // 2, 128)), np.float32)
        for part in (high, turns - high)
    )


def rotations(positions, high, low):
    tiles = positions.shape[1] // high.shape[1]
    high = jnp.concatenate([high] * tiles, axis=1)
    low = jnp.concatenate([low] * tiles, axis=1)
    whole = positions * high
    part = (whole - jnp.round(whole)) + positions * low
    angle = (part - jnp.round(part)) * math.pi
    square = angle * angle
    sine = square * (-1.0 / 39916800) + 1.0 / 362880
    sine = sine * square - 1.0 / 5040
    sine = sine * square + 1.0 / 120
    sine = sine * square - 1.0 / 6
    sine = (sine * square + 1.0) * angle
    cosine = square * (1.0 / 479001600) - 1.0 / 3628800
    cosine = cosine * square + 1.0 / 40320
    cosine = cosine * square - 1.0 / 720
    cosine = cosine * square + 1.0 / 24
    cosine = cosine * square - 0.5
    cosine = cosine * square + 1.0
    return 1.0 - 2.0 * sine * sine, 2.0 * sine * cosine


def normalize_rope(vectors, cosines, sines):
    rescaled = vectors * lax.rsqrt(jnp.mean(vectors * vectors, axis=0, keepdims=True) + EPS_NORM)
    width = vectors.shape[0] // 2
    front = rescaled[:width]
    back = rescaled[width:]
    return jnp.concatenate([front * cosines - back * sines, front * sines + back * cosines], axis=0)


def pass_kernel(
    place_ref,
    gathered_ref,
    embed_ref,
    weight_ref,
    readout_ref,
    high_ref,
    low_ref,
    score_ref,
    modulation,
    scaled,
    clip,
    places,
    own,
    own_places,
    query,
    key,
    wide,
    attended,
    weights,
    weights_in,
):
    f32 = jnp.float32
    fetch = pltpu.make_async_copy(weight_ref, weights, weights_in)
    fetch.start()
    blocks, used, lanes = gathered_ref.shape
    lat_dim, width = embed_ref.shape
    head_dim = weight_ref.shape[1] // 3
    key_rows = blocks * lanes
    query_rows = query.shape[0]
    quarter = query_rows // blocks
    per_tile = lanes // quarter
    piece = width // blocks
    place = place_ref[0]

    for block in range(blocks):
        at = slice(block * lanes, (block + 1) * lanes)
        clip[:lat_dim, at] = gathered_ref[block, :lat_dim, :]
        clip[lat_dim:, at] = gathered_ref[block, :lat_dim, :]
        extra = gathered_ref[block, lat_dim : lat_dim + 16, :].astype(f32)
        places[0:1, at] = extra[0:1] * 64.0 + extra[1:2]
        pair = extra[2:6] + extra[6:10]
        begin = block * piece
        modulation[0:1, begin : begin + lanes] = pair[0:1]
        modulation[0:1, begin + lanes : begin + piece] = pair[1:2, : piece - lanes]
        modulation[1:2, begin : begin + lanes] = pair[2:3]
        modulation[1:2, begin + lanes : begin + piece] = pair[3:4, : piece - lanes]

    lane = lax.broadcasted_iota(jnp.int32, (lat_dim + 16, lanes), 1)
    for tile in range(blocks // per_tile):
        found = jnp.zeros((lat_dim + 16, lanes), f32)
        for part in range(per_tile):
            block = gathered_ref[tile * per_tile + part, : lat_dim + 16, :].astype(f32)
            shift = lax.rem((part - place + per_tile) * quarter, lanes)
            found = jnp.where(lane // quarter == part, pltpu.roll(block, shift, 1), found)
        at = slice(tile * lanes, (tile + 1) * lanes)
        rows = found[:lat_dim].astype(jnp.bfloat16)
        own[:lat_dim, at] = rows
        own[lat_dim:, at] = rows
        own_places[0:1, at] = found[lat_dim : lat_dim + 1] * 64.0 + found[lat_dim + 1 : lat_dim + 2]

    chunk = width // 5
    for begin in range(0, width, chunk):
        at = slice(begin, begin + chunk)
        high, low = split(embed_ref[:, at].astype(f32) * (1.0 + modulation[1:2, at]))
        scaled[:lat_dim, at] = high
        scaled[lat_dim : 2 * lat_dim, at] = low
        row = lax.broadcasted_iota(jnp.int32, (16, chunk), 0)
        shifted = jnp.broadcast_to(modulation[0:1, at], (16, chunk))
        shifted_high = shifted.astype(jnp.bfloat16).astype(f32)
        shifted = jnp.where(row == 0, shifted_high, shifted - shifted_high)
        scaled[2 * lat_dim :, at] = jnp.where(row < 2, shifted, 0.0).astype(jnp.bfloat16)
    gram = dot_rows(embed_ref[...], embed_ref[...])
    fetch.wait()
    folded = dot32(scaled[...], weights[...])
    matrix = folded[:lat_dim] + folded[lat_dim : 2 * lat_dim]
    offset = folded[2 * lat_dim : 2 * lat_dim + 1] + folded[2 * lat_dim + 1 : 2 * lat_dim + 2]
    turned = jnp.concatenate(
        [matrix, jnp.broadcast_to(offset, (lanes - lat_dim, 3 * head_dim))], axis=0
    ).T
    offsets = jnp.broadcast_to(turned[:, lat_dim : lat_dim + 1], (3 * head_dim, lanes))
    matrix_parts = jnp.concatenate(split(turned[:, :lat_dim]), axis=1)
    gram_parts = jnp.concatenate(split(gram), axis=1)

    def project(parts, offsets, rows):
        product = dot32(jnp.concatenate([parts, gram_parts], axis=0), rows)
        count = parts.shape[0]
        mean = jnp.sum(rows[:lat_dim].astype(f32) * product[count:], axis=0, keepdims=True) / width
        offsets = jnp.concatenate([offsets] * (rows.shape[1] // lanes), axis=1)
        return product[:count] * lax.rsqrt(mean + EPS_NORM) + offsets

    step = 4 * lanes
    wide[:, head_dim:] = jnp.ones((key_rows, head_dim), jnp.bfloat16)
    for begin in range(0, query_rows, step):
        at = slice(begin, begin + step)
        vectors = project(matrix_parts[:head_dim], offsets[:head_dim], own[:, at])
        turns = rotations(own_places[0:1, at], high_ref[...], low_ref[...])
        query[at, :] = normalize_rope(vectors, *turns).T.astype(jnp.bfloat16)

    def keys_and_values(index, carry):
        at = pl.ds(pl.multiple_of(index * step, step), step)
        vectors = project(matrix_parts[head_dim:], offsets[head_dim:], clip[:, at])
        turns = rotations(places[0:1, at], high_ref[...], low_ref[...])
        key[:, at] = normalize_rope(vectors[:head_dim], *turns).astype(jnp.bfloat16)
        wide[at, :head_dim] = vectors[head_dim:].T.astype(jnp.bfloat16)
        return carry

    lax.fori_loop(0, key_rows // step, keys_and_values, 0)

    rows = 256
    factor = SHARPNESS / math.sqrt(head_dim) * math.log2(math.e)

    def attend(index, carry):
        at = pl.ds(pl.multiple_of(index * rows, rows), rows)
        queries = query[at, :]
        total = jnp.zeros((rows, 2 * head_dim), f32)
        for begin in range(0, key_rows, step):
            scores = dot32(queries, key[:, begin : begin + step])
            exponents = jnp.exp2(scores * factor).astype(jnp.bfloat16)
            total = total + dot32(exponents, wide[begin : begin + step, :])
        result = (total[:, :head_dim] / total[:, head_dim:]).astype(jnp.bfloat16)
        attended[pl.ds(index * (rows // quarter), rows // quarter)] = result.reshape(
            rows // quarter, quarter, head_dim
        )
        return carry

    lax.fori_loop(0, query_rows // rows, attend, 0)
    half = quarter // 2
    halves = [
        dot_rows(attended[:, begin : begin + half, :].reshape(blocks * half, head_dim), readout_ref[...])
        for begin in (0, half)
    ]
    score_ref[...] = (
        jnp.concatenate(halves, axis=1).astype(jnp.bfloat16).reshape(blocks, half, 2 * lat_dim)
    )


def run_pass(place, gathered, embed, weights, readout):
    blocks, unused, lanes = gathered.shape
    lat_dim, width = embed.shape
    head_dim = weights.shape[1] // 3
    key_rows = blocks * lanes
    query_rows = key_rows // 4
    bf16, f32 = jnp.bfloat16, jnp.float32
    vmem = pl.BlockSpec(memory_space=pltpu.VMEM)
    return pl.pallas_call(
        pass_kernel,
        out_shape=jax.ShapeDtypeStruct((blocks, lanes // 8, lanes), bf16),
        in_specs=[
            pl.BlockSpec(memory_space=pltpu.SMEM),
            vmem,
            vmem,
            pl.BlockSpec(memory_space=pl.ANY),
            vmem,
            vmem,
            vmem,
        ],
        out_specs=vmem,
        scratch_shapes=[
            pltpu.VMEM((8, width), f32),
            pltpu.VMEM((2 * lat_dim + 16, width), bf16),
            pltpu.VMEM((2 * lat_dim, key_rows), bf16),
            pltpu.VMEM((8, key_rows), f32),
            pltpu.VMEM((2 * lat_dim, query_rows), bf16),
            pltpu.VMEM((8, query_rows), f32),
            pltpu.VMEM((query_rows, head_dim), bf16),
            pltpu.VMEM((head_dim, key_rows), bf16),
            pltpu.VMEM((key_rows, 2 * head_dim), bf16),
            pltpu.VMEM((blocks, lanes // 4, head_dim), bf16),
            pltpu.VMEM(weights.shape, bf16),
            pltpu.SemaphoreType.DMA,
        ],
        compiler_params=pltpu.CompilerParams(vmem_limit_bytes=32 * 1024 * 1024),
    )(place, gathered, embed, weights, readout, *rotation_tables(head_dim))


def call(kernel, outputs, *operands, scalars=0, scratch=()):
    vmem = pl.BlockSpec(memory_space=pltpu.VMEM)
    smem = pl.BlockSpec(memory_space=pltpu.SMEM)
    return pl.pallas_call(
        kernel,
        out_shape=[jax.ShapeDtypeStruct(*output) for output in outputs],
        in_specs=[smem] * scalars + [vmem] * (len(operands) - scalars),
        out_specs=[vmem] * len(outputs),
        scratch_shapes=scratch,
        compiler_params=pltpu.CompilerParams(vmem_limit_bytes=16 * 1024 * 1024),
    )(*operands)


def start_kernel(hidden_ref, out_ref, active_ref, time_ref, first_ref):
    hidden = hidden_ref[...]
    lat_dim = out_ref.shape[0]
    partial = dot_rows(out_ref[...], hidden)
    wide = hidden.astype(jnp.float32)
    ones = jnp.ones((8, hidden.shape[1]), jnp.bfloat16)
    high, low = split(wide * wide)
    squares = dot_rows(ones, high) + dot_rows(ones, low)
    modulation = lax.dot_general(
        jnp.broadcast_to(active_ref[...], (8, active_ref.shape[1])),
        time_ref[...],
        (((1,), (1,)), ((), ())),
        precision=lax.Precision.HIGHEST,
        preferred_element_type=jnp.float32,
    )
    lanes = hidden.shape[0]
    modulation = jnp.concatenate(
        [modulation, jnp.zeros((8, lanes - modulation.shape[1]), jnp.float32)], axis=1
    )
    row = lax.broadcasted_iota(jnp.int32, (8, lanes), 0)
    extra = jnp.where(row == 0, squares, modulation)
    for peer in range(first_ref.shape[0]):
        first_ref[peer, :lat_dim, :] = partial
        first_ref[peer, lat_dim:, :] = extra


def noise_kernel(level_ref, first_ref, noise_ref, order_ref, second_ref, kept_ref, pair, extra):
    f32 = jnp.float32
    level = level_ref[0]
    peers, used, lanes = first_ref.shape
    lat_dim = noise_ref.shape[0]
    mod_width = 40
    total = first_ref[0]
    for peer in range(1, peers):
        total = total + first_ref[peer]
    projected = total[:lat_dim]
    root_mean = jnp.sqrt(total[lat_dim : lat_dim + 1] / D + EPS_NORM)
    latent = projected / root_mean
    noisy = ((1.0 - level) * latent + level * noise_ref[...].astype(f32)).astype(jnp.bfloat16)
    kept_ref[:lat_dim, :] = projected
    kept_ref[lat_dim : 2 * lat_dim, :] = latent - noisy.astype(f32)
    kept_ref[2 * lat_dim :, :] = jnp.broadcast_to(root_mean, (8, lanes))
    pair[...] = jnp.zeros_like(pair)
    for peer in range(peers):
        at = slice(peer * mod_width, (peer + 1) * mod_width)
        row = first_ref[peer, lat_dim : lat_dim + 8, :]
        pair[0:1, at] = row[1:2, :mod_width]
        pair[1:2, at] = row[1:2, mod_width : 2 * mod_width]
    order = order_ref[...]
    extra[...] = jnp.zeros_like(extra)
    extra[0:1, :] = (order // 64).astype(f32)
    extra[1:2, :] = (order % 64).astype(f32)
    for index in range(2):
        for half in range(2):
            part = pair[index : index + 1, half * lanes : (half + 1) * lanes]
            high = part.astype(jnp.bfloat16).astype(f32)
            at = 2 + 2 * index + half
            extra[at : at + 1, :] = high
            extra[at + 4 : at + 5, :] = part - high
    rows = jnp.concatenate([noisy, extra[...].astype(jnp.bfloat16)], axis=0)
    for peer in range(second_ref.shape[0]):
        second_ref[peer] = rows


def heads_kernel(scores_ref, score_ref):
    total = jnp.sum(scores_ref[...].astype(jnp.float32), axis=0)
    for peer in range(score_ref.shape[0]):
        score_ref[peer] = total


def gradient_kernel(level_ref, score_ref, kept_ref, hidden_ref, third_ref, side_ref):
    f32 = jnp.float32
    level = level_ref[0]
    peers, half, lanes = score_ref.shape
    parts = peers // 4
    lat_dim = lanes // 2
    left = lax.broadcasted_iota(jnp.int32, (half, lanes), 1) < lat_dim
    pieces = []
    for part in range(parts):
        realistic = GUIDANCE * score_ref[parts + part] + (1.0 - GUIDANCE) * score_ref[2 * parts + part]
        difference = score_ref[3 * parts + part] - realistic
        pieces.append(jnp.where(left, difference, pltpu.roll(realistic, lat_dim, 1)))
        pieces.append(jnp.where(left, pltpu.roll(difference, lat_dim, 1), realistic))
    both = jnp.concatenate(pieces, axis=0).T
    difference = both[:lat_dim]
    realistic = both[lat_dim:]
    projected = kept_ref[:lat_dim, :]
    root_mean = kept_ref[2 * lat_dim : 2 * lat_dim + 1, :]
    distance = jnp.abs(kept_ref[lat_dim : 2 * lat_dim, :] + level * realistic)
    magnitude = jnp.sum(jnp.sum(distance, axis=0, keepdims=True), axis=1, keepdims=True)
    direction = difference / root_mean
    high, low = split(direction)
    hidden = hidden_ref[...]
    weight_part = dot32(high, hidden) + dot32(low, hidden)

    row = lax.broadcasted_iota(jnp.int32, (8, lat_dim), 0)
    first = magnitude.astype(jnp.bfloat16).astype(f32)
    second = (magnitude - first).astype(jnp.bfloat16).astype(f32)
    third = magnitude - first - second
    extra = jnp.where(row == 0, first, jnp.where(row == 1, second, jnp.where(row == 2, third, 0.0)))
    groups = third_ref.shape[0] // (lat_dim // 8)
    width = weight_part.shape[1] // groups
    for group in range(groups):
        columns = weight_part[:, group * width : (group + 1) * width]
        for block in range(lat_dim // 8):
            third_ref[block * groups + group] = jnp.concatenate(
                [columns[8 * block : 8 * (block + 1)], extra], axis=1
            ).astype(jnp.bfloat16)

    coefficient = jnp.sum(difference * projected, axis=0, keepdims=True) / (
        D * root_mean * root_mean * root_mean
    )
    side_ref[...] = jnp.concatenate(
        [direction, jnp.broadcast_to(coefficient, (lat_dim, lanes))], axis=0
    ).T


def scale_kernel(cells, rows, level_ref, third_ref, fourth_ref, factor_ref):
    total = jnp.sum(third_ref[...].astype(jnp.float32), axis=0)
    width = total.shape[1] - 64
    sums = total[:, width : width + 1]
    spread = (sums[0:1] + sums[1:2] + sums[2:3]) / cells + EPS_MEAN
    factor = -level_ref[0] / spread
    factor_ref[...] = jnp.broadcast_to(factor, factor_ref.shape)
    scaled = (total * (factor / math.sqrt(rows))).astype(jnp.bfloat16)
    for peer in range(fourth_ref.shape[0]):
        fourth_ref[peer] = scaled


def weight_kernel(fourth_ref, weight_ref):
    lat_dim, columns = weight_ref.shape
    groups = fourth_ref.shape[0] // (lat_dim // 8)
    width = columns // groups
    for block in range(lat_dim // 8):
        parts = [
            fourth_ref[block * groups + group].astype(jnp.float32)[:, :width]
            for group in range(groups)
        ]
        weight_ref[8 * block : 8 * (block + 1), :] = jnp.concatenate(parts, axis=1)


def hidden_kernel(factor_ref, side_ref, hidden_ref, out_ref, grad_ref):
    lat_dim = out_ref.shape[0]
    high, low = split(side_ref[:, :lat_dim])
    backward = dot32(high, out_ref[...]) + dot32(low, out_ref[...])
    coefficient = side_ref[:, lat_dim : lat_dim + 1]
    factor = factor_ref[0:1, 0:1]
    grad_ref[...] = (
        factor * (backward - hidden_ref[...].astype(jnp.float32) * coefficient)
    ).astype(jnp.bfloat16)


def body(
    gen_hidden,
    out_weight,
    noise,
    step_index,
    token_order,
    time_weight,
    embed_weight,
    qkv_weight,
    readout_weight,
):
    seq_count = lax.axis_size("seq")
    mp_count = lax.axis_size("mp")
    role_count = lax.axis_size("role")
    mp_index = lax.axis_index("mp")
    local_rows, columns = gen_hidden.shape
    lat_dim = out_weight.shape[1]
    bf16, f32 = jnp.bfloat16, jnp.float32
    timestep = step_index[0].astype(f32)
    level = (timestep / T_STEPS)[None]
    out_turned = out_weight.T

    half_freq = FREQ // 2
    frequencies = jnp.exp(-math.log(ROPE_BASE) * jnp.arange(half_freq, dtype=f32) / half_freq)
    phases = timestep * frequencies
    activated = jax.nn.silu(jnp.concatenate([jnp.cos(phases), jnp.sin(phases)]))
    time_turned = time_weight[0].transpose(1, 2, 0).reshape(-1, FREQ)

    (first,) = call(
        start_kernel,
        [((mp_count, lat_dim + 8, local_rows), f32)],
        gen_hidden,
        out_turned,
        activated[None],
        time_turned,
    )
    first = exchange(first, "mp")

    second, kept = call(
        noise_kernel,
        [((seq_count, lat_dim + 16, local_rows), bf16), ((2 * lat_dim + 8, local_rows), f32)],
        level,
        first,
        noise.T,
        token_order[None],
        scalars=1,
        scratch=[pltpu.VMEM((8, 2 * local_rows), f32), pltpu.VMEM((16, local_rows), f32)],
    )
    second = exchange(second, "seq")
    scores = run_pass(
        mp_index.astype(jnp.int32)[None],
        second,
        embed_weight[0],
        qkv_weight[0, 0],
        readout_weight[0, 0].T,
    )

    scores = exchange(scores, "seq")
    quarter = local_rows // mp_count
    peers = role_count * mp_count
    (score,) = call(heads_kernel, [((peers, quarter // 2, 2 * lat_dim), f32)], scores)

    score = exchange(score, ("role", "mp"))

    width = columns // 4 + lat_dim
    third, side = call(
        gradient_kernel,
        [((seq_count, 8, width), bf16), ((local_rows, 2 * lat_dim), f32)],
        level,
        score,
        kept,
        gen_hidden,
        scalars=1,
    )

    third = exchange(third, "seq")
    cells = local_rows * seq_count * lat_dim
    fourth, factor = call(
        functools.partial(scale_kernel, cells, local_rows * seq_count),
        [((seq_count, 8, width), bf16), ((8, 128), f32)],
        level,
        third,
        scalars=1,
    )
    fourth = exchange(fourth, "seq")
    (hidden_grad,) = call(
        hidden_kernel, [((local_rows, columns), bf16)], factor, side, gen_hidden, out_turned
    )
    (weight_grad,) = call(weight_kernel, [((lat_dim, columns), f32)], fourth)
    return (hidden_grad, weight_grad.T)


def solution(mesh):
    placed = (
        P("seq", "mp"),
        P("mp", None),
        P("seq", None),
        P(),
        P("seq"),
        P("role", None, None, ("seq", "mp")),
        P("role", None, None),
        P("role", "seq", None, None),
        P("role", "seq", None, None),
    )
    return jax.shard_map(
        body, mesh=mesh, in_specs=placed, out_specs=(P("seq", "mp"), P("mp", None)), check_vma=False
    )
```

```python
import functools
import math

import jax
import jax.numpy as jnp
import numpy as np
from jax import lax
from jax.experimental import pallas as pl
from jax.experimental.pallas import tpu as pltpu
from jax.sharding import PartitionSpec as P

D = 5120
FREQ = 256
T_STEPS = 1000


EPS_NORM = 1e-06
EPS_MEAN = 1e-05
GUIDANCE = 5.0
ROPE_BASE = 10000.0
SHARPNESS = 4.0
VMEM_LIMIT = 61 * 1024 * 1024
CHUNK = 1024


def split(values):
    high = values.astype(jnp.bfloat16)
    return high, (values - high.astype(jnp.float32)).astype(jnp.bfloat16)


def exchange(chunks, axes):
    return lax.all_to_all(chunks, axes, 0, 0, tiled=True)


def dot32(left, right):
    return jnp.dot(left, right, preferred_element_type=jnp.float32)


def dot_rows(left, right):
    return lax.dot_general(
        left, right, (((1,), (1,)), ((), ())), preferred_element_type=jnp.float32
    )


def fetch_all(arrived, *pairs):
    fetches = [
        pltpu.make_async_copy(source, target, arrived.at[index])
        for index, (source, target) in enumerate(pairs)
    ]
    for fetch in fetches:
        fetch.start()
    return fetches


def rotation_tables(head_dim):
    turns = ROPE_BASE ** (-2.0 * np.arange(head_dim // 2) / head_dim) / (2.0 * np.pi)
    grain = 2.0 ** (np.floor(np.log2(turns)) - 11)
    high = np.floor(turns / grain) * grain
    both = np.concatenate([high, turns - high])
    return np.ascontiguousarray(np.broadcast_to(both[:, None], (head_dim, 128)), np.float32)


def rotations(positions, table):
    table = jnp.concatenate([table] * (positions.shape[1] // table.shape[1]), axis=1)
    high = table[: table.shape[0] // 2]
    low = table[table.shape[0] // 2 :]
    whole = positions * high
    part = (whole - jnp.round(whole)) + positions * low
    angle = (part - jnp.round(part)) * math.pi
    square = angle * angle
    sine = square * (-1.0 / 39916800) + 1.0 / 362880
    sine = sine * square - 1.0 / 5040
    sine = sine * square + 1.0 / 120
    sine = sine * square - 1.0 / 6
    sine = (sine * square + 1.0) * angle
    cosine = square * (1.0 / 479001600) - 1.0 / 3628800
    cosine = cosine * square + 1.0 / 40320
    cosine = cosine * square - 1.0 / 720
    cosine = cosine * square + 1.0 / 24
    cosine = cosine * square - 0.5
    cosine = cosine * square + 1.0
    return 1.0 - 2.0 * sine * sine, 2.0 * sine * cosine


def normalize_rope(vectors, cosines, sines):
    rescaled = vectors * lax.rsqrt(jnp.mean(vectors * vectors, axis=0, keepdims=True) + EPS_NORM)
    width = vectors.shape[0] // 2
    front = rescaled[:width]
    back = rescaled[width:]
    return jnp.concatenate([front * cosines - back * sines, front * sines + back * cosines], axis=0)


def pass_kernel(
    place_ref,
    gathered_ref,
    embed_in,
    weight_in,
    readout_in,
    table_in,
    score_ref,
    modulation,
    scaled,
    clip,
    places,
    own,
    own_places,
    query,
    key,
    wide,
    attended,
    embed_ref,
    weight_ref,
    readout_ref,
    table_ref,
    arrived,
):
    f32 = jnp.float32
    fetches = fetch_all(
        arrived,
        (embed_in, embed_ref),
        *(
            (weight_in.at[pl.ds(begin, CHUNK), :], weight_ref.at[pl.ds(begin, CHUNK), :])
            for begin in range(0, weight_ref.shape[0], CHUNK)
        ),
        (table_in, table_ref),
        (readout_in, readout_ref),
    )
    blocks, used, lanes = gathered_ref.shape
    lat_dim, width = embed_ref.shape
    head_dim = weight_ref.shape[1] // 3
    key_rows = blocks * lanes
    query_rows = query.shape[0]
    quarter = query_rows // blocks
    per_tile = lanes // quarter
    piece = width // blocks
    place = place_ref[0]

    for block in range(blocks):
        at = slice(block * lanes, (block + 1) * lanes)
        received = gathered_ref[block]
        clip[:lat_dim, at] = received[:lat_dim]
        clip[lat_dim:, at] = received[:lat_dim]
        extra = received[lat_dim:].astype(f32)
        places[0:1, at] = extra[0:1] * 64.0 + extra[1:2]
        pair = extra[2:4] + extra[4:6]
        tail = extra[6:7] + pltpu.roll(extra[6:7], lanes // 2, 1)
        begin = block * piece
        rest = piece - lanes
        modulation[0:2, begin : begin + lanes] = pair
        modulation[0:1, begin + lanes : begin + piece] = tail[:, :rest]
        modulation[1:2, begin + lanes : begin + piece] = tail[:, rest : 2 * rest]

    lane = lax.broadcasted_iota(jnp.int32, (used, lanes), 1)
    for tile in range(blocks // per_tile):
        found = jnp.zeros((used, lanes), f32)
        for part in range(per_tile):
            block = gathered_ref[tile * per_tile + part].astype(f32)
            shift = lax.rem((part - place + per_tile) * quarter, lanes)
            found = jnp.where(lane // quarter == part, pltpu.roll(block, shift, 1), found)
        at = slice(tile * lanes, (tile + 1) * lanes)
        rows = found[:lat_dim].astype(jnp.bfloat16)
        own[:lat_dim, at] = rows
        own[lat_dim:, at] = rows
        own_places[0:1, at] = found[lat_dim : lat_dim + 1] * 64.0 + found[lat_dim + 1 : lat_dim + 2]

    fetches[0].wait()
    folded = jnp.zeros((2 * lat_dim + 16, 3 * head_dim), f32)
    for begin in range(0, width, CHUNK):
        at = slice(begin, begin + CHUNK)
        high, low = split(embed_ref[:, at].astype(f32) * (1.0 + modulation[1:2, at]))
        scaled[:lat_dim, at] = high
        scaled[lat_dim : 2 * lat_dim, at] = low
        row = lax.broadcasted_iota(jnp.int32, (16, CHUNK), 0)
        shifted = jnp.broadcast_to(modulation[0:1, at], (16, CHUNK))
        shifted_high = shifted.astype(jnp.bfloat16).astype(f32)
        shifted = jnp.where(row == 0, shifted_high, shifted - shifted_high)
        scaled[2 * lat_dim :, at] = jnp.where(row < 2, shifted, 0.0).astype(jnp.bfloat16)
        fetches[1 + begin // CHUNK].wait()
        folded = folded + dot32(scaled[:, at], weight_ref[at, :])
    gram = dot_rows(embed_ref[...], embed_ref[...])
    matrix = folded[:lat_dim] + folded[lat_dim : 2 * lat_dim]
    offset = folded[2 * lat_dim : 2 * lat_dim + 1] + folded[2 * lat_dim + 1 : 2 * lat_dim + 2]
    turned = jnp.concatenate(
        [matrix, jnp.broadcast_to(offset, (lanes - lat_dim, 3 * head_dim))], axis=0
    ).T
    offsets = jnp.broadcast_to(turned[:, lat_dim : lat_dim + 1], (3 * head_dim, lanes))
    matrix_parts = jnp.concatenate(split(turned[:, :lat_dim]), axis=1)
    gram_parts = jnp.concatenate(split(gram), axis=1)

    def project(parts, offsets, rows):
        product = dot32(jnp.concatenate([parts, gram_parts], axis=0), rows)
        count = parts.shape[0]
        mean = jnp.sum(rows[:lat_dim].astype(f32) * product[count:], axis=0, keepdims=True) / width
        offsets = jnp.concatenate([offsets] * (rows.shape[1] // lanes), axis=1)
        return product[:count] * lax.rsqrt(mean + EPS_NORM) + offsets

    step = 4 * lanes
    fetches[-2].wait()
    table = table_ref[...]
    wide[:, head_dim:] = jnp.ones((key_rows, head_dim), jnp.bfloat16)
    for begin in range(0, query_rows, step):
        at = slice(begin, begin + step)
        vectors = project(matrix_parts[:head_dim], offsets[:head_dim], own[:, at])
        turns = rotations(own_places[0:1, at], table)
        query[at, :] = normalize_rope(vectors, *turns).T.astype(jnp.bfloat16)

    def keys_and_values(index, carry):
        at = pl.ds(pl.multiple_of(index * step, step), step)
        vectors = project(matrix_parts[head_dim:], offsets[head_dim:], clip[:, at])
        turns = rotations(places[0:1, at], table)
        key[:, at] = normalize_rope(vectors[:head_dim], *turns).astype(jnp.bfloat16)
        wide[at, :head_dim] = vectors[head_dim:].T.astype(jnp.bfloat16)
        return carry

    lax.fori_loop(0, key_rows // step, keys_and_values, 0, unroll=True)

    rows = 512
    factor = SHARPNESS / math.sqrt(head_dim) * math.log2(math.e)

    def attend(index, carry):
        at = pl.ds(pl.multiple_of(index * rows, rows), rows)
        queries = query[at, :]
        total = jnp.zeros((rows, 2 * head_dim), f32)
        for begin in range(0, key_rows, step):
            scores = dot32(queries, key[:, begin : begin + step])
            exponents = jnp.exp2(scores * factor).astype(jnp.bfloat16)
            total = total + dot32(exponents, wide[begin : begin + step, :])
        result = (total[:, :head_dim] / total[:, head_dim:]).astype(jnp.bfloat16)
        attended[pl.ds(index * (rows // quarter), rows // quarter)] = result.reshape(
            rows // quarter, quarter, head_dim
        )
        return carry

    lax.fori_loop(0, query_rows // rows, attend, 0, unroll=True)
    half = quarter // 2
    fetches[-1].wait()
    halves = [
        dot_rows(attended[:, begin : begin + half, :].reshape(blocks * half, head_dim), readout_ref[...])
        for begin in (0, half)
    ]
    score_ref[...] = (
        jnp.concatenate(halves, axis=1).astype(jnp.bfloat16).reshape(blocks, half, 2 * lat_dim)
    )


def run_pass(place, gathered, embed, weights, readout):
    blocks, unused, lanes = gathered.shape
    lat_dim, width = embed.shape
    head_dim = weights.shape[1] // 3
    key_rows = blocks * lanes
    query_rows = key_rows // 4
    bf16, f32 = jnp.bfloat16, jnp.float32
    vmem = pl.BlockSpec(memory_space=pltpu.VMEM)
    return pl.pallas_call(
        pass_kernel,
        out_shape=jax.ShapeDtypeStruct((blocks, lanes // 8, lanes), bf16),
        in_specs=[
            pl.BlockSpec(memory_space=pltpu.SMEM),
            vmem,
        ]
        + [pl.BlockSpec(memory_space=pl.ANY)] * 4,
        out_specs=vmem,
        scratch_shapes=[
            pltpu.VMEM((8, width), f32),
            pltpu.VMEM((2 * lat_dim + 16, width), bf16),
            pltpu.VMEM((2 * lat_dim, key_rows), bf16),
            pltpu.VMEM((8, key_rows), f32),
            pltpu.VMEM((2 * lat_dim, query_rows), bf16),
            pltpu.VMEM((8, query_rows), f32),
            pltpu.VMEM((query_rows, head_dim), bf16),
            pltpu.VMEM((head_dim, key_rows), bf16),
            pltpu.VMEM((key_rows, 2 * head_dim), bf16),
            pltpu.VMEM((blocks, lanes // 4, head_dim), bf16),
            pltpu.VMEM(embed.shape, bf16),
            pltpu.VMEM(weights.shape, bf16),
            pltpu.VMEM(readout.shape, bf16),
            pltpu.VMEM((head_dim, 128), f32),
            pltpu.SemaphoreType.DMA((3 + width // CHUNK,)),
        ],
        compiler_params=pltpu.CompilerParams(vmem_limit_bytes=VMEM_LIMIT),
    )(place, gathered, embed, weights, readout, jnp.asarray(rotation_tables(head_dim)))


def call(kernel, outputs, *operands, scalars=0, fetched=0, scratch=()):
    vmem = pl.BlockSpec(memory_space=pltpu.VMEM)
    smem = pl.BlockSpec(memory_space=pltpu.SMEM)
    plain = len(operands) - scalars - fetched
    scratch = list(scratch)
    if fetched:
        scratch += [pltpu.VMEM(a.shape, a.dtype) for a in operands[-fetched:]]
        scratch.append(pltpu.SemaphoreType.DMA((fetched,)))
    return pl.pallas_call(
        kernel,
        out_shape=[jax.ShapeDtypeStruct(*output) for output in outputs],
        in_specs=[smem] * scalars + [vmem] * plain + [pl.BlockSpec(memory_space=pl.ANY)] * fetched,
        out_specs=[vmem] * len(outputs),
        scratch_shapes=scratch,
        compiler_params=pltpu.CompilerParams(
            vmem_limit_bytes=VMEM_LIMIT if fetched else 16 * 1024 * 1024
        ),
    )(*operands)


def start_kernel(
    active_ref, hidden_in, out_in, time_in, first_ref, hidden_ref, out_ref, time_ref, arrived
):
    fetches = fetch_all(arrived, (hidden_in, hidden_ref), (out_in, out_ref), (time_in, time_ref))
    lanes = hidden_ref.shape[0]
    lat_dim = out_ref.shape[0]
    active = jnp.broadcast_to(active_ref[...], (8, active_ref.shape[1]))
    fetches[2].wait()
    modulation = lax.dot_general(
        active,
        time_ref[...],
        (((1,), (1,)), ((), ())),
        precision=lax.Precision.HIGHEST,
        preferred_element_type=jnp.float32,
    )
    modulation = jnp.concatenate(
        [modulation, jnp.zeros((8, lanes - modulation.shape[1]), jnp.float32)], axis=1
    )
    fetches[0].wait()
    hidden = hidden_ref[...]
    wide = hidden.astype(jnp.float32)
    ones = jnp.ones((8, hidden.shape[1]), jnp.bfloat16)
    high, low = split(wide * wide)
    squares = dot_rows(ones, high) + dot_rows(ones, low)
    fetches[1].wait()
    partial = dot_rows(out_ref[...], hidden)
    row = lax.broadcasted_iota(jnp.int32, (8, lanes), 0)
    extra = jnp.where(row == 0, squares, modulation)
    for peer in range(first_ref.shape[0]):
        first_ref[peer, :lat_dim, :] = partial
        first_ref[peer, lat_dim:, :] = extra


def noise_kernel(
    level_ref,
    first_ref,
    noise_in,
    order_in,
    second_ref,
    kept_ref,
    pair,
    extra,
    noise_ref,
    order_ref,
    arrived,
):
    fetches = fetch_all(arrived, (noise_in, noise_ref), (order_in, order_ref))
    f32 = jnp.float32
    level = level_ref[0]
    peers, used, lanes = first_ref.shape
    lat_dim = noise_ref.shape[0]
    mod_width = 40
    total = first_ref[0]
    for peer in range(1, peers):
        total = total + first_ref[peer]
    projected = total[:lat_dim]
    root_mean = jnp.sqrt(total[lat_dim : lat_dim + 1] / D + EPS_NORM)
    latent = projected / root_mean
    kept_ref[:lat_dim, :] = projected
    kept_ref[2 * lat_dim :, :] = jnp.broadcast_to(root_mean, (8, lanes))
    pair[...] = jnp.zeros_like(pair)
    for peer in range(peers):
        at = slice(peer * mod_width, (peer + 1) * mod_width)
        row = first_ref[peer, lat_dim : lat_dim + 8, :]
        pair[0:1, at] = row[1:2, :mod_width]
        pair[1:2, at] = row[1:2, mod_width : 2 * mod_width]
    rest = peers * mod_width - lanes
    head = pair[0:2, :lanes]
    head_high = head.astype(jnp.bfloat16).astype(f32)
    tail = jnp.concatenate([pair[0:1, lanes : lanes + rest], pair[1:2, lanes : lanes + rest]], axis=1)
    tail_high = tail.astype(jnp.bfloat16).astype(f32)
    extra[2:4, :] = head_high
    extra[4:6, :] = head - head_high
    extra[6:7, :] = jnp.concatenate([tail_high, tail - tail_high], axis=1)
    extra[7:8, :] = jnp.zeros((1, lanes), f32)
    fetches[1].wait()
    order = order_ref[...]
    extra[0:1, :] = (order // 64).astype(f32)
    extra[1:2, :] = (order % 64).astype(f32)
    fetches[0].wait()
    noisy = ((1.0 - level) * latent + level * noise_ref[...].astype(f32)).astype(jnp.bfloat16)
    kept_ref[lat_dim : 2 * lat_dim, :] = latent - noisy.astype(f32)
    rows = jnp.concatenate([noisy, extra[...].astype(jnp.bfloat16)], axis=0)
    for peer in range(second_ref.shape[0]):
        second_ref[peer] = rows


def heads_kernel(scores_ref, score_ref):
    total = jnp.sum(scores_ref[...].astype(jnp.float32), axis=0)
    for peer in range(score_ref.shape[0]):
        score_ref[peer] = total


def gradient_kernel(level_ref, score_ref, kept_ref, hidden_ref, third_ref, side_ref):
    f32 = jnp.float32
    level = level_ref[0]
    peers, half, lanes = score_ref.shape
    parts = peers // 4
    lat_dim = lanes // 2
    left = lax.broadcasted_iota(jnp.int32, (half, lanes), 1) < lat_dim
    pieces = []
    for part in range(parts):
        realistic = GUIDANCE * score_ref[parts + part] + (1.0 - GUIDANCE) * score_ref[2 * parts + part]
        difference = score_ref[3 * parts + part] - realistic
        pieces.append(jnp.where(left, difference, pltpu.roll(realistic, lat_dim, 1)))
        pieces.append(jnp.where(left, pltpu.roll(difference, lat_dim, 1), realistic))
    both = jnp.concatenate(pieces, axis=0).T
    difference = both[:lat_dim]
    realistic = both[lat_dim:]
    projected = kept_ref[:lat_dim, :]
    root_mean = kept_ref[2 * lat_dim : 2 * lat_dim + 1, :]
    distance = jnp.abs(kept_ref[lat_dim : 2 * lat_dim, :] + level * realistic)
    magnitude = jnp.sum(jnp.sum(distance, axis=0, keepdims=True), axis=1, keepdims=True)
    direction = difference / root_mean
    high, low = split(direction)
    hidden = hidden_ref[...]
    weight_part = dot32(high, hidden) + dot32(low, hidden)

    row = lax.broadcasted_iota(jnp.int32, (8, lat_dim), 0)
    first = magnitude.astype(jnp.bfloat16).astype(f32)
    second = (magnitude - first).astype(jnp.bfloat16).astype(f32)
    third = magnitude - first - second
    extra = jnp.where(row == 0, first, jnp.where(row == 1, second, jnp.where(row == 2, third, 0.0)))
    groups = third_ref.shape[0] // (lat_dim // 8)
    width = weight_part.shape[1] // groups
    for group in range(groups):
        columns = weight_part[:, group * width : (group + 1) * width]
        for block in range(lat_dim // 8):
            third_ref[block * groups + group] = jnp.concatenate(
                [columns[8 * block : 8 * (block + 1)], extra], axis=1
            ).astype(jnp.bfloat16)

    coefficient = jnp.sum(difference * projected, axis=0, keepdims=True) / (
        D * root_mean * root_mean * root_mean
    )
    side_ref[...] = jnp.concatenate(
        [direction, jnp.broadcast_to(coefficient, (lat_dim, lanes))], axis=0
    ).T


def scale_kernel(cells, rows, level_ref, third_ref, fourth_ref, factor_ref):
    total = jnp.sum(third_ref[...].astype(jnp.float32), axis=0)
    width = total.shape[1] - 64
    sums = total[:, width : width + 1]
    spread = (sums[0:1] + sums[1:2] + sums[2:3]) / cells + EPS_MEAN
    factor = -level_ref[0] / spread
    factor_ref[...] = jnp.broadcast_to(factor, factor_ref.shape)
    scaled = (total * (factor / math.sqrt(rows))).astype(jnp.bfloat16)
    for peer in range(fourth_ref.shape[0]):
        fourth_ref[peer] = scaled


def weight_kernel(fourth_ref, weight_ref):
    lat_dim, columns = weight_ref.shape
    groups = fourth_ref.shape[0] // (lat_dim // 8)
    width = columns // groups
    for block in range(lat_dim // 8):
        parts = [
            fourth_ref[block * groups + group].astype(jnp.float32)[:, :width]
            for group in range(groups)
        ]
        weight_ref[8 * block : 8 * (block + 1), :] = jnp.concatenate(parts, axis=1)


def hidden_kernel(factor_ref, side_ref, hidden_ref, out_ref, grad_ref):
    lat_dim = out_ref.shape[0]
    high, low = split(side_ref[:, :lat_dim])
    backward = dot32(high, out_ref[...]) + dot32(low, out_ref[...])
    coefficient = side_ref[:, lat_dim : lat_dim + 1]
    factor = factor_ref[0:1, 0:1]
    grad_ref[...] = (
        factor * (backward - hidden_ref[...].astype(jnp.float32) * coefficient)
    ).astype(jnp.bfloat16)


def body(
    gen_hidden,
    out_weight,
    noise,
    step_index,
    token_order,
    time_weight,
    embed_weight,
    qkv_weight,
    readout_weight,
):
    seq_count = lax.axis_size("seq")
    mp_count = lax.axis_size("mp")
    role_count = lax.axis_size("role")
    mp_index = lax.axis_index("mp")
    local_rows, columns = gen_hidden.shape
    lat_dim = out_weight.shape[1]
    bf16, f32 = jnp.bfloat16, jnp.float32
    timestep = step_index[0].astype(f32)
    level = (timestep / T_STEPS)[None]
    out_turned = out_weight.T

    half_freq = FREQ // 2
    frequencies = jnp.exp(-math.log(ROPE_BASE) * jnp.arange(half_freq, dtype=f32) / half_freq)
    phases = timestep * frequencies
    activated = jax.nn.silu(jnp.concatenate([jnp.cos(phases), jnp.sin(phases)]))
    time_turned = time_weight[0].transpose(1, 2, 0).reshape(-1, FREQ)

    (first,) = call(
        start_kernel,
        [((mp_count, lat_dim + 8, local_rows), f32)],
        activated[None],
        gen_hidden,
        out_turned,
        time_turned,
        fetched=3,
    )
    first = exchange(first, "mp")

    second, kept = call(
        noise_kernel,
        [((seq_count, lat_dim + 8, local_rows), bf16), ((2 * lat_dim + 8, local_rows), f32)],
        level,
        first,
        noise.T,
        token_order[None],
        scalars=1,
        fetched=2,
        scratch=[pltpu.VMEM((8, 2 * local_rows), f32), pltpu.VMEM((8, local_rows), f32)],
    )
    second = exchange(second, "seq")
    scores = run_pass(
        mp_index.astype(jnp.int32)[None],
        second,
        embed_weight[0],
        qkv_weight[0, 0],
        readout_weight[0, 0].T,
    )

    scores = exchange(scores, "seq")
    quarter = local_rows // mp_count
    peers = role_count * mp_count
    (score,) = call(heads_kernel, [((peers, quarter // 2, 2 * lat_dim), f32)], scores)

    score = exchange(score, ("role", "mp"))

    width = columns // 4 + lat_dim
    third, side = call(
        gradient_kernel,
        [((seq_count, 8, width), bf16), ((local_rows, 2 * lat_dim), f32)],
        level,
        score,
        kept,
        gen_hidden,
        scalars=1,
    )

    third = exchange(third, "seq")
    cells = local_rows * seq_count * lat_dim
    fourth, factor = call(
        functools.partial(scale_kernel, cells, local_rows * seq_count),
        [((seq_count, 8, width), bf16), ((8, 128), f32)],
        level,
        third,
        scalars=1,
    )
    fourth = exchange(fourth, "seq")
    (hidden_grad,) = call(
        hidden_kernel, [((local_rows, columns), bf16)], factor, side, gen_hidden, out_turned
    )
    (weight_grad,) = call(weight_kernel, [((lat_dim, columns), f32)], fourth)
    return (hidden_grad, weight_grad.T)


def solution(mesh):
    placed = (
        P("seq", "mp"),
        P("mp", None),
        P("seq", None),
        P(),
        P("seq"),
        P("role", None, None, ("seq", "mp")),
        P("role", None, None),
        P("role", "seq", None, None),
        P("role", "seq", None, None),
    )
    return jax.shard_map(
        body, mesh=mesh, in_specs=placed, out_specs=(P("seq", "mp"), P("mp", None)), check_vma=False
    )
```

```python
import functools
import math

import jax
import jax.numpy as jnp
import numpy as np
from jax import lax
from jax.experimental import pallas as pl
from jax.experimental.pallas import tpu as pltpu
from jax.sharding import PartitionSpec as P

D = 5120
FREQ = 256
T_STEPS = 1000


EPS_NORM = 1e-06
EPS_MEAN = 1e-05
GUIDANCE = 5.0
ROPE_BASE = 10000.0
SHARPNESS = 4.0
VMEM_LIMIT = 61 * 1024 * 1024
CHUNK = 1024


def split(values):
    high = values.astype(jnp.bfloat16)
    return high, (values - high.astype(jnp.float32)).astype(jnp.bfloat16)


def exchange(chunks, axes):
    return lax.all_to_all(chunks, axes, 0, 0, tiled=True)


def dot32(left, right):
    return jnp.dot(left, right, preferred_element_type=jnp.float32)


def dot_rows(left, right):
    return lax.dot_general(
        left, right, (((1,), (1,)), ((), ())), preferred_element_type=jnp.float32
    )


def fetch_all(arrived, *pairs):
    fetches = [
        pltpu.make_async_copy(source, target, arrived.at[index])
        for index, (source, target) in enumerate(pairs)
    ]
    for fetch in fetches:
        fetch.start()
    return fetches


def in_parts(turns):
    grain = 2.0 ** (np.floor(np.log2(turns)) - 11)
    high = np.floor(turns / grain) * grain
    return np.stack([high, turns - high]).astype(np.float32)


def rotation_tables(head_dim):
    turns = ROPE_BASE ** (-2.0 * np.arange(head_dim // 2) / head_dim) / (2.0 * np.pi)
    both = in_parts(turns).reshape(head_dim)
    return np.ascontiguousarray(np.broadcast_to(both[:, None], (head_dim, 128)))


def rotations(positions, table):
    table = jnp.concatenate([table] * (positions.shape[1] // table.shape[1]), axis=1)
    high = table[: table.shape[0] // 2]
    low = table[table.shape[0] // 2 :]
    whole = positions * high
    part = (whole - jnp.round(whole)) + positions * low
    angle = (part - jnp.round(part)) * math.pi
    square = angle * angle
    sine = square * (-1.0 / 39916800) + 1.0 / 362880
    sine = sine * square - 1.0 / 5040
    sine = sine * square + 1.0 / 120
    sine = sine * square - 1.0 / 6
    sine = (sine * square + 1.0) * angle
    cosine = square * (1.0 / 479001600) - 1.0 / 3628800
    cosine = cosine * square + 1.0 / 40320
    cosine = cosine * square - 1.0 / 720
    cosine = cosine * square + 1.0 / 24
    cosine = cosine * square - 0.5
    cosine = cosine * square + 1.0
    return 1.0 - 2.0 * sine * sine, 2.0 * sine * cosine


def normalize_rope(vectors, cosines, sines):
    rescaled = vectors * lax.rsqrt(jnp.mean(vectors * vectors, axis=0, keepdims=True) + EPS_NORM)
    width = vectors.shape[0] // 2
    front = rescaled[:width]
    back = rescaled[width:]
    return jnp.concatenate([front * cosines - back * sines, front * sines + back * cosines], axis=0)


def pass_kernel(
    place_ref,
    gathered_in,
    embed_in,
    weight_in,
    readout_in,
    table_in,
    score_ref,
    modulation,
    scaled,
    clip,
    places,
    own,
    own_places,
    query,
    key,
    wide,
    attended,
    gathered_ref,
    embed_ref,
    weight_ref,
    readout_ref,
    table_ref,
    arrived,
):
    f32 = jnp.float32
    fetches = fetch_all(
        arrived,
        (gathered_in, gathered_ref),
        (embed_in, embed_ref),
        *(
            (weight_in.at[pl.ds(begin, CHUNK), :], weight_ref.at[pl.ds(begin, CHUNK), :])
            for begin in range(0, weight_ref.shape[0], CHUNK)
        ),
        (table_in, table_ref),
        (readout_in, readout_ref),
    )
    blocks, used, lanes = gathered_ref.shape
    lat_dim, width = embed_ref.shape
    head_dim = weight_ref.shape[1] // 3
    key_rows = blocks * lanes
    query_rows = query.shape[0]
    quarter = query_rows // blocks
    per_tile = lanes // quarter
    piece = width // blocks
    place = place_ref[0]

    fetches[0].wait()
    for block in range(blocks):
        at = slice(block * lanes, (block + 1) * lanes)
        received = gathered_ref[block]
        clip[:lat_dim, at] = received[:lat_dim]
        clip[lat_dim:, at] = received[:lat_dim]
        extra = received[lat_dim:].astype(f32)
        places[0:1, at] = extra[0:1] * 64.0 + extra[1:2]
        pair = extra[2:4] + extra[4:6]
        tail = extra[6:7] + pltpu.roll(extra[6:7], lanes // 2, 1)
        begin = block * piece
        rest = piece - lanes
        modulation[0:2, begin : begin + lanes] = pair
        modulation[0:1, begin + lanes : begin + piece] = tail[:, :rest]
        modulation[1:2, begin + lanes : begin + piece] = tail[:, rest : 2 * rest]

    lane = lax.broadcasted_iota(jnp.int32, (used, lanes), 1)
    for tile in range(blocks // per_tile):
        found = jnp.zeros((used, lanes), f32)
        for part in range(per_tile):
            block = gathered_ref[tile * per_tile + part].astype(f32)
            shift = lax.rem((part - place + per_tile) * quarter, lanes)
            found = jnp.where(lane // quarter == part, pltpu.roll(block, shift, 1), found)
        at = slice(tile * lanes, (tile + 1) * lanes)
        rows = found[:lat_dim].astype(jnp.bfloat16)
        own[:lat_dim, at] = rows
        own[lat_dim:, at] = rows
        own_places[0:1, at] = found[lat_dim : lat_dim + 1] * 64.0 + found[lat_dim + 1 : lat_dim + 2]

    fetches[1].wait()
    folded = jnp.zeros((2 * lat_dim + 16, 3 * head_dim), f32)
    for begin in range(0, width, CHUNK):
        at = slice(begin, begin + CHUNK)
        high, low = split(embed_ref[:, at].astype(f32) * (1.0 + modulation[1:2, at]))
        scaled[:lat_dim, at] = high
        scaled[lat_dim : 2 * lat_dim, at] = low
        row = lax.broadcasted_iota(jnp.int32, (16, CHUNK), 0)
        shifted = jnp.broadcast_to(modulation[0:1, at], (16, CHUNK))
        shifted_high = shifted.astype(jnp.bfloat16).astype(f32)
        shifted = jnp.where(row == 0, shifted_high, shifted - shifted_high)
        scaled[2 * lat_dim :, at] = jnp.where(row < 2, shifted, 0.0).astype(jnp.bfloat16)
        fetches[2 + begin // CHUNK].wait()
        folded = folded + dot32(scaled[:, at], weight_ref[at, :])
    gram = dot_rows(embed_ref[...], embed_ref[...])
    matrix = folded[:lat_dim] + folded[lat_dim : 2 * lat_dim]
    offset = folded[2 * lat_dim : 2 * lat_dim + 1] + folded[2 * lat_dim + 1 : 2 * lat_dim + 2]
    turned = jnp.concatenate(
        [matrix, jnp.broadcast_to(offset, (lanes - lat_dim, 3 * head_dim))], axis=0
    ).T
    offsets = jnp.broadcast_to(turned[:, lat_dim : lat_dim + 1], (3 * head_dim, lanes))
    matrix_parts = jnp.concatenate(split(turned[:, :lat_dim]), axis=1)
    gram_parts = jnp.concatenate(split(gram), axis=1)

    def project(parts, offsets, rows):
        product = dot32(jnp.concatenate([parts, gram_parts], axis=0), rows)
        count = parts.shape[0]
        mean = jnp.sum(rows[:lat_dim].astype(f32) * product[count:], axis=0, keepdims=True) / width
        offsets = jnp.concatenate([offsets] * (rows.shape[1] // lanes), axis=1)
        return product[:count] * lax.rsqrt(mean + EPS_NORM) + offsets

    step = 4 * lanes
    fetches[-2].wait()
    table = table_ref[...]
    wide[:, head_dim:] = jnp.ones((key_rows, head_dim), jnp.bfloat16)
    for begin in range(0, query_rows, step):
        at = slice(begin, begin + step)
        vectors = project(matrix_parts[:head_dim], offsets[:head_dim], own[:, at])
        turns = rotations(own_places[0:1, at], table)
        query[at, :] = normalize_rope(vectors, *turns).T.astype(jnp.bfloat16)

    def keys_and_values(index, carry):
        at = pl.ds(pl.multiple_of(index * step, step), step)
        vectors = project(matrix_parts[head_dim:], offsets[head_dim:], clip[:, at])
        turns = rotations(places[0:1, at], table)
        key[:, at] = normalize_rope(vectors[:head_dim], *turns).astype(jnp.bfloat16)
        wide[at, :head_dim] = vectors[head_dim:].T.astype(jnp.bfloat16)
        return carry

    lax.fori_loop(0, key_rows // step, keys_and_values, 0, unroll=True)

    rows = 512
    factor = SHARPNESS / math.sqrt(head_dim) * math.log2(math.e)

    def attend(index, carry):
        at = pl.ds(pl.multiple_of(index * rows, rows), rows)
        queries = query[at, :]
        total = jnp.zeros((rows, 2 * head_dim), f32)
        for begin in range(0, key_rows, step):
            scores = dot32(queries, key[:, begin : begin + step])
            exponents = jnp.exp2(scores * factor).astype(jnp.bfloat16)
            total = total + dot32(exponents, wide[begin : begin + step, :])
        result = (total[:, :head_dim] / total[:, head_dim:]).astype(jnp.bfloat16)
        attended[pl.ds(index * (rows // quarter), rows // quarter)] = result.reshape(
            rows // quarter, quarter, head_dim
        )
        return carry

    lax.fori_loop(0, query_rows // rows, attend, 0, unroll=True)
    half = quarter // 2
    fetches[-1].wait()
    halves = [
        dot_rows(attended[:, begin : begin + half, :].reshape(blocks * half, head_dim), readout_ref[...])
        for begin in (0, half)
    ]
    score_ref[...] = (
        jnp.concatenate(halves, axis=1).astype(jnp.bfloat16).reshape(blocks, half, 2 * lat_dim)
    )


def run_pass(place, gathered, embed, weights, readout):
    blocks, unused, lanes = gathered.shape
    lat_dim, width = embed.shape
    head_dim = weights.shape[1] // 3
    key_rows = blocks * lanes
    query_rows = key_rows // 4
    bf16, f32 = jnp.bfloat16, jnp.float32
    vmem = pl.BlockSpec(memory_space=pltpu.VMEM)
    return pl.pallas_call(
        pass_kernel,
        out_shape=jax.ShapeDtypeStruct((blocks, lanes // 8, lanes), bf16),
        in_specs=[pl.BlockSpec(memory_space=pltpu.SMEM)] + [pl.BlockSpec(memory_space=pl.ANY)] * 5,
        out_specs=vmem,
        scratch_shapes=[
            pltpu.VMEM((8, width), f32),
            pltpu.VMEM((2 * lat_dim + 16, width), bf16),
            pltpu.VMEM((2 * lat_dim, key_rows), bf16),
            pltpu.VMEM((8, key_rows), f32),
            pltpu.VMEM((2 * lat_dim, query_rows), bf16),
            pltpu.VMEM((8, query_rows), f32),
            pltpu.VMEM((query_rows, head_dim), bf16),
            pltpu.VMEM((head_dim, key_rows), bf16),
            pltpu.VMEM((key_rows, 2 * head_dim), bf16),
            pltpu.VMEM((blocks, lanes // 4, head_dim), bf16),
            pltpu.VMEM(gathered.shape, bf16),
            pltpu.VMEM(embed.shape, bf16),
            pltpu.VMEM(weights.shape, bf16),
            pltpu.VMEM(readout.shape, bf16),
            pltpu.VMEM((head_dim, 128), f32),
            pltpu.SemaphoreType.DMA((4 + width // CHUNK,)),
        ],
        compiler_params=pltpu.CompilerParams(vmem_limit_bytes=VMEM_LIMIT),
    )(place, gathered, embed, weights, readout, jnp.asarray(rotation_tables(head_dim)))


def call(kernel, outputs, *operands, scalars=0, fetched=0, scratch=()):
    vmem = pl.BlockSpec(memory_space=pltpu.VMEM)
    smem = pl.BlockSpec(memory_space=pltpu.SMEM)
    plain = len(operands) - scalars - fetched
    scratch = list(scratch)
    if fetched:
        scratch += [pltpu.VMEM(a.shape, a.dtype) for a in operands[-fetched:]]
        scratch.append(pltpu.SemaphoreType.DMA((fetched,)))
    return pl.pallas_call(
        kernel,
        out_shape=[jax.ShapeDtypeStruct(*output) for output in outputs],
        in_specs=[smem] * scalars + [vmem] * plain + [pl.BlockSpec(memory_space=pl.ANY)] * fetched,
        out_specs=[vmem] * len(outputs),
        scratch_shapes=scratch,
        compiler_params=pltpu.CompilerParams(
            vmem_limit_bytes=VMEM_LIMIT if fetched else 16 * 1024 * 1024
        ),
    )(*operands)


def start_kernel(
    time_ref,
    hidden_in,
    out_in,
    weight_in,
    table_in,
    first_ref,
    hidden_ref,
    out_ref,
    weight_ref,
    table_ref,
    arrived,
):
    fetches = fetch_all(
        arrived,
        (table_in, table_ref),
        (weight_in, weight_ref),
        (hidden_in, hidden_ref),
        (out_in, out_ref),
    )
    lanes = hidden_ref.shape[0]
    lat_dim = out_ref.shape[0]
    fetches[0].wait()
    waves = rotations(jnp.broadcast_to(time_ref[0], (1, lanes)), table_ref[...])
    active = jnp.concatenate([wave / (1.0 + jnp.exp(-wave)) for wave in waves], axis=1)
    fetches[1].wait()
    modulation = lax.dot_general(
        active,
        weight_ref[...],
        (((1,), (1,)), ((), ())),
        precision=lax.Precision.HIGHEST,
        preferred_element_type=jnp.float32,
    )
    modulation = jnp.concatenate(
        [modulation, jnp.zeros((8, lanes - modulation.shape[1]), jnp.float32)], axis=1
    )
    fetches[2].wait()
    hidden = hidden_ref[...]
    wide = hidden.astype(jnp.float32)
    ones = jnp.ones((8, hidden.shape[1]), jnp.bfloat16)
    high, low = split(wide * wide)
    squares = dot_rows(ones, high) + dot_rows(ones, low)
    fetches[3].wait()
    partial = dot_rows(out_ref[...], hidden)
    row = lax.broadcasted_iota(jnp.int32, (8, lanes), 0)
    extra = jnp.where(row == 0, squares, modulation)
    for peer in range(first_ref.shape[0]):
        first_ref[peer, :lat_dim, :] = partial
        first_ref[peer, lat_dim:, :] = extra


def noise_kernel(
    level_ref,
    first_in,
    noise_in,
    order_in,
    second_ref,
    kept_ref,
    pair,
    extra,
    first_ref,
    noise_ref,
    order_ref,
    arrived,
):
    fetches = fetch_all(
        arrived, (first_in, first_ref), (noise_in, noise_ref), (order_in, order_ref)
    )
    f32 = jnp.float32
    level = level_ref[0]
    peers, used, lanes = first_ref.shape
    lat_dim = noise_ref.shape[0]
    mod_width = 40
    fetches[0].wait()
    total = first_ref[0]
    for peer in range(1, peers):
        total = total + first_ref[peer]
    projected = total[:lat_dim]
    root_mean = jnp.sqrt(total[lat_dim : lat_dim + 1] / D + EPS_NORM)
    latent = projected / root_mean
    kept_ref[:lat_dim, :] = projected
    kept_ref[2 * lat_dim :, :] = jnp.broadcast_to(root_mean, (8, lanes))
    pair[...] = jnp.zeros_like(pair)
    for peer in range(peers):
        at = slice(peer * mod_width, (peer + 1) * mod_width)
        row = first_ref[peer, lat_dim : lat_dim + 8, :]
        pair[0:1, at] = row[1:2, :mod_width]
        pair[1:2, at] = row[1:2, mod_width : 2 * mod_width]
    rest = peers * mod_width - lanes
    head = pair[0:2, :lanes]
    head_high = head.astype(jnp.bfloat16).astype(f32)
    tail = jnp.concatenate([pair[0:1, lanes : lanes + rest], pair[1:2, lanes : lanes + rest]], axis=1)
    tail_high = tail.astype(jnp.bfloat16).astype(f32)
    extra[2:4, :] = head_high
    extra[4:6, :] = head - head_high
    extra[6:7, :] = jnp.concatenate([tail_high, tail - tail_high], axis=1)
    extra[7:8, :] = jnp.zeros((1, lanes), f32)
    fetches[2].wait()
    order = order_ref[...]
    extra[0:1, :] = (order // 64).astype(f32)
    extra[1:2, :] = (order % 64).astype(f32)
    fetches[1].wait()
    noisy = ((1.0 - level) * latent + level * noise_ref[...].astype(f32)).astype(jnp.bfloat16)
    kept_ref[lat_dim : 2 * lat_dim, :] = latent - noisy.astype(f32)
    rows = jnp.concatenate([noisy, extra[...].astype(jnp.bfloat16)], axis=0)
    for peer in range(second_ref.shape[0]):
        second_ref[peer] = rows


def heads_kernel(scores_ref, score_ref):
    total = jnp.sum(scores_ref[...].astype(jnp.float32), axis=0)
    for peer in range(score_ref.shape[0]):
        score_ref[peer] = total


def gradient_kernel(level_ref, score_ref, kept_ref, hidden_ref, third_ref, side_ref):
    f32 = jnp.float32
    level = level_ref[0]
    peers, half, lanes = score_ref.shape
    parts = peers // 4
    lat_dim = lanes // 2
    left = lax.broadcasted_iota(jnp.int32, (half, lanes), 1) < lat_dim
    pieces = []
    for part in range(parts):
        realistic = GUIDANCE * score_ref[parts + part] + (1.0 - GUIDANCE) * score_ref[2 * parts + part]
        difference = score_ref[3 * parts + part] - realistic
        pieces.append(jnp.where(left, difference, pltpu.roll(realistic, lat_dim, 1)))
        pieces.append(jnp.where(left, pltpu.roll(difference, lat_dim, 1), realistic))
    both = jnp.concatenate(pieces, axis=0).T
    difference = both[:lat_dim]
    realistic = both[lat_dim:]
    projected = kept_ref[:lat_dim, :]
    root_mean = kept_ref[2 * lat_dim : 2 * lat_dim + 1, :]
    distance = jnp.abs(kept_ref[lat_dim : 2 * lat_dim, :] + level * realistic)
    magnitude = jnp.sum(jnp.sum(distance, axis=0, keepdims=True), axis=1, keepdims=True)
    direction = difference / root_mean
    high, low = split(direction)
    hidden = hidden_ref[...]
    weight_part = dot32(high, hidden) + dot32(low, hidden)

    row = lax.broadcasted_iota(jnp.int32, (8, lat_dim), 0)
    first = magnitude.astype(jnp.bfloat16).astype(f32)
    second = (magnitude - first).astype(jnp.bfloat16).astype(f32)
    third = magnitude - first - second
    extra = jnp.where(row == 0, first, jnp.where(row == 1, second, jnp.where(row == 2, third, 0.0)))
    groups = third_ref.shape[0] // (lat_dim // 8)
    width = weight_part.shape[1] // groups
    for group in range(groups):
        columns = weight_part[:, group * width : (group + 1) * width]
        for block in range(lat_dim // 8):
            third_ref[block * groups + group] = jnp.concatenate(
                [columns[8 * block : 8 * (block + 1)], extra], axis=1
            ).astype(jnp.bfloat16)

    coefficient = jnp.sum(difference * projected, axis=0, keepdims=True) / (
        D * root_mean * root_mean * root_mean
    )
    side_ref[...] = jnp.concatenate(
        [direction, jnp.broadcast_to(coefficient, (lat_dim, lanes))], axis=0
    ).T


def scale_kernel(cells, rows, level_ref, third_ref, fourth_ref, factor_ref):
    total = jnp.sum(third_ref[...].astype(jnp.float32), axis=0)
    width = total.shape[1] - 64
    sums = total[:, width : width + 1]
    spread = (sums[0:1] + sums[1:2] + sums[2:3]) / cells + EPS_MEAN
    factor = -level_ref[0] / spread
    factor_ref[...] = jnp.broadcast_to(factor, factor_ref.shape)
    scaled = (total * (factor / math.sqrt(rows))).astype(jnp.bfloat16)
    for peer in range(fourth_ref.shape[0]):
        fourth_ref[peer] = scaled


def weight_kernel(fourth_ref, weight_ref):
    lat_dim, columns = weight_ref.shape
    groups = fourth_ref.shape[0] // (lat_dim // 8)
    width = columns // groups
    for block in range(lat_dim // 8):
        parts = [
            fourth_ref[block * groups + group].astype(jnp.float32)[:, :width]
            for group in range(groups)
        ]
        weight_ref[8 * block : 8 * (block + 1), :] = jnp.concatenate(parts, axis=1)


def hidden_kernel(factor_ref, side_ref, hidden_ref, out_ref, grad_ref):
    lat_dim = out_ref.shape[0]
    high, low = split(side_ref[:, :lat_dim])
    backward = dot32(high, out_ref[...]) + dot32(low, out_ref[...])
    coefficient = side_ref[:, lat_dim : lat_dim + 1]
    factor = factor_ref[0:1, 0:1]
    grad_ref[...] = (
        factor * (backward - hidden_ref[...].astype(jnp.float32) * coefficient)
    ).astype(jnp.bfloat16)


def body(
    gen_hidden,
    out_weight,
    noise,
    step_index,
    token_order,
    time_weight,
    embed_weight,
    qkv_weight,
    readout_weight,
):
    seq_count = lax.axis_size("seq")
    mp_count = lax.axis_size("mp")
    role_count = lax.axis_size("role")
    mp_index = lax.axis_index("mp")
    local_rows, columns = gen_hidden.shape
    lat_dim = out_weight.shape[1]
    bf16, f32 = jnp.bfloat16, jnp.float32
    timestep = step_index[0].astype(f32)
    level = (timestep / T_STEPS)[None]
    out_turned = out_weight.T

    time_turned = time_weight[0].transpose(1, 2, 0).reshape(-1, FREQ)
    turns = ROPE_BASE ** (-np.arange(FREQ // 2) / (FREQ // 2)) / (2.0 * np.pi)

    (first,) = call(
        start_kernel,
        [((mp_count, lat_dim + 8, local_rows), f32)],
        timestep[None],
        gen_hidden,
        out_turned,
        time_turned,
        jnp.asarray(np.repeat(in_parts(turns), 8, axis=0)),
        scalars=1,
        fetched=4,
    )
    first = exchange(first, "mp")

    second, kept = call(
        noise_kernel,
        [((seq_count, lat_dim + 8, local_rows), bf16), ((2 * lat_dim + 8, local_rows), f32)],
        level,
        first,
        noise.T,
        token_order[None],
        scalars=1,
        fetched=3,
        scratch=[pltpu.VMEM((8, 2 * local_rows), f32), pltpu.VMEM((8, local_rows), f32)],
    )
    second = exchange(second, "seq")
    scores = run_pass(
        mp_index.astype(jnp.int32)[None],
        second,
        embed_weight[0],
        qkv_weight[0, 0],
        readout_weight[0, 0].T,
    )

    scores = exchange(scores, "seq")
    quarter = local_rows // mp_count
    peers = role_count * mp_count
    (score,) = call(heads_kernel, [((peers, quarter // 2, 2 * lat_dim), f32)], scores)

    score = exchange(score, ("role", "mp"))

    width = columns // 4 + lat_dim
    third, side = call(
        gradient_kernel,
        [((seq_count, 8, width), bf16), ((local_rows, 2 * lat_dim), f32)],
        level,
        score,
        kept,
        gen_hidden,
        scalars=1,
    )

    third = exchange(third, "seq")
    cells = local_rows * seq_count * lat_dim
    fourth, factor = call(
        functools.partial(scale_kernel, cells, local_rows * seq_count),
        [((seq_count, 8, width), bf16), ((8, 128), f32)],
        level,
        third,
        scalars=1,
    )
    fourth = exchange(fourth, "seq")
    (hidden_grad,) = call(
        hidden_kernel, [((local_rows, columns), bf16)], factor, side, gen_hidden, out_turned
    )
    (weight_grad,) = call(weight_kernel, [((lat_dim, columns), f32)], fourth)
    return (hidden_grad, weight_grad.T)


def solution(mesh):
    placed = (
        P("seq", "mp"),
        P("mp", None),
        P("seq", None),
        P(),
        P("seq"),
        P("role", None, None, ("seq", "mp")),
        P("role", None, None),
        P("role", "seq", None, None),
        P("role", "seq", None, None),
    )
    return jax.shard_map(
        body, mesh=mesh, in_specs=placed, out_specs=(P("seq", "mp"), P("mp", None)), check_vma=False
    )
```

```python
import functools
import math

import jax
import jax.numpy as jnp
import numpy as np
from jax import lax
from jax.experimental import pallas as pl
from jax.experimental.pallas import tpu as pltpu
from jax.sharding import PartitionSpec as P

D = 5120
FREQ = 256
T_STEPS = 1000


EPS_NORM = 1e-06
EPS_MEAN = 1e-05
GUIDANCE = 5.0
ROPE_BASE = 10000.0
SHARPNESS = 4.0
VMEM_LIMIT = 61 * 1024 * 1024
CHUNK = 1024


def split(values):
    high = values.astype(jnp.bfloat16)
    return high, (values - high.astype(jnp.float32)).astype(jnp.bfloat16)


def exchange(chunks, axes):
    return lax.all_to_all(chunks, axes, 0, 0, tiled=True)


def dot32(left, right):
    return jnp.dot(left, right, preferred_element_type=jnp.float32)


def dot_rows(left, right):
    return lax.dot_general(
        left, right, (((1,), (1,)), ((), ())), preferred_element_type=jnp.float32
    )


def fetch_all(arrived, *pairs):
    fetches = [
        pltpu.make_async_copy(source, target, arrived.at[index])
        for index, (source, target) in enumerate(pairs)
    ]
    for fetch in fetches:
        fetch.start()
    return fetches


def in_parts(turns):
    grain = 2.0 ** (np.floor(np.log2(turns)) - 11)
    high = np.floor(turns / grain) * grain
    return np.stack([high, turns - high]).astype(np.float32)


def rotation_tables(head_dim):
    turns = ROPE_BASE ** (-2.0 * np.arange(head_dim // 2) / head_dim) / (2.0 * np.pi)
    both = in_parts(turns).reshape(head_dim)
    return np.ascontiguousarray(np.broadcast_to(both[:, None], (head_dim, 128)))


def rotations(positions, table):
    table = jnp.concatenate([table] * (positions.shape[1] // table.shape[1]), axis=1)
    high = table[: table.shape[0] // 2]
    low = table[table.shape[0] // 2 :]
    whole = positions * high
    part = (whole - jnp.round(whole)) + positions * low
    angle = (part - jnp.round(part)) * math.pi
    square = angle * angle
    sine = square * (-1.0 / 39916800) + 1.0 / 362880
    sine = sine * square - 1.0 / 5040
    sine = sine * square + 1.0 / 120
    sine = sine * square - 1.0 / 6
    sine = (sine * square + 1.0) * angle
    cosine = square * (1.0 / 479001600) - 1.0 / 3628800
    cosine = cosine * square + 1.0 / 40320
    cosine = cosine * square - 1.0 / 720
    cosine = cosine * square + 1.0 / 24
    cosine = cosine * square - 0.5
    cosine = cosine * square + 1.0
    return 1.0 - 2.0 * sine * sine, 2.0 * sine * cosine


def normalize_rope(vectors, cosines, sines):
    rescaled = vectors * lax.rsqrt(jnp.mean(vectors * vectors, axis=0, keepdims=True) + EPS_NORM)
    width = vectors.shape[0] // 2
    front = rescaled[:width]
    back = rescaled[width:]
    return jnp.concatenate([front * cosines - back * sines, front * sines + back * cosines], axis=0)


def pass_kernel(
    place_ref,
    gathered_ref,
    embed_ref,
    weight_ref,
    small_ref,
    score_ref,
    modulation,
    scaled,
    clip,
    places,
    own,
    own_places,
    query,
    key,
    wide,
    attended,
):
    f32 = jnp.float32
    blocks, used, lanes = gathered_ref.shape
    lat_dim, width = embed_ref.shape
    head_dim = weight_ref.shape[1] // 3
    key_rows = blocks * lanes
    query_rows = query.shape[0]
    quarter = query_rows // blocks
    per_tile = lanes // quarter
    piece = width // blocks
    place = place_ref[0]

    for block in range(blocks):
        at = slice(block * lanes, (block + 1) * lanes)
        received = gathered_ref[block]
        clip[:lat_dim, at] = received[:lat_dim]
        clip[lat_dim:, at] = received[:lat_dim]
        extra = received[lat_dim:].astype(f32)
        places[0:1, at] = extra[0:1] * 64.0 + extra[1:2]
        pair = extra[2:4] + extra[4:6]
        tail = extra[6:7] + pltpu.roll(extra[6:7], lanes // 2, 1)
        begin = block * piece
        rest = piece - lanes
        modulation[0:2, begin : begin + lanes] = pair
        modulation[0:1, begin + lanes : begin + piece] = tail[:, :rest]
        modulation[1:2, begin + lanes : begin + piece] = tail[:, rest : 2 * rest]

    lane = lax.broadcasted_iota(jnp.int32, (used, lanes), 1)
    for tile in range(blocks // per_tile):
        found = jnp.zeros((used, lanes), f32)
        for part in range(per_tile):
            block = gathered_ref[tile * per_tile + part].astype(f32)
            shift = lax.rem((part - place + per_tile) * quarter, lanes)
            found = jnp.where(lane // quarter == part, pltpu.roll(block, shift, 1), found)
        at = slice(tile * lanes, (tile + 1) * lanes)
        rows = found[:lat_dim].astype(jnp.bfloat16)
        own[:lat_dim, at] = rows
        own[lat_dim:, at] = rows
        own_places[0:1, at] = found[lat_dim : lat_dim + 1] * 64.0 + found[lat_dim + 1 : lat_dim + 2]

    folded = jnp.zeros((2 * lat_dim + 16, 3 * head_dim), f32)
    for begin in range(0, width, CHUNK):
        at = slice(begin, begin + CHUNK)
        high, low = split(embed_ref[:, at] * (1.0 + modulation[1:2, at]))
        scaled[:lat_dim, at] = high
        scaled[lat_dim : 2 * lat_dim, at] = low
        row = lax.broadcasted_iota(jnp.int32, (16, CHUNK), 0)
        shifted = jnp.broadcast_to(modulation[0:1, at], (16, CHUNK))
        shifted_high = shifted.astype(jnp.bfloat16).astype(f32)
        shifted = jnp.where(row == 0, shifted_high, shifted - shifted_high)
        scaled[2 * lat_dim :, at] = jnp.where(row < 2, shifted, 0.0).astype(jnp.bfloat16)
        folded = folded + dot32(scaled[:, at], weight_ref[at, :])
    embed = embed_ref[...].astype(jnp.bfloat16)
    gram = dot_rows(embed, embed)
    matrix = folded[:lat_dim] + folded[lat_dim : 2 * lat_dim]
    offset = folded[2 * lat_dim : 2 * lat_dim + 1] + folded[2 * lat_dim + 1 : 2 * lat_dim + 2]
    turned = jnp.concatenate(
        [matrix, jnp.broadcast_to(offset, (lanes - lat_dim, 3 * head_dim))], axis=0
    ).T
    offsets = jnp.broadcast_to(turned[:, lat_dim : lat_dim + 1], (3 * head_dim, lanes))
    matrix_parts = jnp.concatenate(split(turned[:, :lat_dim]), axis=1)
    gram_parts = jnp.concatenate(split(gram), axis=1)

    def project(parts, offsets, rows):
        product = dot32(jnp.concatenate([parts, gram_parts], axis=0), rows)
        count = parts.shape[0]
        mean = jnp.sum(rows[:lat_dim].astype(f32) * product[count:], axis=0, keepdims=True) / width
        offsets = jnp.concatenate([offsets] * (rows.shape[1] // lanes), axis=1)
        return product[:count] * lax.rsqrt(mean + EPS_NORM) + offsets

    step = 4 * lanes
    table = small_ref[lat_dim:, :]
    wide[:, head_dim:] = jnp.ones((key_rows, head_dim), jnp.bfloat16)
    for begin in range(0, query_rows, step):
        at = slice(begin, begin + step)
        vectors = project(matrix_parts[:head_dim], offsets[:head_dim], own[:, at])
        turns = rotations(own_places[0:1, at], table)
        query[at, :] = normalize_rope(vectors, *turns).T.astype(jnp.bfloat16)

    def keys_and_values(index, carry):
        at = pl.ds(pl.multiple_of(index * step, step), step)
        vectors = project(matrix_parts[head_dim:], offsets[head_dim:], clip[:, at])
        turns = rotations(places[0:1, at], table)
        key[:, at] = normalize_rope(vectors[:head_dim], *turns).astype(jnp.bfloat16)
        wide[at, :head_dim] = vectors[head_dim:].T.astype(jnp.bfloat16)
        return carry

    lax.fori_loop(0, key_rows // step, keys_and_values, 0, unroll=True)

    rows = 512
    factor = SHARPNESS / math.sqrt(head_dim) * math.log2(math.e)

    def attend(index, carry):
        at = pl.ds(pl.multiple_of(index * rows, rows), rows)
        queries = query[at, :]
        total = jnp.zeros((rows, 2 * head_dim), f32)
        for begin in range(0, key_rows, step):
            scores = dot32(queries, key[:, begin : begin + step])
            exponents = jnp.exp2(scores * factor).astype(jnp.bfloat16)
            total = total + dot32(exponents, wide[begin : begin + step, :])
        result = (total[:, :head_dim] / total[:, head_dim:]).astype(jnp.bfloat16)
        attended[pl.ds(index * (rows // quarter), rows // quarter)] = result.reshape(
            rows // quarter, quarter, head_dim
        )
        return carry

    lax.fori_loop(0, query_rows // rows, attend, 0, unroll=True)
    half = quarter // 2
    readout = small_ref[:lat_dim, :].astype(jnp.bfloat16)
    halves = [
        dot_rows(attended[:, begin : begin + half, :].reshape(blocks * half, head_dim), readout)
        for begin in (0, half)
    ]
    score_ref[...] = (
        jnp.concatenate(halves, axis=1).astype(jnp.bfloat16).reshape(blocks, half, 2 * lat_dim)
    )


def run_pass(place, gathered, embed, weights, small):
    blocks, unused, lanes = gathered.shape
    lat_dim, width = embed.shape
    head_dim = weights.shape[1] // 3
    key_rows = blocks * lanes
    query_rows = key_rows // 4
    bf16, f32 = jnp.bfloat16, jnp.float32
    vmem = pl.BlockSpec(memory_space=pltpu.VMEM)
    return pl.pallas_call(
        pass_kernel,
        out_shape=jax.ShapeDtypeStruct((blocks, lanes // 8, lanes), bf16),
        in_specs=[pl.BlockSpec(memory_space=pltpu.SMEM)] + [vmem] * 4,
        out_specs=vmem,
        scratch_shapes=[
            pltpu.VMEM((8, width), f32),
            pltpu.VMEM((2 * lat_dim + 16, width), bf16),
            pltpu.VMEM((2 * lat_dim, key_rows), bf16),
            pltpu.VMEM((8, key_rows), f32),
            pltpu.VMEM((2 * lat_dim, query_rows), bf16),
            pltpu.VMEM((8, query_rows), f32),
            pltpu.VMEM((query_rows, head_dim), bf16),
            pltpu.VMEM((head_dim, key_rows), bf16),
            pltpu.VMEM((key_rows, 2 * head_dim), bf16),
            pltpu.VMEM((blocks, lanes // 4, head_dim), bf16),
        ],
        compiler_params=pltpu.CompilerParams(vmem_limit_bytes=40 * 1024 * 1024),
    )(place, gathered, embed, weights, small)


def call(kernel, outputs, *operands, scalars=0, fetched=0, scratch=()):
    vmem = pl.BlockSpec(memory_space=pltpu.VMEM)
    smem = pl.BlockSpec(memory_space=pltpu.SMEM)
    plain = len(operands) - scalars - fetched
    scratch = list(scratch)
    if fetched:
        scratch += [pltpu.VMEM(a.shape, a.dtype) for a in operands[-fetched:]]
        scratch.append(pltpu.SemaphoreType.DMA((fetched,)))
    return pl.pallas_call(
        kernel,
        out_shape=[jax.ShapeDtypeStruct(*output) for output in outputs],
        in_specs=[smem] * scalars + [vmem] * plain + [pl.BlockSpec(memory_space=pl.ANY)] * fetched,
        out_specs=[vmem] * len(outputs),
        scratch_shapes=scratch,
        compiler_params=pltpu.CompilerParams(
            vmem_limit_bytes=VMEM_LIMIT if fetched else 16 * 1024 * 1024
        ),
    )(*operands)


def start_kernel(
    time_ref,
    hidden_in,
    out_in,
    weight_in,
    table_in,
    first_ref,
    hidden_ref,
    out_ref,
    weight_ref,
    table_ref,
    arrived,
):
    fetches = fetch_all(
        arrived,
        (table_in, table_ref),
        (weight_in, weight_ref),
        (hidden_in, hidden_ref),
        (out_in, out_ref),
    )
    lanes = hidden_ref.shape[0]
    lat_dim = out_ref.shape[0]
    fetches[0].wait()
    waves = rotations(jnp.broadcast_to(time_ref[0], (1, lanes)), table_ref[...])
    active = jnp.concatenate([wave / (1.0 + jnp.exp(-wave)) for wave in waves], axis=1)
    fetches[1].wait()
    modulation = lax.dot_general(
        active,
        weight_ref[...],
        (((1,), (1,)), ((), ())),
        precision=lax.Precision.HIGHEST,
        preferred_element_type=jnp.float32,
    )
    modulation = jnp.concatenate(
        [modulation, jnp.zeros((8, lanes - modulation.shape[1]), jnp.float32)], axis=1
    )
    fetches[2].wait()
    hidden = hidden_ref[...]
    wide = hidden.astype(jnp.float32)
    ones = jnp.ones((8, hidden.shape[1]), jnp.bfloat16)
    high, low = split(wide * wide)
    squares = dot_rows(ones, high) + dot_rows(ones, low)
    fetches[3].wait()
    partial = dot_rows(out_ref[...], hidden)
    row = lax.broadcasted_iota(jnp.int32, (8, lanes), 0)
    extra = jnp.where(row == 0, squares, modulation)
    for peer in range(first_ref.shape[0]):
        first_ref[peer, :lat_dim, :] = partial
        first_ref[peer, lat_dim:, :] = extra


def noise_kernel(
    level_ref,
    first_ref,
    noise_ref,
    order_ref,
    second_ref,
    kept_ref,
    pair,
    extra,
):
    f32 = jnp.float32
    level = level_ref[0]
    peers, used, lanes = first_ref.shape
    lat_dim = noise_ref.shape[0]
    mod_width = 40
    total = first_ref[0]
    for peer in range(1, peers):
        total = total + first_ref[peer]
    projected = total[:lat_dim]
    root_mean = jnp.sqrt(total[lat_dim : lat_dim + 1] / D + EPS_NORM)
    latent = projected / root_mean
    kept_ref[:lat_dim, :] = projected
    kept_ref[2 * lat_dim :, :] = jnp.broadcast_to(root_mean, (8, lanes))
    pair[...] = jnp.zeros_like(pair)
    for peer in range(peers):
        at = slice(peer * mod_width, (peer + 1) * mod_width)
        row = first_ref[peer, lat_dim : lat_dim + 8, :]
        pair[0:1, at] = row[1:2, :mod_width]
        pair[1:2, at] = row[1:2, mod_width : 2 * mod_width]
    rest = peers * mod_width - lanes
    head = pair[0:2, :lanes]
    head_high = head.astype(jnp.bfloat16).astype(f32)
    tail = jnp.concatenate([pair[0:1, lanes : lanes + rest], pair[1:2, lanes : lanes + rest]], axis=1)
    tail_high = tail.astype(jnp.bfloat16).astype(f32)
    extra[2:4, :] = head_high
    extra[4:6, :] = head - head_high
    extra[6:7, :] = jnp.concatenate([tail_high, tail - tail_high], axis=1)
    extra[7:8, :] = jnp.zeros((1, lanes), f32)
    extra[0:2, :] = order_ref[...]
    noisy = ((1.0 - level) * latent + level * noise_ref[...]).astype(jnp.bfloat16)
    kept_ref[lat_dim : 2 * lat_dim, :] = latent - noisy.astype(f32)
    rows = jnp.concatenate([noisy, extra[...].astype(jnp.bfloat16)], axis=0)
    for peer in range(second_ref.shape[0]):
        second_ref[peer] = rows


def heads_kernel(scores_ref, score_ref):
    total = jnp.sum(scores_ref[...].astype(jnp.float32), axis=0)
    for peer in range(score_ref.shape[0]):
        score_ref[peer] = total


def gradient_kernel(level_ref, score_ref, kept_ref, hidden_ref, third_ref, side_ref):
    f32 = jnp.float32
    level = level_ref[0]
    peers, half, lanes = score_ref.shape
    parts = peers // 4
    lat_dim = lanes // 2
    left = lax.broadcasted_iota(jnp.int32, (half, lanes), 1) < lat_dim
    pieces = []
    for part in range(parts):
        realistic = GUIDANCE * score_ref[parts + part] + (1.0 - GUIDANCE) * score_ref[2 * parts + part]
        difference = score_ref[3 * parts + part] - realistic
        pieces.append(jnp.where(left, difference, pltpu.roll(realistic, lat_dim, 1)))
        pieces.append(jnp.where(left, pltpu.roll(difference, lat_dim, 1), realistic))
    both = jnp.concatenate(pieces, axis=0).T
    difference = both[:lat_dim]
    realistic = both[lat_dim:]
    projected = kept_ref[:lat_dim, :]
    root_mean = kept_ref[2 * lat_dim : 2 * lat_dim + 1, :]
    distance = jnp.abs(kept_ref[lat_dim : 2 * lat_dim, :] + level * realistic)
    magnitude = jnp.sum(jnp.sum(distance, axis=0, keepdims=True), axis=1, keepdims=True)
    direction = difference / root_mean
    high, low = split(direction)
    hidden = hidden_ref[...]
    weight_part = dot32(high, hidden) + dot32(low, hidden)

    row = lax.broadcasted_iota(jnp.int32, (8, lat_dim), 0)
    first = magnitude.astype(jnp.bfloat16).astype(f32)
    second = (magnitude - first).astype(jnp.bfloat16).astype(f32)
    third = magnitude - first - second
    extra = jnp.where(row == 0, first, jnp.where(row == 1, second, jnp.where(row == 2, third, 0.0)))
    groups = third_ref.shape[0] // (lat_dim // 8)
    width = weight_part.shape[1] // groups
    for group in range(groups):
        columns = weight_part[:, group * width : (group + 1) * width]
        for block in range(lat_dim // 8):
            third_ref[block * groups + group] = jnp.concatenate(
                [columns[8 * block : 8 * (block + 1)], extra], axis=1
            ).astype(jnp.bfloat16)

    coefficient = jnp.sum(difference * projected, axis=0, keepdims=True) / (
        D * root_mean * root_mean * root_mean
    )
    side_ref[...] = jnp.concatenate(
        [direction, jnp.broadcast_to(coefficient, (lat_dim, lanes))], axis=0
    ).T


def scale_kernel(cells, rows, level_ref, third_ref, fourth_ref, factor_ref):
    total = jnp.sum(third_ref[...].astype(jnp.float32), axis=0)
    width = total.shape[1] - 64
    sums = total[:, width : width + 1]
    spread = (sums[0:1] + sums[1:2] + sums[2:3]) / cells + EPS_MEAN
    factor = -level_ref[0] / spread
    factor_ref[...] = jnp.broadcast_to(factor, factor_ref.shape)
    scaled = (total * (factor / math.sqrt(rows))).astype(jnp.bfloat16)
    for peer in range(fourth_ref.shape[0]):
        fourth_ref[peer] = scaled


def weight_kernel(fourth_ref, weight_ref):
    lat_dim, columns = weight_ref.shape
    groups = fourth_ref.shape[0] // (lat_dim // 8)
    width = columns // groups
    for block in range(lat_dim // 8):
        parts = [
            fourth_ref[block * groups + group].astype(jnp.float32)[:, :width]
            for group in range(groups)
        ]
        weight_ref[8 * block : 8 * (block + 1), :] = jnp.concatenate(parts, axis=1)


def hidden_kernel(factor_ref, side_ref, hidden_ref, out_ref, grad_ref):
    lat_dim = out_ref.shape[0]
    high, low = split(side_ref[:, :lat_dim])
    backward = dot32(high, out_ref[...]) + dot32(low, out_ref[...])
    coefficient = side_ref[:, lat_dim : lat_dim + 1]
    factor = factor_ref[0:1, 0:1]
    grad_ref[...] = (
        factor * (backward - hidden_ref[...].astype(jnp.float32) * coefficient)
    ).astype(jnp.bfloat16)


def body(
    gen_hidden,
    out_weight,
    noise,
    step_index,
    token_order,
    time_weight,
    embed_weight,
    qkv_weight,
    readout_weight,
):
    seq_count = lax.axis_size("seq")
    mp_count = lax.axis_size("mp")
    role_count = lax.axis_size("role")
    mp_index = lax.axis_index("mp")
    local_rows, columns = gen_hidden.shape
    lat_dim = out_weight.shape[1]
    bf16, f32 = jnp.bfloat16, jnp.float32
    timestep = step_index[0].astype(f32)
    level = (timestep / T_STEPS)[None]
    out_turned = out_weight.T

    time_turned = time_weight[0].transpose(1, 2, 0).reshape(-1, FREQ)
    turns = ROPE_BASE ** (-np.arange(FREQ // 2) / (FREQ // 2)) / (2.0 * np.pi)

    (first,) = call(
        start_kernel,
        [((mp_count, lat_dim + 8, local_rows), f32)],
        timestep[None],
        gen_hidden,
        out_turned,
        time_turned,
        jnp.asarray(np.repeat(in_parts(turns), 8, axis=0)),
        scalars=1,
        fetched=4,
    )
    first = exchange(first, "mp")

    second, kept = call(
        noise_kernel,
        [((seq_count, lat_dim + 8, local_rows), bf16), ((2 * lat_dim + 8, local_rows), f32)],
        level,
        first,
        noise.T.astype(f32),
        jnp.stack([token_order // 64, token_order % 64]).astype(f32),
        scalars=1,
        scratch=[pltpu.VMEM((8, 2 * local_rows), f32), pltpu.VMEM((8, local_rows), f32)],
    )
    second = exchange(second, "seq")
    scores = run_pass(
        mp_index.astype(jnp.int32)[None],
        second,
        embed_weight[0].astype(f32),
        qkv_weight[0, 0],
        jnp.concatenate(
            [readout_weight[0, 0].T.astype(f32), rotation_tables(qkv_weight.shape[3] // 3)]
        ),
    )

    scores = exchange(scores, "seq")
    quarter = local_rows // mp_count
    peers = role_count * mp_count
    (score,) = call(heads_kernel, [((peers, quarter // 2, 2 * lat_dim), f32)], scores)

    score = exchange(score, ("role", "mp"))

    width = columns // 4 + lat_dim
    third, side = call(
        gradient_kernel,
        [((seq_count, 8, width), bf16), ((local_rows, 2 * lat_dim), f32)],
        level,
        score,
        kept,
        gen_hidden,
        scalars=1,
    )

    third = exchange(third, "seq")
    cells = local_rows * seq_count * lat_dim
    fourth, factor = call(
        functools.partial(scale_kernel, cells, local_rows * seq_count),
        [((seq_count, 8, width), bf16), ((8, 128), f32)],
        level,
        third,
        scalars=1,
    )
    fourth = exchange(fourth, "seq")
    (hidden_grad,) = call(
        hidden_kernel, [((local_rows, columns), bf16)], factor, side, gen_hidden, out_turned
    )
    (weight_grad,) = call(weight_kernel, [((lat_dim, columns), f32)], fourth)
    return (hidden_grad, weight_grad.T)


def solution(mesh):
    placed = (
        P("seq", "mp"),
        P("mp", None),
        P("seq", None),
        P(),
        P("seq"),
        P("role", None, None, ("seq", "mp")),
        P("role", None, None),
        P("role", "seq", None, None),
        P("role", "seq", None, None),
    )
    return jax.shard_map(
        body, mesh=mesh, in_specs=placed, out_specs=(P("seq", "mp"), P("mp", None)), check_vma=False
    )
```

```python
import functools
import math

import jax
import jax.numpy as jnp
import numpy as np
from jax import lax
from jax.experimental import pallas as pl
from jax.experimental.pallas import tpu as pltpu
from jax.sharding import PartitionSpec as P

D = 5120
FREQ = 256
T_STEPS = 1000


EPS_NORM = 1e-06
EPS_MEAN = 1e-05
GUIDANCE = 5.0
ROPE_BASE = 10000.0
SHARPNESS = 4.0
VMEM_LIMIT = 61 * 1024 * 1024
CHUNK = 1024


def split(values):
    high = values.astype(jnp.bfloat16)
    return high, (values - high.astype(jnp.float32)).astype(jnp.bfloat16)


def exchange(chunks, axes):
    return lax.all_to_all(chunks, axes, 0, 0, tiled=True)


def dot32(left, right):
    return jnp.dot(left, right, preferred_element_type=jnp.float32)


def dot_rows(left, right):
    return lax.dot_general(
        left, right, (((1,), (1,)), ((), ())), preferred_element_type=jnp.float32
    )


def fetch_all(arrived, *pairs):
    fetches = [
        pltpu.make_async_copy(source, target, arrived.at[index])
        for index, (source, target) in enumerate(pairs)
    ]
    for fetch in fetches:
        fetch.start()
    return fetches


def in_parts(turns):
    grain = 2.0 ** (np.floor(np.log2(turns)) - 11)
    high = np.floor(turns / grain) * grain
    return np.stack([high, turns - high]).astype(np.float32)


def rotation_tables(head_dim):
    turns = ROPE_BASE ** (-2.0 * np.arange(head_dim // 2) / head_dim) / (2.0 * np.pi)
    both = in_parts(turns).reshape(head_dim)
    return np.ascontiguousarray(np.broadcast_to(both[:, None], (head_dim, 128)))


def rotations(positions, table):
    table = jnp.concatenate([table] * (positions.shape[1] // table.shape[1]), axis=1)
    high = table[: table.shape[0] // 2]
    low = table[table.shape[0] // 2 :]
    whole = positions * high
    part = (whole - jnp.round(whole)) + positions * low
    angle = (part - jnp.round(part)) * math.pi
    square = angle * angle
    sine = square * (-1.0 / 39916800) + 1.0 / 362880
    sine = sine * square - 1.0 / 5040
    sine = sine * square + 1.0 / 120
    sine = sine * square - 1.0 / 6
    sine = (sine * square + 1.0) * angle
    cosine = square * (1.0 / 479001600) - 1.0 / 3628800
    cosine = cosine * square + 1.0 / 40320
    cosine = cosine * square - 1.0 / 720
    cosine = cosine * square + 1.0 / 24
    cosine = cosine * square - 0.5
    cosine = cosine * square + 1.0
    return 1.0 - 2.0 * sine * sine, 2.0 * sine * cosine


def normalize_rope(vectors, cosines, sines):
    rescaled = vectors * lax.rsqrt(jnp.mean(vectors * vectors, axis=0, keepdims=True) + EPS_NORM)
    width = vectors.shape[0] // 2
    front = rescaled[:width]
    back = rescaled[width:]
    return jnp.concatenate([front * cosines - back * sines, front * sines + back * cosines], axis=0)


def pass_kernel(
    place_ref,
    gathered_ref,
    embed_ref,
    weight_ref,
    small_ref,
    score_ref,
    modulation,
    scaled,
    clip,
    places,
    own,
    own_places,
    query,
    key,
    wide,
    attended,
):
    f32 = jnp.float32
    blocks, used, lanes = gathered_ref.shape
    lat_dim, width = embed_ref.shape
    head_dim = weight_ref.shape[1] // 3
    key_rows = blocks * lanes
    query_rows = query.shape[0]
    quarter = query_rows // blocks
    per_tile = lanes // quarter
    piece = width // blocks
    place = place_ref[0]

    for block in range(blocks):
        at = slice(block * lanes, (block + 1) * lanes)
        received = gathered_ref[block]
        clip[:lat_dim, at] = received[:lat_dim]
        clip[lat_dim:, at] = received[:lat_dim]
        extra = received[lat_dim:].astype(f32)
        places[0:1, at] = extra[0:1] * 64.0 + extra[1:2]
        pair = extra[2:4] + extra[4:6]
        tail = extra[6:7] + pltpu.roll(extra[6:7], lanes // 2, 1)
        begin = block * piece
        rest = piece - lanes
        modulation[0:2, begin : begin + lanes] = pair
        modulation[0:1, begin + lanes : begin + piece] = tail[:, :rest]
        modulation[1:2, begin + lanes : begin + piece] = tail[:, rest : 2 * rest]

    lane = lax.broadcasted_iota(jnp.int32, (used, lanes), 1)
    for tile in range(blocks // per_tile):
        found = jnp.zeros((used, lanes), f32)
        for part in range(per_tile):
            block = gathered_ref[tile * per_tile + part].astype(f32)
            shift = lax.rem((part - place + per_tile) * quarter, lanes)
            found = jnp.where(lane // quarter == part, pltpu.roll(block, shift, 1), found)
        at = slice(tile * lanes, (tile + 1) * lanes)
        rows = found[:lat_dim].astype(jnp.bfloat16)
        own[:lat_dim, at] = rows
        own[lat_dim:, at] = rows
        own_places[0:1, at] = found[lat_dim : lat_dim + 1] * 64.0 + found[lat_dim + 1 : lat_dim + 2]

    folded = jnp.zeros((2 * lat_dim + 16, 3 * head_dim), f32)
    for begin in range(0, width, CHUNK):
        at = slice(begin, begin + CHUNK)
        high, low = split(embed_ref[:, at] * (1.0 + modulation[1:2, at]))
        scaled[:lat_dim, at] = high
        scaled[lat_dim : 2 * lat_dim, at] = low
        row = lax.broadcasted_iota(jnp.int32, (16, CHUNK), 0)
        shifted = jnp.broadcast_to(modulation[0:1, at], (16, CHUNK))
        shifted_high = shifted.astype(jnp.bfloat16).astype(f32)
        shifted = jnp.where(row == 0, shifted_high, shifted - shifted_high)
        scaled[2 * lat_dim :, at] = jnp.where(row < 2, shifted, 0.0).astype(jnp.bfloat16)
        folded = folded + dot32(scaled[:, at], weight_ref[at, :])
    embed = embed_ref[...].astype(jnp.bfloat16)
    gram = dot_rows(embed, embed)
    matrix = folded[:lat_dim] + folded[lat_dim : 2 * lat_dim]
    offset = folded[2 * lat_dim : 2 * lat_dim + 1] + folded[2 * lat_dim + 1 : 2 * lat_dim + 2]
    turned = jnp.concatenate(
        [matrix, jnp.broadcast_to(offset, (lanes - lat_dim, 3 * head_dim))], axis=0
    ).T
    offsets = jnp.broadcast_to(turned[:, lat_dim : lat_dim + 1], (3 * head_dim, lanes))
    matrix_parts = jnp.concatenate(split(turned[:, :lat_dim]), axis=1)
    gram_parts = jnp.concatenate(split(gram), axis=1)

    def project(parts, offsets, rows):
        product = dot32(jnp.concatenate([parts, gram_parts], axis=0), rows)
        count = parts.shape[0]
        mean = jnp.sum(rows[:lat_dim].astype(f32) * product[count:], axis=0, keepdims=True) / width
        offsets = jnp.concatenate([offsets] * (rows.shape[1] // lanes), axis=1)
        return product[:count] * lax.rsqrt(mean + EPS_NORM) + offsets

    step = 4 * lanes
    table = small_ref[lat_dim:, :]
    wide[:, head_dim:] = jnp.ones((key_rows, head_dim), jnp.bfloat16)
    for begin in range(0, query_rows, step):
        at = slice(begin, begin + step)
        vectors = project(matrix_parts[:head_dim], offsets[:head_dim], own[:, at])
        turns = rotations(own_places[0:1, at], table)
        query[at, :] = normalize_rope(vectors, *turns).T.astype(jnp.bfloat16)

    def keys_and_values(index, carry):
        at = pl.ds(pl.multiple_of(index * step, step), step)
        vectors = project(matrix_parts[head_dim:], offsets[head_dim:], clip[:, at])
        turns = rotations(places[0:1, at], table)
        key[:, at] = normalize_rope(vectors[:head_dim], *turns).astype(jnp.bfloat16)
        wide[at, :head_dim] = vectors[head_dim:].T.astype(jnp.bfloat16)
        return carry

    lax.fori_loop(0, key_rows // step, keys_and_values, 0, unroll=True)

    rows, step = 1024, 256
    factor = SHARPNESS / math.sqrt(head_dim) * math.log2(math.e)

    def attend(index, carry):
        at = pl.ds(pl.multiple_of(index * rows, rows), rows)
        queries = query[at, :]
        total = jnp.zeros((rows, 2 * head_dim), f32)
        for begin in range(0, key_rows, step):
            scores = dot32(queries, key[:, begin : begin + step])
            exponents = jnp.exp2(scores * factor).astype(jnp.bfloat16)
            total = total + dot32(exponents, wide[begin : begin + step, :])
        result = (total[:, :head_dim] / total[:, head_dim:]).astype(jnp.bfloat16)
        attended[pl.ds(index * (rows // quarter), rows // quarter)] = result.reshape(
            rows // quarter, quarter, head_dim
        )
        return carry

    lax.fori_loop(0, query_rows // rows, attend, 0, unroll=True)
    half = quarter // 2
    readout = small_ref[:lat_dim, :].astype(jnp.bfloat16)
    halves = [
        dot_rows(attended[:, begin : begin + half, :].reshape(blocks * half, head_dim), readout)
        for begin in (0, half)
    ]
    score_ref[...] = (
        jnp.concatenate(halves, axis=1).astype(jnp.bfloat16).reshape(blocks, half, 2 * lat_dim)
    )


def run_pass(place, gathered, embed, weights, small):
    blocks, unused, lanes = gathered.shape
    lat_dim, width = embed.shape
    head_dim = weights.shape[1] // 3
    key_rows = blocks * lanes
    query_rows = key_rows // 4
    bf16, f32 = jnp.bfloat16, jnp.float32
    vmem = pl.BlockSpec(memory_space=pltpu.VMEM)
    return pl.pallas_call(
        pass_kernel,
        out_shape=jax.ShapeDtypeStruct((blocks, lanes // 8, lanes), bf16),
        in_specs=[pl.BlockSpec(memory_space=pltpu.SMEM)] + [vmem] * 4,
        out_specs=vmem,
        scratch_shapes=[
            pltpu.VMEM((8, width), f32),
            pltpu.VMEM((2 * lat_dim + 16, width), bf16),
            pltpu.VMEM((2 * lat_dim, key_rows), bf16),
            pltpu.VMEM((8, key_rows), f32),
            pltpu.VMEM((2 * lat_dim, query_rows), bf16),
            pltpu.VMEM((8, query_rows), f32),
            pltpu.VMEM((query_rows, head_dim), bf16),
            pltpu.VMEM((head_dim, key_rows), bf16),
            pltpu.VMEM((key_rows, 2 * head_dim), bf16),
            pltpu.VMEM((blocks, lanes // 4, head_dim), bf16),
        ],
        compiler_params=pltpu.CompilerParams(vmem_limit_bytes=40 * 1024 * 1024),
    )(place, gathered, embed, weights, small)


def call(kernel, outputs, *operands, scalars=0, fetched=0, scratch=()):
    vmem = pl.BlockSpec(memory_space=pltpu.VMEM)
    smem = pl.BlockSpec(memory_space=pltpu.SMEM)
    plain = len(operands) - scalars - fetched
    scratch = list(scratch)
    if fetched:
        scratch += [pltpu.VMEM(a.shape, a.dtype) for a in operands[-fetched:]]
        scratch.append(pltpu.SemaphoreType.DMA((fetched,)))
    return pl.pallas_call(
        kernel,
        out_shape=[jax.ShapeDtypeStruct(*output) for output in outputs],
        in_specs=[smem] * scalars + [vmem] * plain + [pl.BlockSpec(memory_space=pl.ANY)] * fetched,
        out_specs=[vmem] * len(outputs),
        scratch_shapes=scratch,
        compiler_params=pltpu.CompilerParams(
            vmem_limit_bytes=VMEM_LIMIT if fetched else 16 * 1024 * 1024
        ),
    )(*operands)


def start_kernel(
    time_ref,
    hidden_in,
    out_in,
    weight_in,
    table_in,
    first_ref,
    hidden_ref,
    out_ref,
    weight_ref,
    table_ref,
    arrived,
):
    fetches = fetch_all(
        arrived,
        (table_in, table_ref),
        (weight_in, weight_ref),
        (hidden_in, hidden_ref),
        (out_in, out_ref),
    )
    lanes = hidden_ref.shape[0]
    lat_dim = out_ref.shape[0]
    for fetch in fetches:
        fetch.wait()
    waves = rotations(jnp.broadcast_to(time_ref[0], (1, lanes)), table_ref[...])
    active = jnp.concatenate([wave / (1.0 + jnp.exp(-wave)) for wave in waves], axis=1)
    modulation = lax.dot_general(
        active,
        weight_ref[...],
        (((1,), (1,)), ((), ())),
        precision=lax.Precision.HIGHEST,
        preferred_element_type=jnp.float32,
    )
    modulation = jnp.concatenate(
        [modulation, jnp.zeros((8, lanes - modulation.shape[1]), jnp.float32)], axis=1
    )
    hidden = hidden_ref[...]
    wide = hidden.astype(jnp.float32)
    ones = jnp.ones((8, hidden.shape[1]), jnp.bfloat16)
    high, low = split(wide * wide)
    squares = dot_rows(ones, high) + dot_rows(ones, low)
    partial = dot_rows(out_ref[...], hidden)
    row = lax.broadcasted_iota(jnp.int32, (8, lanes), 0)
    values = jnp.where(row < 2, squares, jnp.where(row < 4, modulation, 0.0))
    high = values.astype(jnp.bfloat16).astype(jnp.float32)
    extra = jnp.where(row % 2 == 0, high, values - high)
    rows = jnp.concatenate([partial, extra], axis=0).astype(jnp.bfloat16)
    for peer in range(first_ref.shape[0]):
        first_ref[peer] = rows


def noise_kernel(
    level_ref,
    first_ref,
    noise_ref,
    order_ref,
    second_ref,
    kept_ref,
    pair,
    extra,
):
    f32 = jnp.float32
    level = level_ref[0]
    peers, used, lanes = first_ref.shape
    lat_dim = noise_ref.shape[0]
    mod_width = 40
    parts = [first_ref[peer].astype(f32) for peer in range(peers)]
    total = sum(parts[1:], parts[0])
    projected = total[:lat_dim]
    root_mean = jnp.sqrt(
        (total[lat_dim : lat_dim + 1] + total[lat_dim + 1 : lat_dim + 2]) / D + EPS_NORM
    )
    latent = projected / root_mean
    kept_ref[:lat_dim, :] = projected
    kept_ref[2 * lat_dim :, :] = jnp.broadcast_to(root_mean, (8, lanes))
    pair[...] = jnp.zeros_like(pair)
    for peer in range(peers):
        at = slice(peer * mod_width, (peer + 1) * mod_width)
        row = parts[peer][lat_dim + 2 : lat_dim + 3] + parts[peer][lat_dim + 3 : lat_dim + 4]
        pair[0:1, at] = row[:, :mod_width]
        pair[1:2, at] = row[:, mod_width : 2 * mod_width]
    rest = peers * mod_width - lanes
    head = pair[0:2, :lanes]
    head_high = head.astype(jnp.bfloat16).astype(f32)
    tail = jnp.concatenate([pair[0:1, lanes : lanes + rest], pair[1:2, lanes : lanes + rest]], axis=1)
    tail_high = tail.astype(jnp.bfloat16).astype(f32)
    extra[2:4, :] = head_high
    extra[4:6, :] = head - head_high
    extra[6:7, :] = jnp.concatenate([tail_high, tail - tail_high], axis=1)
    extra[7:8, :] = jnp.zeros((1, lanes), f32)
    extra[0:2, :] = order_ref[...]
    noisy = ((1.0 - level) * latent + level * noise_ref[...]).astype(jnp.bfloat16)
    kept_ref[lat_dim : 2 * lat_dim, :] = latent - noisy.astype(f32)
    rows = jnp.concatenate([noisy, extra[...].astype(jnp.bfloat16)], axis=0)
    for peer in range(second_ref.shape[0]):
        second_ref[peer] = rows


def heads_kernel(scores_ref, score_ref):
    total = jnp.sum(scores_ref[...].astype(jnp.float32), axis=0)
    for peer in range(score_ref.shape[0]):
        score_ref[peer] = total


def gradient_kernel(level_ref, score_ref, kept_ref, hidden_ref, third_ref, side_ref):
    f32 = jnp.float32
    level = level_ref[0]
    peers, half, lanes = score_ref.shape
    parts = peers // 4
    lat_dim = lanes // 2
    left = lax.broadcasted_iota(jnp.int32, (half, lanes), 1) < lat_dim
    pieces = []
    for part in range(parts):
        realistic = GUIDANCE * score_ref[parts + part] + (1.0 - GUIDANCE) * score_ref[2 * parts + part]
        difference = score_ref[3 * parts + part] - realistic
        pieces.append(jnp.where(left, difference, pltpu.roll(realistic, lat_dim, 1)))
        pieces.append(jnp.where(left, pltpu.roll(difference, lat_dim, 1), realistic))
    both = jnp.concatenate(pieces, axis=0).T
    difference = both[:lat_dim]
    realistic = both[lat_dim:]
    projected = kept_ref[:lat_dim, :]
    root_mean = kept_ref[2 * lat_dim : 2 * lat_dim + 1, :]
    distance = jnp.abs(kept_ref[lat_dim : 2 * lat_dim, :] + level * realistic)
    magnitude = jnp.sum(jnp.sum(distance, axis=0, keepdims=True), axis=1, keepdims=True)
    direction = difference / root_mean
    high, low = split(direction)
    hidden = hidden_ref[...]
    weight_part = dot32(high, hidden) + dot32(low, hidden)

    row = lax.broadcasted_iota(jnp.int32, (8, lat_dim), 0)
    first = magnitude.astype(jnp.bfloat16).astype(f32)
    second = (magnitude - first).astype(jnp.bfloat16).astype(f32)
    third = magnitude - first - second
    extra = jnp.where(row == 0, first, jnp.where(row == 1, second, jnp.where(row == 2, third, 0.0)))
    groups = third_ref.shape[0] // (lat_dim // 8)
    width = weight_part.shape[1] // groups
    for group in range(groups):
        columns = weight_part[:, group * width : (group + 1) * width]
        for block in range(lat_dim // 8):
            third_ref[block * groups + group] = jnp.concatenate(
                [columns[8 * block : 8 * (block + 1)], extra], axis=1
            ).astype(jnp.bfloat16)

    coefficient = jnp.sum(difference * projected, axis=0, keepdims=True) / (
        D * root_mean * root_mean * root_mean
    )
    side_ref[...] = jnp.concatenate(
        [direction, jnp.broadcast_to(coefficient, (lat_dim, lanes))], axis=0
    ).T


def scale_kernel(cells, rows, level_ref, third_ref, fourth_ref, factor_ref):
    total = jnp.sum(third_ref[...].astype(jnp.float32), axis=0)
    width = total.shape[1] - 64
    sums = total[:, width : width + 1]
    spread = (sums[0:1] + sums[1:2] + sums[2:3]) / cells + EPS_MEAN
    factor = -level_ref[0] / spread
    factor_ref[...] = jnp.broadcast_to(factor, factor_ref.shape)
    scaled = (total * (factor / math.sqrt(rows))).astype(jnp.bfloat16)
    for peer in range(fourth_ref.shape[0]):
        fourth_ref[peer] = scaled


def weight_kernel(fourth_ref, weight_ref):
    lat_dim, columns = weight_ref.shape
    groups = fourth_ref.shape[0] // (lat_dim // 8)
    width = columns // groups
    for block in range(lat_dim // 8):
        parts = [
            fourth_ref[block * groups + group].astype(jnp.float32)[:, :width]
            for group in range(groups)
        ]
        weight_ref[8 * block : 8 * (block + 1), :] = jnp.concatenate(parts, axis=1)


def hidden_kernel(factor_ref, side_ref, hidden_ref, out_ref, grad_ref):
    lat_dim = out_ref.shape[0]
    high, low = split(side_ref[:, :lat_dim])
    backward = dot32(high, out_ref[...]) + dot32(low, out_ref[...])
    coefficient = side_ref[:, lat_dim : lat_dim + 1]
    factor = factor_ref[0:1, 0:1]
    grad_ref[...] = (
        factor * (backward - hidden_ref[...].astype(jnp.float32) * coefficient)
    ).astype(jnp.bfloat16)


def body(
    gen_hidden,
    out_weight,
    noise,
    step_index,
    token_order,
    time_weight,
    embed_weight,
    qkv_weight,
    readout_weight,
):
    seq_count = lax.axis_size("seq")
    mp_count = lax.axis_size("mp")
    role_count = lax.axis_size("role")
    mp_index = lax.axis_index("mp")
    local_rows, columns = gen_hidden.shape
    lat_dim = out_weight.shape[1]
    bf16, f32 = jnp.bfloat16, jnp.float32
    timestep = step_index[0].astype(f32)
    level = (timestep / T_STEPS)[None]
    out_turned = out_weight.T

    time_turned = time_weight[0].transpose(1, 2, 0).reshape(-1, FREQ)
    turns = ROPE_BASE ** (-np.arange(FREQ // 2) / (FREQ // 2)) / (2.0 * np.pi)

    (first,) = call(
        start_kernel,
        [((mp_count, lat_dim + 8, local_rows), bf16)],
        timestep[None],
        gen_hidden,
        out_turned,
        time_turned,
        jnp.asarray(np.repeat(in_parts(turns), 8, axis=0)),
        scalars=1,
        fetched=4,
    )
    first = exchange(first, "mp")

    second, kept = call(
        noise_kernel,
        [((seq_count, lat_dim + 8, local_rows), bf16), ((2 * lat_dim + 8, local_rows), f32)],
        level,
        first,
        noise.T.astype(f32),
        jnp.stack([token_order // 64, token_order % 64]).astype(f32),
        scalars=1,
        scratch=[pltpu.VMEM((8, 2 * local_rows), f32), pltpu.VMEM((8, local_rows), f32)],
    )
    second = exchange(second, "seq")
    scores = run_pass(
        mp_index.astype(jnp.int32)[None],
        second,
        embed_weight[0].astype(f32),
        qkv_weight[0, 0],
        jnp.concatenate(
            [readout_weight[0, 0].T.astype(f32), rotation_tables(qkv_weight.shape[3] // 3)]
        ),
    )

    scores = exchange(scores, "seq")
    quarter = local_rows // mp_count
    peers = role_count * mp_count
    (score,) = call(heads_kernel, [((peers, quarter // 2, 2 * lat_dim), f32)], scores)

    score = exchange(score, ("role", "mp"))

    width = columns // 4 + lat_dim
    third, side = call(
        gradient_kernel,
        [((seq_count, 8, width), bf16), ((local_rows, 2 * lat_dim), f32)],
        level,
        score,
        kept,
        gen_hidden,
        scalars=1,
    )

    third = exchange(third, "seq")
    cells = local_rows * seq_count * lat_dim
    fourth, factor = call(
        functools.partial(scale_kernel, cells, local_rows * seq_count),
        [((seq_count, 8, width), bf16), ((8, 128), f32)],
        level,
        third,
        scalars=1,
    )
    fourth = exchange(fourth, "seq")
    (hidden_grad,) = call(
        hidden_kernel, [((local_rows, columns), bf16)], factor, side, gen_hidden, out_turned
    )
    (weight_grad,) = call(weight_kernel, [((lat_dim, columns), f32)], fourth)
    return (hidden_grad, weight_grad.T)


def solution(mesh):
    placed = (
        P("seq", "mp"),
        P("mp", None),
        P("seq", None),
        P(),
        P("seq"),
        P("role", None, None, ("seq", "mp")),
        P("role", None, None),
        P("role", "seq", None, None),
        P("role", "seq", None, None),
    )
    return jax.shard_map(
        body, mesh=mesh, in_specs=placed, out_specs=(P("seq", "mp"), P("mp", None)), check_vma=False
    )
```

```python
import functools
import math

import jax
import jax.numpy as jnp
import numpy as np
from jax import lax
from jax.experimental import pallas as pl
from jax.experimental.pallas import tpu as pltpu
from jax.sharding import PartitionSpec as P

D = 5120
FREQ = 256
T_STEPS = 1000


EPS_NORM = 1e-06
EPS_MEAN = 1e-05
GUIDANCE = 5.0
ROPE_BASE = 10000.0
SHARPNESS = 4.0
VMEM_LIMIT = 61 * 1024 * 1024
CHUNK = 1024


def split(values):
    high = values.astype(jnp.bfloat16)
    return high, (values - high.astype(jnp.float32)).astype(jnp.bfloat16)


def exchange(chunks, axes):
    return lax.all_to_all(chunks, axes, 0, 0, tiled=True)


def dot32(left, right):
    return jnp.dot(left, right, preferred_element_type=jnp.float32)


def dot_rows(left, right):
    return lax.dot_general(
        left, right, (((1,), (1,)), ((), ())), preferred_element_type=jnp.float32
    )


def fetch_all(arrived, *pairs):
    fetches = [
        pltpu.make_async_copy(source, target, arrived.at[index])
        for index, (source, target) in enumerate(pairs)
    ]
    for fetch in fetches:
        fetch.start()
    return fetches


def in_parts(turns):
    grain = 2.0 ** (np.floor(np.log2(turns)) - 11)
    high = np.floor(turns / grain) * grain
    return np.stack([high, turns - high]).astype(np.float32)


def rotation_tables(head_dim):
    turns = ROPE_BASE ** (-2.0 * np.arange(head_dim // 2) / head_dim) / (2.0 * np.pi)
    both = in_parts(turns).reshape(head_dim)
    return np.ascontiguousarray(np.broadcast_to(both[:, None], (head_dim, 128)))


def rotations(positions, table):
    table = jnp.concatenate([table] * (positions.shape[1] // table.shape[1]), axis=1)
    high = table[: table.shape[0] // 2]
    low = table[table.shape[0] // 2 :]
    whole = positions * high
    part = (whole - jnp.round(whole)) + positions * low
    angle = (part - jnp.round(part)) * math.pi
    square = angle * angle
    sine = square * (-1.0 / 39916800) + 1.0 / 362880
    sine = sine * square - 1.0 / 5040
    sine = sine * square + 1.0 / 120
    sine = sine * square - 1.0 / 6
    sine = (sine * square + 1.0) * angle
    cosine = square * (1.0 / 479001600) - 1.0 / 3628800
    cosine = cosine * square + 1.0 / 40320
    cosine = cosine * square - 1.0 / 720
    cosine = cosine * square + 1.0 / 24
    cosine = cosine * square - 0.5
    cosine = cosine * square + 1.0
    return 1.0 - 2.0 * sine * sine, 2.0 * sine * cosine


def normalize_rope(vectors, cosines, sines):
    rescaled = vectors * lax.rsqrt(jnp.mean(vectors * vectors, axis=0, keepdims=True) + EPS_NORM)
    width = vectors.shape[0] // 2
    front = rescaled[:width]
    back = rescaled[width:]
    return jnp.concatenate([front * cosines - back * sines, front * sines + back * cosines], axis=0)


def pass_kernel(
    place_ref,
    gathered_ref,
    embed_ref,
    weight_ref,
    small_ref,
    score_ref,
    modulation,
    scaled,
    clip,
    places,
    own,
    own_places,
    query,
    key,
    wide,
    attended,
):
    f32 = jnp.float32
    blocks, used, lanes = gathered_ref.shape
    lat_dim, width = embed_ref.shape
    head_dim = weight_ref.shape[1] // 3
    key_rows = blocks * lanes
    query_rows = query.shape[0]
    quarter = query_rows // blocks
    per_tile = lanes // quarter
    piece = width // blocks
    place = place_ref[0]

    for block in range(blocks):
        at = slice(block * lanes, (block + 1) * lanes)
        received = gathered_ref[block]
        clip[:lat_dim, at] = received[:lat_dim]
        clip[lat_dim:, at] = received[:lat_dim]
        extra = received[lat_dim:].astype(f32)
        places[0:1, at] = extra[0:1] * 64.0 + extra[1:2]
        pair = extra[2:4] + extra[4:6]
        tail = extra[6:7] + pltpu.roll(extra[6:7], lanes // 2, 1)
        begin = block * piece
        rest = piece - lanes
        modulation[0:2, begin : begin + lanes] = pair
        modulation[0:1, begin + lanes : begin + piece] = tail[:, :rest]
        modulation[1:2, begin + lanes : begin + piece] = tail[:, rest : 2 * rest]

    lane = lax.broadcasted_iota(jnp.int32, (used, lanes), 1)
    for tile in range(blocks // per_tile):
        found = jnp.zeros((used, lanes), f32)
        for part in range(per_tile):
            block = gathered_ref[tile * per_tile + part].astype(f32)
            shift = lax.rem((part - place + per_tile) * quarter, lanes)
            found = jnp.where(lane // quarter == part, pltpu.roll(block, shift, 1), found)
        at = slice(tile * lanes, (tile + 1) * lanes)
        rows = found[:lat_dim].astype(jnp.bfloat16)
        own[:lat_dim, at] = rows
        own[lat_dim:, at] = rows
        own_places[0:1, at] = found[lat_dim : lat_dim + 1] * 64.0 + found[lat_dim + 1 : lat_dim + 2]

    folded = jnp.zeros((2 * lat_dim + 16, 3 * head_dim), f32)
    for begin in range(0, width, CHUNK):
        at = slice(begin, begin + CHUNK)
        high, low = split(embed_ref[:, at] * (1.0 + modulation[1:2, at]))
        scaled[:lat_dim, at] = high
        scaled[lat_dim : 2 * lat_dim, at] = low
        row = lax.broadcasted_iota(jnp.int32, (16, CHUNK), 0)
        shifted = jnp.broadcast_to(modulation[0:1, at], (16, CHUNK))
        shifted_high = shifted.astype(jnp.bfloat16).astype(f32)
        shifted = jnp.where(row == 0, shifted_high, shifted - shifted_high)
        scaled[2 * lat_dim :, at] = jnp.where(row < 2, shifted, 0.0).astype(jnp.bfloat16)
        folded = folded + dot32(scaled[:, at], weight_ref[at, :])
    embed = embed_ref[...].astype(jnp.bfloat16)
    gram = dot_rows(embed, embed)
    matrix = folded[:lat_dim] + folded[lat_dim : 2 * lat_dim]
    offset = folded[2 * lat_dim : 2 * lat_dim + 1] + folded[2 * lat_dim + 1 : 2 * lat_dim + 2]
    turned = jnp.concatenate(
        [matrix, jnp.broadcast_to(offset, (lanes - lat_dim, 3 * head_dim))], axis=0
    ).T
    offsets = jnp.broadcast_to(turned[:, lat_dim : lat_dim + 1], (3 * head_dim, lanes))
    matrix_parts = jnp.concatenate(split(turned[:, :lat_dim]), axis=1)
    gram_parts = jnp.concatenate(split(gram), axis=1)

    def project(parts, offsets, rows):
        product = dot32(jnp.concatenate([parts, gram_parts], axis=0), rows)
        count = parts.shape[0]
        mean = jnp.sum(rows[:lat_dim].astype(f32) * product[count:], axis=0, keepdims=True) / width
        offsets = jnp.concatenate([offsets] * (rows.shape[1] // lanes), axis=1)
        return product[:count] * lax.rsqrt(mean + EPS_NORM) + offsets

    step = 4 * lanes
    table = small_ref[lat_dim:, :]
    wide[:, head_dim:] = jnp.ones((key_rows, head_dim), jnp.bfloat16)
    for begin in range(0, query_rows, step):
        at = slice(begin, begin + step)
        vectors = project(matrix_parts[:head_dim], offsets[:head_dim], own[:, at])
        turns = rotations(own_places[0:1, at], table)
        query[at, :] = normalize_rope(vectors, *turns).T.astype(jnp.bfloat16)

    def keys_and_values(index, carry):
        at = pl.ds(pl.multiple_of(index * step, step), step)
        vectors = project(matrix_parts[head_dim:], offsets[head_dim:], clip[:, at])
        turns = rotations(places[0:1, at], table)
        key[:, at] = normalize_rope(vectors[:head_dim], *turns).astype(jnp.bfloat16)
        wide[at, :head_dim] = vectors[head_dim:].T.astype(jnp.bfloat16)
        return carry

    lax.fori_loop(0, key_rows // step, keys_and_values, 0, unroll=True)

    rows, step = 1024, 256
    factor = SHARPNESS / math.sqrt(head_dim) * math.log2(math.e)

    def attend(index, carry):
        at = pl.ds(pl.multiple_of(index * rows, rows), rows)
        queries = query[at, :]
        total = jnp.zeros((rows, 2 * head_dim), f32)
        for begin in range(0, key_rows, step):
            scores = dot32(queries, key[:, begin : begin + step])
            exponents = jnp.exp2(scores * factor).astype(jnp.bfloat16)
            total = total + dot32(exponents, wide[begin : begin + step, :])
        result = (total[:, :head_dim] / total[:, head_dim:]).astype(jnp.bfloat16)
        attended[pl.ds(index * (rows // quarter), rows // quarter)] = result.reshape(
            rows // quarter, quarter, head_dim
        )
        return carry

    lax.fori_loop(0, query_rows // rows, attend, 0, unroll=True)
    half = quarter // 2
    readout = small_ref[:lat_dim, :].astype(jnp.bfloat16)
    halves = [
        dot_rows(attended[:, begin : begin + half, :].reshape(blocks * half, head_dim), readout)
        for begin in (0, half)
    ]
    score_ref[...] = (
        jnp.concatenate(halves, axis=1).astype(jnp.bfloat16).reshape(blocks, half, 2 * lat_dim)
    )


def run_pass(place, gathered, embed, weights, small):
    blocks, unused, lanes = gathered.shape
    lat_dim, width = embed.shape
    head_dim = weights.shape[1] // 3
    key_rows = blocks * lanes
    query_rows = key_rows // 4
    bf16, f32 = jnp.bfloat16, jnp.float32
    vmem = pl.BlockSpec(memory_space=pltpu.VMEM)
    return pl.pallas_call(
        pass_kernel,
        out_shape=jax.ShapeDtypeStruct((blocks, lanes // 8, lanes), bf16),
        in_specs=[pl.BlockSpec(memory_space=pltpu.SMEM)] + [vmem] * 4,
        out_specs=vmem,
        scratch_shapes=[
            pltpu.VMEM((8, width), f32),
            pltpu.VMEM((2 * lat_dim + 16, width), bf16),
            pltpu.VMEM((2 * lat_dim, key_rows), bf16),
            pltpu.VMEM((8, key_rows), f32),
            pltpu.VMEM((2 * lat_dim, query_rows), bf16),
            pltpu.VMEM((8, query_rows), f32),
            pltpu.VMEM((query_rows, head_dim), bf16),
            pltpu.VMEM((head_dim, key_rows), bf16),
            pltpu.VMEM((key_rows, 2 * head_dim), bf16),
            pltpu.VMEM((blocks, lanes // 4, head_dim), bf16),
        ],
        compiler_params=pltpu.CompilerParams(vmem_limit_bytes=40 * 1024 * 1024),
    )(place, gathered, embed, weights, small)


def call(kernel, outputs, *operands, scalars=0, fetched=0, scratch=()):
    vmem = pl.BlockSpec(memory_space=pltpu.VMEM)
    smem = pl.BlockSpec(memory_space=pltpu.SMEM)
    plain = len(operands) - scalars - fetched
    scratch = list(scratch)
    if fetched:
        scratch += [pltpu.VMEM(a.shape, a.dtype) for a in operands[-fetched:]]
        scratch.append(pltpu.SemaphoreType.DMA((fetched,)))
    return pl.pallas_call(
        kernel,
        out_shape=[jax.ShapeDtypeStruct(*output) for output in outputs],
        in_specs=[smem] * scalars + [vmem] * plain + [pl.BlockSpec(memory_space=pl.ANY)] * fetched,
        out_specs=[vmem] * len(outputs),
        scratch_shapes=scratch,
        compiler_params=pltpu.CompilerParams(
            vmem_limit_bytes=VMEM_LIMIT if fetched else 16 * 1024 * 1024
        ),
    )(*operands)


def start_kernel(
    time_ref,
    hidden_in,
    out_in,
    weight_in,
    table_in,
    first_ref,
    hidden_ref,
    out_ref,
    weight_ref,
    table_ref,
    arrived,
):
    fetches = fetch_all(
        arrived,
        (table_in, table_ref),
        (weight_in, weight_ref),
        (hidden_in, hidden_ref),
        (out_in, out_ref),
    )
    lanes = hidden_ref.shape[0]
    lat_dim = out_ref.shape[0]
    for fetch in fetches:
        fetch.wait()
    waves = rotations(jnp.broadcast_to(time_ref[0], (1, lanes)), table_ref[...])
    active = jnp.concatenate([wave / (1.0 + jnp.exp(-wave)) for wave in waves], axis=1)
    modulation = lax.dot_general(
        active,
        weight_ref[...],
        (((1,), (1,)), ((), ())),
        precision=lax.Precision.HIGHEST,
        preferred_element_type=jnp.float32,
    )
    modulation = jnp.concatenate(
        [modulation, jnp.zeros((8, lanes - modulation.shape[1]), jnp.float32)], axis=1
    )
    hidden = hidden_ref[...]
    wide = hidden.astype(jnp.float32)
    ones = jnp.ones((8, hidden.shape[1]), jnp.bfloat16)
    high, low = split(wide * wide)
    squares = dot_rows(ones, high) + dot_rows(ones, low)
    partial = dot_rows(out_ref[...], hidden)
    row = lax.broadcasted_iota(jnp.int32, (8, lanes), 0)
    values = jnp.where(row < 2, squares, jnp.where(row < 4, modulation, 0.0))
    high = values.astype(jnp.bfloat16).astype(jnp.float32)
    extra = jnp.where(row % 2 == 0, high, values - high)
    rows = jnp.concatenate([partial, extra], axis=0).astype(jnp.bfloat16)
    for peer in range(first_ref.shape[0]):
        first_ref[peer] = rows


def noise_kernel(
    level_ref,
    first_ref,
    noise_ref,
    second_ref,
    kept_ref,
    pair,
    extra,
):
    f32 = jnp.float32
    level = level_ref[0]
    peers, used, lanes = first_ref.shape
    lat_dim = used - 8
    mod_width = 40
    parts = [first_ref[peer].astype(f32) for peer in range(peers)]
    total = sum(parts[1:], parts[0])
    projected = total[:lat_dim]
    root_mean = jnp.sqrt(
        (total[lat_dim : lat_dim + 1] + total[lat_dim + 1 : lat_dim + 2]) / D + EPS_NORM
    )
    latent = projected / root_mean
    kept_ref[:lat_dim, :] = projected
    kept_ref[2 * lat_dim :, :] = jnp.broadcast_to(root_mean, (8, lanes))
    pair[...] = jnp.zeros_like(pair)
    for peer in range(peers):
        at = slice(peer * mod_width, (peer + 1) * mod_width)
        row = parts[peer][lat_dim + 2 : lat_dim + 3] + parts[peer][lat_dim + 3 : lat_dim + 4]
        pair[0:1, at] = row[:, :mod_width]
        pair[1:2, at] = row[:, mod_width : 2 * mod_width]
    rest = peers * mod_width - lanes
    head = pair[0:2, :lanes]
    head_high = head.astype(jnp.bfloat16).astype(f32)
    tail = jnp.concatenate([pair[0:1, lanes : lanes + rest], pair[1:2, lanes : lanes + rest]], axis=1)
    tail_high = tail.astype(jnp.bfloat16).astype(f32)
    extra[2:4, :] = head_high
    extra[4:6, :] = head - head_high
    extra[6:7, :] = jnp.concatenate([tail_high, tail - tail_high], axis=1)
    extra[7:8, :] = jnp.zeros((1, lanes), f32)
    order = noise_ref[lat_dim : lat_dim + 1, :]
    coarse = jnp.floor(order * (1.0 / 64.0))
    extra[0:1, :] = coarse
    extra[1:2, :] = order - 64.0 * coarse
    noisy = ((1.0 - level) * latent + level * noise_ref[:lat_dim, :]).astype(jnp.bfloat16)
    kept_ref[lat_dim : 2 * lat_dim, :] = latent - noisy.astype(f32)
    rows = jnp.concatenate([noisy, extra[...].astype(jnp.bfloat16)], axis=0)
    for peer in range(second_ref.shape[0]):
        second_ref[peer] = rows


def heads_kernel(scores_ref, score_ref):
    total = jnp.sum(scores_ref[...].astype(jnp.float32), axis=0)
    for peer in range(score_ref.shape[0]):
        score_ref[peer] = total


def gradient_kernel(level_ref, score_ref, kept_ref, hidden_ref, third_ref, side_ref):
    f32 = jnp.float32
    level = level_ref[0]
    peers, half, lanes = score_ref.shape
    parts = peers // 4
    lat_dim = lanes // 2
    left = lax.broadcasted_iota(jnp.int32, (half, lanes), 1) < lat_dim
    pieces = []
    for part in range(parts):
        realistic = GUIDANCE * score_ref[parts + part] + (1.0 - GUIDANCE) * score_ref[2 * parts + part]
        difference = score_ref[3 * parts + part] - realistic
        pieces.append(jnp.where(left, difference, pltpu.roll(realistic, lat_dim, 1)))
        pieces.append(jnp.where(left, pltpu.roll(difference, lat_dim, 1), realistic))
    both = jnp.concatenate(pieces, axis=0).T
    difference = both[:lat_dim]
    realistic = both[lat_dim:]
    projected = kept_ref[:lat_dim, :]
    root_mean = kept_ref[2 * lat_dim : 2 * lat_dim + 1, :]
    distance = jnp.abs(kept_ref[lat_dim : 2 * lat_dim, :] + level * realistic)
    magnitude = jnp.sum(jnp.sum(distance, axis=0, keepdims=True), axis=1, keepdims=True)
    direction = difference / root_mean
    high, low = split(direction)
    hidden = hidden_ref[...]
    weight_part = dot32(high, hidden) + dot32(low, hidden)

    row = lax.broadcasted_iota(jnp.int32, (8, lat_dim), 0)
    first = magnitude.astype(jnp.bfloat16).astype(f32)
    second = (magnitude - first).astype(jnp.bfloat16).astype(f32)
    third = magnitude - first - second
    extra = jnp.where(row == 0, first, jnp.where(row == 1, second, jnp.where(row == 2, third, 0.0)))
    groups = third_ref.shape[0] // (lat_dim // 8)
    width = weight_part.shape[1] // groups
    for group in range(groups):
        columns = weight_part[:, group * width : (group + 1) * width]
        for block in range(lat_dim // 8):
            third_ref[block * groups + group] = jnp.concatenate(
                [columns[8 * block : 8 * (block + 1)], extra], axis=1
            ).astype(jnp.bfloat16)

    coefficient = jnp.sum(difference * projected, axis=0, keepdims=True) / (
        D * root_mean * root_mean * root_mean
    )
    side_ref[...] = jnp.concatenate(
        [direction, jnp.broadcast_to(coefficient, (lat_dim, lanes))], axis=0
    ).T


def scale_kernel(cells, rows, level_ref, third_ref, fourth_ref, factor_ref):
    total = jnp.sum(third_ref[...].astype(jnp.float32), axis=0)
    width = total.shape[1] - 64
    sums = total[:, width : width + 1]
    spread = (sums[0:1] + sums[1:2] + sums[2:3]) / cells + EPS_MEAN
    factor = -level_ref[0] / spread
    factor_ref[...] = jnp.broadcast_to(factor, factor_ref.shape)
    scaled = (total * (factor / math.sqrt(rows))).astype(jnp.bfloat16)
    for peer in range(fourth_ref.shape[0]):
        fourth_ref[peer] = scaled


def weight_kernel(fourth_ref, weight_ref):
    lat_dim, columns = weight_ref.shape
    groups = fourth_ref.shape[0] // (lat_dim // 8)
    width = columns // groups
    for block in range(lat_dim // 8):
        parts = [
            fourth_ref[block * groups + group].astype(jnp.float32)[:, :width]
            for group in range(groups)
        ]
        weight_ref[8 * block : 8 * (block + 1), :] = jnp.concatenate(parts, axis=1)


def hidden_kernel(factor_ref, side_ref, hidden_ref, out_ref, grad_ref):
    lat_dim = out_ref.shape[0]
    high, low = split(side_ref[:, :lat_dim])
    backward = dot32(high, out_ref[...]) + dot32(low, out_ref[...])
    coefficient = side_ref[:, lat_dim : lat_dim + 1]
    factor = factor_ref[0:1, 0:1]
    grad_ref[...] = (
        factor * (backward - hidden_ref[...].astype(jnp.float32) * coefficient)
    ).astype(jnp.bfloat16)


def body(
    gen_hidden,
    out_weight,
    noise,
    step_index,
    token_order,
    time_weight,
    embed_weight,
    qkv_weight,
    readout_weight,
):
    seq_count = lax.axis_size("seq")
    mp_count = lax.axis_size("mp")
    role_count = lax.axis_size("role")
    mp_index = lax.axis_index("mp")
    local_rows, columns = gen_hidden.shape
    lat_dim = out_weight.shape[1]
    bf16, f32 = jnp.bfloat16, jnp.float32
    timestep = step_index[0].astype(f32)
    level = (timestep / T_STEPS)[None]
    out_turned = out_weight.T

    time_turned = time_weight[0].transpose(1, 2, 0).reshape(-1, FREQ)
    turns = ROPE_BASE ** (-np.arange(FREQ // 2) / (FREQ // 2)) / (2.0 * np.pi)

    (first,) = call(
        start_kernel,
        [((mp_count, lat_dim + 8, local_rows), bf16)],
        timestep[None],
        gen_hidden,
        out_turned,
        time_turned,
        jnp.asarray(np.repeat(in_parts(turns), 8, axis=0)),
        scalars=1,
        fetched=4,
    )
    first = exchange(first, "mp")

    second, kept = call(
        noise_kernel,
        [((seq_count, lat_dim + 8, local_rows), bf16), ((2 * lat_dim + 8, local_rows), f32)],
        level,
        first,
        jnp.concatenate(
            [
                noise.T.astype(f32),
                token_order.astype(f32)[None],
                jnp.zeros((7, local_rows), f32),
            ]
        ),
        scalars=1,
        scratch=[pltpu.VMEM((8, 2 * local_rows), f32), pltpu.VMEM((8, local_rows), f32)],
    )
    readout, kept = lax.optimization_barrier((readout_weight[0, 0], kept))
    second = exchange(second, "seq")
    scores = run_pass(
        mp_index.astype(jnp.int32)[None],
        second,
        embed_weight[0].astype(f32),
        qkv_weight[0, 0],
        jnp.concatenate(
            [readout.T.astype(f32), rotation_tables(qkv_weight.shape[3] // 3)]
        ),
    )

    scores = exchange(scores, "seq")
    quarter = local_rows // mp_count
    peers = role_count * mp_count
    (score,) = call(heads_kernel, [((peers, quarter // 2, 2 * lat_dim), f32)], scores)

    score = exchange(score, ("role", "mp"))

    width = columns // 4 + lat_dim
    third, side = call(
        gradient_kernel,
        [((seq_count, 8, width), bf16), ((local_rows, 2 * lat_dim), f32)],
        level,
        score,
        kept,
        gen_hidden,
        scalars=1,
    )

    third = exchange(third, "seq")
    cells = local_rows * seq_count * lat_dim
    fourth, factor = call(
        functools.partial(scale_kernel, cells, local_rows * seq_count),
        [((seq_count, 8, width), bf16), ((8, 128), f32)],
        level,
        third,
        scalars=1,
    )
    fourth = exchange(fourth, "seq")
    (hidden_grad,) = call(
        hidden_kernel, [((local_rows, columns), bf16)], factor, side, gen_hidden, out_turned
    )
    (weight_grad,) = call(weight_kernel, [((lat_dim, columns), f32)], fourth)
    return (hidden_grad, weight_grad.T)


def solution(mesh):
    placed = (
        P("seq", "mp"),
        P("mp", None),
        P("seq", None),
        P(),
        P("seq"),
        P("role", None, None, ("seq", "mp")),
        P("role", None, None),
        P("role", "seq", None, None),
        P("role", "seq", None, None),
    )
    return jax.shard_map(
        body, mesh=mesh, in_specs=placed, out_specs=(P("seq", "mp"), P("mp", None)), check_vma=False
    )
```

```python
import functools
import math

import jax
import jax.numpy as jnp
import numpy as np
from jax import lax
from jax.experimental import pallas as pl
from jax.experimental.pallas import tpu as pltpu
from jax.sharding import PartitionSpec as P

D = 5120
FREQ = 256
T_STEPS = 1000


EPS_NORM = 1e-06
EPS_MEAN = 1e-05
GUIDANCE = 5.0
ROPE_BASE = 10000.0
SHARPNESS = 4.0
VMEM_LIMIT = 61 * 1024 * 1024
CHUNK = 1024


def split(values):
    high = values.astype(jnp.bfloat16)
    return high, (values - high.astype(jnp.float32)).astype(jnp.bfloat16)


def exchange(chunks, axes):
    return lax.all_to_all(chunks, axes, 0, 0, tiled=True)


def dot32(left, right):
    return jnp.dot(left, right, preferred_element_type=jnp.float32)


def dot_rows(left, right):
    return lax.dot_general(
        left, right, (((1,), (1,)), ((), ())), preferred_element_type=jnp.float32
    )


def fetch_all(arrived, *pairs):
    fetches = [
        pltpu.make_async_copy(source, target, arrived.at[index])
        for index, (source, target) in enumerate(pairs)
    ]
    for fetch in fetches:
        fetch.start()
    return fetches


def in_parts(turns):
    grain = 2.0 ** (np.floor(np.log2(turns)) - 11)
    high = np.floor(turns / grain) * grain
    return np.stack([high, turns - high]).astype(np.float32)


def rotation_tables(head_dim):
    turns = ROPE_BASE ** (-2.0 * np.arange(head_dim // 2) / head_dim) / (2.0 * np.pi)
    both = in_parts(turns).reshape(head_dim)
    return np.ascontiguousarray(np.broadcast_to(both[:, None], (head_dim, 128)))


def rotations(positions, table):
    table = jnp.concatenate([table] * (positions.shape[1] // table.shape[1]), axis=1)
    high = table[: table.shape[0] // 2]
    low = table[table.shape[0] // 2 :]
    whole = positions * high
    part = (whole - jnp.round(whole)) + positions * low
    angle = (part - jnp.round(part)) * math.pi
    square = angle * angle
    sine = square * (-1.0 / 39916800) + 1.0 / 362880
    sine = sine * square - 1.0 / 5040
    sine = sine * square + 1.0 / 120
    sine = sine * square - 1.0 / 6
    sine = (sine * square + 1.0) * angle
    cosine = square * (1.0 / 479001600) - 1.0 / 3628800
    cosine = cosine * square + 1.0 / 40320
    cosine = cosine * square - 1.0 / 720
    cosine = cosine * square + 1.0 / 24
    cosine = cosine * square - 0.5
    cosine = cosine * square + 1.0
    return 1.0 - 2.0 * sine * sine, 2.0 * sine * cosine


def normalize_rope(vectors, cosines, sines):
    rescaled = vectors * lax.rsqrt(jnp.mean(vectors * vectors, axis=0, keepdims=True) + EPS_NORM)
    width = vectors.shape[0] // 2
    front = rescaled[:width]
    back = rescaled[width:]
    return jnp.concatenate([front * cosines - back * sines, front * sines + back * cosines], axis=0)


def pass_kernel(
    place_ref,
    gathered_ref,
    embed_ref,
    weight_ref,
    small_ref,
    score_ref,
    modulation,
    scaled,
    clip,
    places,
    own,
    own_places,
    query,
    key,
    wide,
    attended,
):
    f32 = jnp.float32
    blocks, used, lanes = gathered_ref.shape
    lat_dim, width = embed_ref.shape
    head_dim = weight_ref.shape[1] // 3
    key_rows = blocks * lanes
    query_rows = query.shape[0]
    quarter = query_rows // blocks
    per_tile = lanes // quarter
    piece = width // blocks
    place = place_ref[0]

    for block in range(blocks):
        at = slice(block * lanes, (block + 1) * lanes)
        received = gathered_ref[block]
        clip[:lat_dim, at] = received[:lat_dim]
        clip[lat_dim:, at] = received[:lat_dim]
        extra = received[lat_dim:].astype(f32)
        places[0:1, at] = extra[0:1] * 64.0 + extra[1:2]
        pair = extra[2:4] + extra[4:6]
        tail = extra[6:7] + pltpu.roll(extra[6:7], lanes // 2, 1)
        begin = block * piece
        rest = piece - lanes
        modulation[0:2, begin : begin + lanes] = pair
        modulation[0:1, begin + lanes : begin + piece] = tail[:, :rest]
        modulation[1:2, begin + lanes : begin + piece] = tail[:, rest : 2 * rest]

    lane = lax.broadcasted_iota(jnp.int32, (used, lanes), 1)
    for tile in range(blocks // per_tile):
        found = jnp.zeros((used, lanes), f32)
        for part in range(per_tile):
            block = gathered_ref[tile * per_tile + part].astype(f32)
            shift = lax.rem((part - place + per_tile) * quarter, lanes)
            found = jnp.where(lane // quarter == part, pltpu.roll(block, shift, 1), found)
        at = slice(tile * lanes, (tile + 1) * lanes)
        rows = found[:lat_dim].astype(jnp.bfloat16)
        own[:lat_dim, at] = rows
        own[lat_dim:, at] = rows
        own_places[0:1, at] = found[lat_dim : lat_dim + 1] * 64.0 + found[lat_dim + 1 : lat_dim + 2]

    folded = jnp.zeros((2 * lat_dim + 16, 3 * head_dim), f32)
    for begin in range(0, width, CHUNK):
        at = slice(begin, begin + CHUNK)
        high, low = split(embed_ref[:, at] * (1.0 + modulation[1:2, at]))
        scaled[:lat_dim, at] = high
        scaled[lat_dim : 2 * lat_dim, at] = low
        row = lax.broadcasted_iota(jnp.int32, (16, CHUNK), 0)
        shifted = jnp.broadcast_to(modulation[0:1, at], (16, CHUNK))
        shifted_high = shifted.astype(jnp.bfloat16).astype(f32)
        shifted = jnp.where(row == 0, shifted_high, shifted - shifted_high)
        scaled[2 * lat_dim :, at] = jnp.where(row < 2, shifted, 0.0).astype(jnp.bfloat16)
        folded = folded + dot32(scaled[:, at], weight_ref[at, :])
    embed = embed_ref[...].astype(jnp.bfloat16)
    gram = dot_rows(embed, embed)
    matrix = folded[:lat_dim] + folded[lat_dim : 2 * lat_dim]
    offset = folded[2 * lat_dim : 2 * lat_dim + 1] + folded[2 * lat_dim + 1 : 2 * lat_dim + 2]
    turned = jnp.concatenate(
        [matrix, jnp.broadcast_to(offset, (lanes - lat_dim, 3 * head_dim))], axis=0
    ).T
    offsets = jnp.broadcast_to(turned[:, lat_dim : lat_dim + 1], (3 * head_dim, lanes))
    matrix_parts = jnp.concatenate(split(turned[:, :lat_dim]), axis=1)
    gram_parts = jnp.concatenate(split(gram), axis=1)

    def project(parts, offsets, rows):
        product = dot32(jnp.concatenate([parts, gram_parts], axis=0), rows)
        count = parts.shape[0]
        mean = jnp.sum(rows[:lat_dim].astype(f32) * product[count:], axis=0, keepdims=True) / width
        offsets = jnp.concatenate([offsets] * (rows.shape[1] // lanes), axis=1)
        return product[:count] * lax.rsqrt(mean + EPS_NORM) + offsets

    step = 4 * lanes
    table = small_ref[lat_dim:, :]
    wide[:, head_dim:] = jnp.ones((key_rows, head_dim), jnp.bfloat16)
    for begin in range(0, query_rows, step):
        at = slice(begin, begin + step)
        vectors = project(matrix_parts[:head_dim], offsets[:head_dim], own[:, at])
        turns = rotations(own_places[0:1, at], table)
        query[at, :] = normalize_rope(vectors, *turns).T.astype(jnp.bfloat16)

    def keys_and_values(index, carry):
        at = pl.ds(pl.multiple_of(index * step, step), step)
        vectors = project(matrix_parts[head_dim:], offsets[head_dim:], clip[:, at])
        turns = rotations(places[0:1, at], table)
        key[:, at] = normalize_rope(vectors[:head_dim], *turns).astype(jnp.bfloat16)
        wide[at, :head_dim] = vectors[head_dim:].T.astype(jnp.bfloat16)
        return carry

    lax.fori_loop(0, key_rows // step, keys_and_values, 0, unroll=True)

    rows, step = 1024, 256
    factor = SHARPNESS / math.sqrt(head_dim) * math.log2(math.e)

    def attend(index, carry):
        at = pl.ds(pl.multiple_of(index * rows, rows), rows)
        queries = query[at, :]
        total = jnp.zeros((rows, 2 * head_dim), f32)
        for begin in range(0, key_rows, step):
            scores = dot32(queries, key[:, begin : begin + step])
            exponents = jnp.exp2(scores * factor).astype(jnp.bfloat16)
            total = total + dot32(exponents, wide[begin : begin + step, :])
        result = (total[:, :head_dim] / total[:, head_dim:]).astype(jnp.bfloat16)
        attended[pl.ds(index * (rows // quarter), rows // quarter)] = result.reshape(
            rows // quarter, quarter, head_dim
        )
        return carry

    lax.fori_loop(0, query_rows // rows, attend, 0, unroll=True)
    half = quarter // 2
    readout = small_ref[:lat_dim, :].astype(jnp.bfloat16)
    halves = [
        dot_rows(attended[:, begin : begin + half, :].reshape(blocks * half, head_dim), readout)
        for begin in (0, half)
    ]
    score_ref[...] = (
        jnp.concatenate(halves, axis=1).astype(jnp.bfloat16).reshape(blocks, half, 2 * lat_dim)
    )


def run_pass(place, gathered, embed, weights, small):
    blocks, unused, lanes = gathered.shape
    lat_dim, width = embed.shape
    head_dim = weights.shape[1] // 3
    key_rows = blocks * lanes
    query_rows = key_rows // 4
    bf16, f32 = jnp.bfloat16, jnp.float32
    vmem = pl.BlockSpec(memory_space=pltpu.VMEM)
    return pl.pallas_call(
        pass_kernel,
        out_shape=jax.ShapeDtypeStruct((blocks, lanes // 8, lanes), bf16),
        in_specs=[pl.BlockSpec(memory_space=pltpu.SMEM)] + [vmem] * 4,
        out_specs=vmem,
        scratch_shapes=[
            pltpu.VMEM((8, width), f32),
            pltpu.VMEM((2 * lat_dim + 16, width), bf16),
            pltpu.VMEM((2 * lat_dim, key_rows), bf16),
            pltpu.VMEM((8, key_rows), f32),
            pltpu.VMEM((2 * lat_dim, query_rows), bf16),
            pltpu.VMEM((8, query_rows), f32),
            pltpu.VMEM((query_rows, head_dim), bf16),
            pltpu.VMEM((head_dim, key_rows), bf16),
            pltpu.VMEM((key_rows, 2 * head_dim), bf16),
            pltpu.VMEM((blocks, lanes // 4, head_dim), bf16),
        ],
        compiler_params=pltpu.CompilerParams(vmem_limit_bytes=40 * 1024 * 1024),
    )(place, gathered, embed, weights, small)


def call(kernel, outputs, *operands, scalars=0, fetched=0, scratch=()):
    vmem = pl.BlockSpec(memory_space=pltpu.VMEM)
    smem = pl.BlockSpec(memory_space=pltpu.SMEM)
    plain = len(operands) - scalars - fetched
    scratch = list(scratch)
    if fetched:
        scratch += [pltpu.VMEM(a.shape, a.dtype) for a in operands[-fetched:]]
        scratch.append(pltpu.SemaphoreType.DMA((fetched,)))
    return pl.pallas_call(
        kernel,
        out_shape=[jax.ShapeDtypeStruct(*output) for output in outputs],
        in_specs=[smem] * scalars + [vmem] * plain + [pl.BlockSpec(memory_space=pl.ANY)] * fetched,
        out_specs=[vmem] * len(outputs),
        scratch_shapes=scratch,
        compiler_params=pltpu.CompilerParams(
            vmem_limit_bytes=VMEM_LIMIT if fetched else 16 * 1024 * 1024
        ),
    )(*operands)


def start_kernel(
    time_ref,
    hidden_in,
    out_in,
    weight_in,
    table_in,
    order_in,
    first_ref,
    hidden_ref,
    out_ref,
    weight_ref,
    table_ref,
    order_ref,
    arrived,
):
    fetches = fetch_all(
        arrived,
        (table_in, table_ref),
        (weight_in, weight_ref),
        (hidden_in, hidden_ref),
        (out_in, out_ref),
        (order_in, order_ref),
    )
    lanes = hidden_ref.shape[0]
    lat_dim = out_ref.shape[0]
    for fetch in fetches:
        fetch.wait()
    waves = rotations(jnp.broadcast_to(time_ref[0], (1, lanes)), table_ref[...])
    active = jnp.concatenate([wave / (1.0 + jnp.exp(-wave)) for wave in waves], axis=1)
    modulation = lax.dot_general(
        active,
        weight_ref[...],
        (((1,), (1,)), ((), ())),
        precision=lax.Precision.HIGHEST,
        preferred_element_type=jnp.float32,
    )
    modulation = jnp.concatenate(
        [modulation, jnp.zeros((8, lanes - modulation.shape[1]), jnp.float32)], axis=1
    )
    hidden = hidden_ref[...]
    wide = hidden.astype(jnp.float32)
    ones = jnp.ones((8, hidden.shape[1]), jnp.bfloat16)
    high, low = split(wide * wide)
    squares = dot_rows(ones, high) + dot_rows(ones, low)
    partial = dot_rows(out_ref[...], hidden)
    row = lax.broadcasted_iota(jnp.int32, (8, lanes), 0)
    values = jnp.where(row < 2, squares, jnp.where(row < 4, modulation, 0.0))
    high = values.astype(jnp.bfloat16).astype(jnp.float32)
    extra = jnp.where(row % 2 == 0, high, values - high)
    order = order_ref[...].astype(jnp.float32)
    coarse = jnp.floor(order * (1.0 / 64.0))
    extra = jnp.where(row == 4, coarse, jnp.where(row == 5, order - 64.0 * coarse, extra))
    rows = jnp.concatenate([partial, extra], axis=0).astype(jnp.bfloat16)
    for peer in range(first_ref.shape[0]):
        first_ref[peer] = rows


def noise_kernel(
    level_ref,
    first_ref,
    noise_ref,
    second_ref,
    kept_ref,
    pair,
    extra,
):
    f32 = jnp.float32
    level = level_ref[0]
    peers, used, lanes = first_ref.shape
    lat_dim = used - 8
    mod_width = 40
    parts = [first_ref[peer].astype(f32) for peer in range(peers)]
    total = sum(parts[1:], parts[0])
    projected = total[:lat_dim]
    root_mean = jnp.sqrt(
        (total[lat_dim : lat_dim + 1] + total[lat_dim + 1 : lat_dim + 2]) / D + EPS_NORM
    )
    latent = projected / root_mean
    kept_ref[:lat_dim, :] = projected
    kept_ref[2 * lat_dim :, :] = jnp.broadcast_to(root_mean, (8, lanes))
    pair[...] = jnp.zeros_like(pair)
    for peer in range(peers):
        at = slice(peer * mod_width, (peer + 1) * mod_width)
        row = parts[peer][lat_dim + 2 : lat_dim + 3] + parts[peer][lat_dim + 3 : lat_dim + 4]
        pair[0:1, at] = row[:, :mod_width]
        pair[1:2, at] = row[:, mod_width : 2 * mod_width]
    rest = peers * mod_width - lanes
    head = pair[0:2, :lanes]
    head_high = head.astype(jnp.bfloat16).astype(f32)
    tail = jnp.concatenate([pair[0:1, lanes : lanes + rest], pair[1:2, lanes : lanes + rest]], axis=1)
    tail_high = tail.astype(jnp.bfloat16).astype(f32)
    extra[2:4, :] = head_high
    extra[4:6, :] = head - head_high
    extra[6:7, :] = jnp.concatenate([tail_high, tail - tail_high], axis=1)
    extra[7:8, :] = jnp.zeros((1, lanes), f32)
    extra[0:2, :] = parts[0][lat_dim + 4 : lat_dim + 6]
    noisy = ((1.0 - level) * latent + level * noise_ref[...]).astype(jnp.bfloat16)
    kept_ref[lat_dim : 2 * lat_dim, :] = latent - noisy.astype(f32)
    rows = jnp.concatenate([noisy, extra[...].astype(jnp.bfloat16)], axis=0)
    for peer in range(second_ref.shape[0]):
        second_ref[peer] = rows


def heads_kernel(scores_ref, score_ref):
    total = jnp.sum(scores_ref[...].astype(jnp.float32), axis=0)
    for peer in range(score_ref.shape[0]):
        score_ref[peer] = total


def gradient_kernel(level_ref, score_ref, kept_ref, hidden_ref, third_ref, side_ref):
    f32 = jnp.float32
    level = level_ref[0]
    peers, half, lanes = score_ref.shape
    parts = peers // 4
    lat_dim = lanes // 2
    left = lax.broadcasted_iota(jnp.int32, (half, lanes), 1) < lat_dim
    pieces = []
    for part in range(parts):
        realistic = GUIDANCE * score_ref[parts + part] + (1.0 - GUIDANCE) * score_ref[2 * parts + part]
        difference = score_ref[3 * parts + part] - realistic
        pieces.append(jnp.where(left, difference, pltpu.roll(realistic, lat_dim, 1)))
        pieces.append(jnp.where(left, pltpu.roll(difference, lat_dim, 1), realistic))
    both = jnp.concatenate(pieces, axis=0).T
    difference = both[:lat_dim]
    realistic = both[lat_dim:]
    projected = kept_ref[:lat_dim, :]
    root_mean = kept_ref[2 * lat_dim : 2 * lat_dim + 1, :]
    distance = jnp.abs(kept_ref[lat_dim : 2 * lat_dim, :] + level * realistic)
    magnitude = jnp.sum(jnp.sum(distance, axis=0, keepdims=True), axis=1, keepdims=True)
    direction = difference / root_mean
    high, low = split(direction)
    hidden = hidden_ref[...]
    weight_part = dot32(high, hidden) + dot32(low, hidden)

    row = lax.broadcasted_iota(jnp.int32, (8, lat_dim), 0)
    first = magnitude.astype(jnp.bfloat16).astype(f32)
    second = (magnitude - first).astype(jnp.bfloat16).astype(f32)
    third = magnitude - first - second
    extra = jnp.where(row == 0, first, jnp.where(row == 1, second, jnp.where(row == 2, third, 0.0)))
    groups = third_ref.shape[0] // (lat_dim // 8)
    width = weight_part.shape[1] // groups
    for group in range(groups):
        columns = weight_part[:, group * width : (group + 1) * width]
        for block in range(lat_dim // 8):
            third_ref[block * groups + group] = jnp.concatenate(
                [columns[8 * block : 8 * (block + 1)], extra], axis=1
            ).astype(jnp.bfloat16)

    coefficient = jnp.sum(difference * projected, axis=0, keepdims=True) / (
        D * root_mean * root_mean * root_mean
    )
    side_ref[...] = jnp.concatenate(
        [direction, jnp.broadcast_to(coefficient, (lat_dim, lanes))], axis=0
    ).T


def scale_kernel(cells, rows, level_ref, third_ref, fourth_ref, factor_ref):
    total = jnp.sum(third_ref[...].astype(jnp.float32), axis=0)
    width = total.shape[1] - 64
    sums = total[:, width : width + 1]
    spread = (sums[0:1] + sums[1:2] + sums[2:3]) / cells + EPS_MEAN
    factor = -level_ref[0] / spread
    factor_ref[...] = jnp.broadcast_to(factor, factor_ref.shape)
    scaled = (total * (factor / math.sqrt(rows))).astype(jnp.bfloat16)
    for peer in range(fourth_ref.shape[0]):
        fourth_ref[peer] = scaled


def weight_kernel(fourth_ref, weight_ref):
    lat_dim, columns = weight_ref.shape
    groups = fourth_ref.shape[0] // (lat_dim // 8)
    width = columns // groups
    for block in range(lat_dim // 8):
        parts = [
            fourth_ref[block * groups + group].astype(jnp.float32)[:, :width]
            for group in range(groups)
        ]
        weight_ref[8 * block : 8 * (block + 1), :] = jnp.concatenate(parts, axis=1)


def hidden_kernel(factor_ref, side_ref, hidden_ref, out_ref, grad_ref):
    lat_dim = out_ref.shape[0]
    high, low = split(side_ref[:, :lat_dim])
    backward = dot32(high, out_ref[...]) + dot32(low, out_ref[...])
    coefficient = side_ref[:, lat_dim : lat_dim + 1]
    factor = factor_ref[0:1, 0:1]
    grad_ref[...] = (
        factor * (backward - hidden_ref[...].astype(jnp.float32) * coefficient)
    ).astype(jnp.bfloat16)


def body(
    gen_hidden,
    out_weight,
    noise,
    step_index,
    token_order,
    time_weight,
    embed_weight,
    qkv_weight,
    readout_weight,
):
    seq_count = lax.axis_size("seq")
    mp_count = lax.axis_size("mp")
    role_count = lax.axis_size("role")
    mp_index = lax.axis_index("mp")
    local_rows, columns = gen_hidden.shape
    lat_dim = out_weight.shape[1]
    bf16, f32 = jnp.bfloat16, jnp.float32
    timestep = step_index[0].astype(f32)
    level = (timestep / T_STEPS)[None]
    out_turned = out_weight.T

    time_turned = time_weight[0].transpose(1, 2, 0).reshape(-1, FREQ)
    turns = ROPE_BASE ** (-np.arange(FREQ // 2) / (FREQ // 2)) / (2.0 * np.pi)

    (first,) = call(
        start_kernel,
        [((mp_count, lat_dim + 8, local_rows), bf16)],
        timestep[None],
        gen_hidden,
        out_turned,
        time_turned,
        jnp.asarray(np.repeat(in_parts(turns), 8, axis=0)),
        token_order[None],
        scalars=1,
        fetched=5,
    )
    first = exchange(first, "mp")

    second, kept = call(
        noise_kernel,
        [((seq_count, lat_dim + 8, local_rows), bf16), ((2 * lat_dim + 8, local_rows), f32)],
        level,
        first,
        noise.T.astype(f32),
        scalars=1,
        scratch=[pltpu.VMEM((8, 2 * local_rows), f32), pltpu.VMEM((8, local_rows), f32)],
    )
    readout, kept = lax.optimization_barrier((readout_weight[0, 0], kept))
    second = exchange(second, "seq")
    scores = run_pass(
        mp_index.astype(jnp.int32)[None],
        second,
        embed_weight[0].astype(f32),
        qkv_weight[0, 0],
        jnp.concatenate(
            [readout.T.astype(f32), rotation_tables(qkv_weight.shape[3] // 3)]
        ),
    )

    scores = exchange(scores, "seq")
    quarter = local_rows // mp_count
    peers = role_count * mp_count
    (score,) = call(heads_kernel, [((peers, quarter // 2, 2 * lat_dim), f32)], scores)

    score = exchange(score, ("role", "mp"))

    width = columns // 4 + lat_dim
    third, side = call(
        gradient_kernel,
        [((seq_count, 8, width), bf16), ((local_rows, 2 * lat_dim), f32)],
        level,
        score,
        kept,
        gen_hidden,
        scalars=1,
    )

    third = exchange(third, "seq")
    cells = local_rows * seq_count * lat_dim
    fourth, factor = call(
        functools.partial(scale_kernel, cells, local_rows * seq_count),
        [((seq_count, 8, width), bf16), ((8, 128), f32)],
        level,
        third,
        scalars=1,
    )
    fourth = exchange(fourth, "seq")
    (hidden_grad,) = call(
        hidden_kernel, [((local_rows, columns), bf16)], factor, side, gen_hidden, out_turned
    )
    (weight_grad,) = call(weight_kernel, [((lat_dim, columns), f32)], fourth)
    return (hidden_grad, weight_grad.T)


def solution(mesh):
    placed = (
        P("seq", "mp"),
        P("mp", None),
        P("seq", None),
        P(),
        P("seq"),
        P("role", None, None, ("seq", "mp")),
        P("role", None, None),
        P("role", "seq", None, None),
        P("role", "seq", None, None),
    )
    return jax.shard_map(
        body, mesh=mesh, in_specs=placed, out_specs=(P("seq", "mp"), P("mp", None)), check_vma=False
    )
```
